32 devices in a mesh: batch: 4 (over x, core), seq: 8 (over z, y).
Axes of the slice: x: 2, y: 2, z: 4, core: 2. Of those that a mesh axis runs over, the one named last changes fastest.
Arguments:
- byte_rows: bfloat16 [8, 1536, 512], P('batch', 'seq'), may hold values from -6 to 6
- item_lengths: int32 [8], P('batch'), may hold values from 153 to 1536, as said below
- out_grad: bfloat16 [8, 1536, 512], P('batch', 'seq'), may hold values from -6 to 6
- pool_weight: bfloat16 [1536, 512], replicated, may hold values from -0.15625 to 0.15625
- norm1_gain: float32 [512], replicated, may hold values from 0.25 to 1.75
- norm1_bias: float32 [512], replicated, may hold values from -1.5 to 1.5
- query_weight: bfloat16 [512, 512], replicated, may hold values from -0.25 to 0.25
- key_weight: bfloat16 [512, 512], replicated, may hold values from -0.25 to 0.25
- value_weight: bfloat16 [512, 512], replicated, may hold values from -0.25 to 0.25
- position_weight: bfloat16 [512, 512], replicated, may hold values from -0.25 to 0.25
- content_bias: float32 [8, 64], replicated, may hold values from -2.5 to 2.5
- position_bias: float32 [8, 64], replicated, may hold values from -2.5 to 2.5
- output_weight: bfloat16 [512, 512], replicated, may hold values from -1 to 1
- norm2_gain: float32 [512], replicated, may hold values from 0.25 to 1.75
- norm2_bias: float32 [512], replicated, may hold values from -1.5 to 1.5
- inner_weight: bfloat16 [512, 2048], replicated, may hold values from -0.25 to 0.25
- outer_weight: bfloat16 [2048, 512], replicated, may hold values from -0.125 to 0.125
- upsample_weight: bfloat16 [512, 1536], replicated, may hold values from -0.25 to 0.25
Outputs:
- block_out: bfloat16 [8, 1536, 512], P('batch', 'seq')
- input_grad: float32 [8, 1536, 512], P('batch', 'seq')
- pool_weight_grad: float32 [1536, 512], replicated
- norm1_gain_grad: float32 [512], replicated
- norm1_bias_grad: float32 [512], replicated
- query_weight_grad: float32 [512, 512], replicated
- key_weight_grad: float32 [512, 512], replicated
- value_weight_grad: float32 [512, 512], replicated
- position_weight_grad: float32 [512, 512], replicated
- content_bias_grad: float32 [8, 64], replicated
- position_bias_grad: float32 [8, 64], replicated
- output_weight_grad: float32 [512, 512], replicated
- norm2_gain_grad: float32 [512], replicated
- norm2_bias_grad: float32 [512], replicated
- inner_weight_grad: float32 [512, 2048], replicated
- outer_weight_grad: float32 [2048, 512], replicated
- upsample_weight_grad: float32 [512, 1536], replicated
The draws below stay inside these ranges and needn't reach their ends.
Inputs may be any that keep to these rules, and one draw needn't show every extreme that they name: `item_lengths`: every length is a multiple of 3. Among the 2 items 2 b to 2 b + 1 of each index b of batch, one has length 1536.
All inputs are finite; a program needn't handle non-finite values.
Results may differ from the reference program's by a relative error of at most 0.02.
Values may be sent and summed in bfloat16 or wider, within the bound.
A program may use at most 384 MiB of HBM per device.

```python
import jax
import jax.numpy as jnp
from jax import lax

D = 512
H = 8
FF = 2048
SEQS = 2
HEAD_DIM = 64
SHORT_LEN = 512
FULL_LEN = 1536
ITEMS = 8


def draw_item_lengths(key, part):
    key = jax.random.fold_in(key, 7)
    first_key, second_key = jax.random.split(key)
    least = max(1, SHORT_LEN // 10)
    groups = ITEMS // SEQS
    short_counts = jax.random.randint(first_key, (groups, SEQS), least, SHORT_LEN + 1)
    chosen = jax.random.randint(second_key, (groups,), 0, SEQS)
    struck = jnp.arange(SEQS)[None, :] == chosen[:, None]
    short_counts = jnp.where(struck, SHORT_LEN, short_counts)
    return (3 * short_counts).reshape(ITEMS).astype(jnp.int32)


def block_scale(own_key, shape, cuts, low, largest):
    def one(position, blocks):
        heights = jax.random.uniform(jax.random.fold_in(jax.random.fold_in(own_key, 6), position), (blocks,), jnp.float32, low / len(cuts), largest / len(cuts))
        return jnp.repeat(jnp.exp(heights), shape[position] // blocks).reshape((-1,) + (1,) * (len(shape) - position - 1))

    gain = one(*cuts[0])
    for cut in cuts[1:]:
        gain = gain * one(*cut)
    return gain


def bell_draw(key, dims, deviation, most, cuts=(), held_as=jnp.bfloat16):
    values = jax.random.normal(key, dims, jnp.float32) * deviation
    if len(cuts) > 0:
        values = block_scale(key, dims, cuts, -0.22, 0.18) * values
    return jnp.clip(values, min=-most, max=most).astype(held_as)


def setup_inputs(seed: int = 0) -> dict:
    key_of = jax.random.split(jax.random.key(seed), 19)
    byte_rows = bell_draw(key_of[0], (ITEMS, FULL_LEN, D), 1.0, 6.0, ((0, 4), (1, 8)))
    item_lengths = draw_item_lengths(jax.random.fold_in(key_of[18], 71), 0)
    out_grad = bell_draw(key_of[2], (ITEMS, FULL_LEN, D), 1.0, 6.0, ((0, 4), (1, 8)))
    pool_weight = bell_draw(key_of[3], (3 * D, D), (3 * D) ** -0.5, 0.15625)
    norm1_gain = jnp.clip(1.0 + 0.15 * jax.random.normal(key_of[4], (D,), jnp.float32), 0.25, 1.75)
    norm1_bias = bell_draw(key_of[5], (D,), 0.3, 1.5, (), jnp.float32)
    query_weight = bell_draw(key_of[6], (D, D), D ** -0.5, 0.25)
    key_weight = bell_draw(key_of[7], (D, D), D ** -0.5, 0.25)
    value_weight = bell_draw(key_of[8], (D, D), D ** -0.5, 0.25)
    position_weight = bell_draw(key_of[9], (D, D), D ** -0.5, 0.25)
    content_bias = bell_draw(key_of[10], (H, HEAD_DIM), 0.5, 2.5, (), jnp.float32)
    position_bias = bell_draw(key_of[11], (H, HEAD_DIM), 0.5, 2.5, (), jnp.float32)
    output_weight = bell_draw(key_of[12], (D, D), (D // 16) ** -0.5, 1.0)
    norm2_gain = jnp.clip(1.0 + 0.15 * jax.random.normal(key_of[13], (D,), jnp.float32), 0.25, 1.75)
    norm2_bias = bell_draw(key_of[14], (D,), 0.3, 1.5, (), jnp.float32)
    inner_weight = bell_draw(key_of[15], (D, FF), D ** -0.5, 0.25)
    outer_weight = bell_draw(key_of[16], (FF, D), FF ** -0.5, 0.125)
    upsample_weight = bell_draw(key_of[17], (D, 3 * D), D ** -0.5, 0.25)
    return {"byte_rows": byte_rows, "item_lengths": item_lengths, "out_grad": out_grad, "pool_weight": pool_weight, "norm1_gain": norm1_gain, "norm1_bias": norm1_bias, "query_weight": query_weight, "key_weight": key_weight, "value_weight": value_weight, "position_weight": position_weight, "content_bias": content_bias, "position_bias": position_bias, "output_weight": output_weight, "norm2_gain": norm2_gain, "norm2_bias": norm2_bias, "inner_weight": inner_weight, "outer_weight": outer_weight, "upsample_weight": upsample_weight}


@jax.custom_vjp
def low(v):
    return lax.optimization_barrier(v.astype(jnp.bfloat16)).astype(jnp.float32)

@jax.custom_vjp
def low_back(v):
    return v

def low_keep(v):
    return (low(v), None)

def low_pass(kept, grad):
    return (grad,)

def back_keep(v):
    return (v, None)

def back_low(kept, grad):
    return (low(grad),)
low.defvjp(low_keep, low_pass)
low_back.defvjp(back_keep, back_low)
epsilon = 1e-05
masked_value = -1e+30

def product(left, right):
    return jnp.dot(left, right, precision=lax.Precision.HIGHEST, preferred_element_type=jnp.float32)

def contraction_spec(form, left, right):
    return jnp.einsum(form, left, right, precision=lax.Precision.HIGHEST, preferred_element_type=jnp.float32)

def layer_norm(rows_in, gain_vec, bias_vec):
    row_mean = lax.optimization_barrier(jnp.mean(rows_in, axis=-1, keepdims=True))
    centered = rows_in - row_mean
    variance = lax.optimization_barrier(jnp.mean(centered * centered, axis=-1, keepdims=True))
    return centered * lax.rsqrt(variance + epsilon) * gain_vec + bias_vec

def relative_table(row_total, short_len, width):
    offsets = jnp.arange(row_total).astype(jnp.float32)
    distance = short_len - 1 - offsets
    steps_in = jnp.arange(0, width, 2).astype(jnp.float32)
    frequency = jnp.exp(-jnp.log(10000.0) * steps_in / width)
    angles = distance[:, None] * frequency[None, :]
    return jnp.concatenate([jnp.sin(angles), jnp.cos(angles)], axis=1)

def skew_scores(scattered_rows, block_rows, key_length_sum):
    head_count, _, extent_length = scattered_rows.shape
    flattened = scattered_rows.reshape(head_count, block_rows * extent_length)
    flattened = lax.slice_in_dim(flattened, block_rows - 1, block_rows - 1 + block_rows * (extent_length - 1), axis=1)
    return flattened.reshape(head_count, block_rows, extent_length - 1)[:, :, :key_length_sum]

def attend_item(query_content, query_location, keys_in, values_in, key_count, position_indices):
    position_indices = low_back(position_indices)
    short_len, head_count, head_width = query_content.shape
    block_rows = min(512, short_len)
    pieces = []
    for block_index in range(short_len // block_rows):
        leading_index = block_index * block_rows
        key_length_sum = leading_index + block_rows
        extent_length = key_length_sum + block_rows - 1
        start_offset = short_len - leading_index - block_rows
        content = contraction_spec('nhd,lhd->hnl', query_content[leading_index:key_length_sum], keys_in[:key_length_sum])
        scattered_rows = contraction_spec('cpt,kpt->pck', query_location[leading_index:key_length_sum], position_indices[start_offset:start_offset + extent_length])
        logits = low_back(content + skew_scores(scattered_rows, block_rows, key_length_sum)) * head_width ** (-0.5)
        query_at = leading_index + jnp.arange(block_rows)[:, None]
        key_at = jnp.arange(key_length_sum)[None, :]
        valid = ((key_at <= query_at) & (key_at < key_count))[None]
        logits = jnp.where(valid, logits, masked_value)
        weights = low(jax.nn.softmax(logits, axis=-1))
        pieces.append(contraction_spec('hnl,lhd->nhd', weights, values_in[:key_length_sum]))
    return jnp.concatenate(pieces, axis=0)

def forward(key_counts, live, byte_rows, pool_weight, norm1_gain, norm1_bias, query_weight, key_weight, value_weight, position_weight, content_bias, position_bias, output_weight, norm2_gain, norm2_bias, inner_weight, outer_weight, upsample_weight):
    item_count, full_len, width = byte_rows.shape
    short_len = full_len // 3
    head_count, head_width = content_bias.shape
    block_rows = min(512, short_len)
    shifted = jnp.pad(byte_rows, ((0, 0), (2, 0), (0, 0)))[:, :full_len]
    grouped = shifted.reshape(item_count * short_len, 3 * width)
    short = low(low_back(product(grouped, pool_weight)))
    attn_in = low(layer_norm(short, norm1_gain, norm1_bias))
    queries = low_back(product(attn_in, query_weight))
    content_q = low(queries + content_bias.reshape(-1))
    position_q = low(queries + position_bias.reshape(-1))
    keys = low(low_back(product(attn_in, key_weight)))
    values = low(low_back(product(attn_in, value_weight)))
    table = low(relative_table(short_len + block_rows - 1, short_len, width))
    position_indices = low(product(table, position_weight)).reshape(-1, head_count, head_width)

    def heads_of(array_in):
        return array_in.reshape(item_count, short_len, head_count, head_width)
    checked = jax.checkpoint(attend_item)

    def per_item(packed):
        return checked(packed[0], packed[1], packed[2], packed[3], packed[4], position_indices)
    attended = lax.map(per_item, (heads_of(content_q), heads_of(position_q), heads_of(keys), heads_of(values), key_counts))
    attended = low(low_back(attended.reshape(item_count * short_len, width)))
    hidden = short + low_back(product(attended, output_weight))
    ffn_in = low(layer_norm(hidden, norm2_gain, norm2_bias))
    inner = low_back(product(ffn_in, inner_weight))
    activated = low(jax.nn.gelu(inner, approximate=False))
    summed = hidden + low_back(product(activated, outer_weight))
    upsampled = product(low(low_back(summed)), upsample_weight).reshape(item_count, full_len, width)
    return byte_rows + upsampled * live

def reference(byte_rows, item_lengths, out_grad, pool_weight, norm1_gain, norm1_bias, query_weight, key_weight, value_weight, position_weight, content_bias, position_bias, output_weight, norm2_gain, norm2_bias, inner_weight, outer_weight, upsample_weight):
    full_len = byte_rows.shape[1]
    key_counts = (item_lengths // 3).astype(jnp.int32)
    live = (jnp.arange(full_len)[None, :] < item_lengths[:, None]).astype(jnp.float32)[:, :, None]
    params = (byte_rows.astype(jnp.float32), pool_weight.astype(jnp.float32), norm1_gain, norm1_bias, query_weight.astype(jnp.float32), key_weight.astype(jnp.float32), value_weight.astype(jnp.float32), position_weight.astype(jnp.float32), content_bias, position_bias, output_weight.astype(jnp.float32), norm2_gain, norm2_bias, inner_weight.astype(jnp.float32), outer_weight.astype(jnp.float32), upsample_weight.astype(jnp.float32))

    def applied(*values_in):
        return forward(key_counts, live, *values_in)
    result, pullback = jax.vjp(applied, *params)
    grads = pullback(out_grad.astype(jnp.float32))
    return (result.astype(jnp.bfloat16), grads[0], grads[1], grads[2], grads[3], grads[4], grads[5], grads[6], grads[7], grads[8], grads[9], grads[10], grads[11], grads[12], grads[13], grads[14], grads[15])
```

```python
import functools

import jax
import jax.numpy as jnp
import numpy as np
from jax import lax
from jax.experimental import pallas as pl
from jax.experimental.pallas import tpu as pltpu
from jax.sharding import PartitionSpec as P

MESH = pl.DeviceIdType.MESH
epsilon = 1e-05
masked_value = -1e30
BLOCK = 128
LANES = 128
VMEM = pl.BlockSpec(memory_space=pltpu.VMEM)
SMEM = pl.BlockSpec(memory_space=pltpu.SMEM)
ANY = pl.BlockSpec(memory_space=pl.ANY)


def dot(left, right):
    return jnp.dot(left, right, preferred_element_type=jnp.float32)


def dot_nt(left, right):
    return lax.dot_general(
        left, right, (((1,), (1,)), ((), ())), preferred_element_type=jnp.float32
    )


def dot_tn(left, right):
    return lax.dot_general(
        left, right, (((0,), (0,)), ((), ())), preferred_element_type=jnp.float32
    )


def low(value):
    return value.astype(jnp.bfloat16)


def distance_table(short_len, width):
    distance = (short_len - 1 - np.arange(short_len)).astype(np.float32)
    steps_in = np.arange(0, width, 2).astype(np.float32)
    frequency = np.exp(-np.log(np.float32(10000.0)) * steps_in / np.float32(width))
    angles = distance[:, None] * frequency[None, :].astype(np.float32)
    both = np.concatenate([np.sin(angles), np.cos(angles)], axis=1)
    return jnp.asarray(both.astype(jnp.bfloat16))


def norm_rows(rows):
    mean = jnp.mean(rows, axis=-1, keepdims=True)
    centered = rows - mean
    inverse = lax.rsqrt(jnp.mean(centered * centered, axis=-1, keepdims=True) + epsilon)
    return centered * inverse, inverse


def norm_backward(gradient, normed, inverse, gain):
    scaled = gradient * gain
    return inverse * (
        scaled
        - jnp.mean(scaled, axis=-1, keepdims=True)
        - normed * jnp.mean(scaled * normed, axis=-1, keepdims=True)
    )


class Sizes:
    def __init__(self, n, items, full_rows, width, heads):
        self.n = n
        self.items = items
        self.r = full_rows // 3
        self.width = width
        self.heads = heads
        self.hd = width // heads
        self.units = items * heads // n
        self.length = n * self.r
        self.rows = items * self.r
        assert n % heads == 0 and self.units * self.hd <= LANES


def greet(n, me):
    barrier = pltpu.get_barrier_semaphore()
    for step in range(1, n):
        pl.semaphore_signal(
            barrier, inc=1, device_id={"seq": lax.rem(me + step, n)}, device_id_type=MESH
        )
    pl.semaphore_wait(barrier, n - 1)


def send_all(n, me, source, target, send_sem, recv_sem):
    copies = []
    for step in range(1, n):
        peer = lax.rem(me + step, n)
        copies.append(
            pltpu.make_async_remote_copy(
                src_ref=source(peer),
                dst_ref=target.at[me],
                send_sem=send_sem.at[step],
                recv_sem=recv_sem.at[step],
                device_id={"seq": peer},
                device_id_type=MESH,
            )
        )
        copies[-1].start()
    return copies


def rows_by_three(z, x_ref, xf_ref):
    for item in range(z.items):
        for slab in range(z.width // LANES):
            xf_ref[item, slab, 8:, :] = x_ref[item, :, slab * LANES : (slab + 1) * LANES].astype(
                jnp.float32
            )


def every_third(z, xf_ref, first):
    items = []
    for item in range(z.items):
        slabs = [
            xf_ref[item, slab, pl.ds(first, z.r, stride=3), :] for slab in range(z.width // LANES)
        ]
        items.append(jnp.concatenate(slabs, axis=1))
    return jnp.concatenate(items, axis=0)


def set_every_third(z, xf_ref, first, value):
    for item in range(z.items):
        for slab in range(z.width // LANES):
            xf_ref[item, slab, pl.ds(first, z.r, stride=3), :] = value[
                item * z.r : (item + 1) * z.r, slab * LANES : (slab + 1) * LANES
            ]


def forward_kernel(
    z,
    counts_ref,
    x_ref,
    pool_w,
    gain_ref,
    bias_ref,
    query_w,
    key_w,
    value_w,
    position_w,
    cb_ref,
    pb_ref,
    table_ref,
    pooled_ref,
    recv_ref,
    attn_in_ref,
    qc_ref,
    qp_ref,
    k_ref,
    v_ref,
    pos_ref,
    probs_ref,
    xf_ref,
    tail_ref,
    halo_ref,
    gather_ref,
    out_ref,
    halo_sems,
    gather_send,
    gather_recv,
    out_send,
    out_recv,
    own_sem,
):
    n, r, width, hd = z.n, z.r, z.width, z.hd
    me = lax.axis_index("seq")
    head = lax.rem(me, z.heads)
    group = lax.div(me, z.heads)
    greet(n, me)
    tail_ref[...] = x_ref[:, 3 * r - 16 :, :]
    halo = pltpu.make_async_remote_copy(
        src_ref=tail_ref,
        dst_ref=halo_ref,
        send_sem=halo_sems.at[0],
        recv_sem=halo_sems.at[1],
        device_id={"seq": lax.rem(me + 1, n)},
        device_id_type=MESH,
    )
    halo.start()
    rows_by_three(z, x_ref, xf_ref)
    halo.wait()
    for item in range(z.items):
        before = jnp.where(me > 0, halo_ref[item].astype(jnp.float32), 0.0)
        for slab in range(width // LANES):
            xf_ref[item, slab, 0:8, :] = before[8:16, slab * LANES : (slab + 1) * LANES]
    pooled = jnp.zeros((z.rows, width), jnp.float32)
    for part in range(3):
        pooled += dot(
            low(every_third(z, xf_ref, 6 + part)), pool_w[part * width : (part + 1) * width, :]
        )
    pooled_ref[...] = low(pooled).reshape(z.items, r, width)

    def items_of(peer):
        return pooled_ref.at[pl.ds(lax.div(peer, z.heads) * z.units, z.units)]

    copies = send_all(n, me, items_of, gather_ref, gather_send, gather_recv)
    gather_ref[me] = pooled_ref[pl.ds(group * z.units, z.units)]
    lane_pair = pl.multiple_of(lax.div(head * hd, LANES) * LANES, LANES)
    pair = pl.ds(lane_pair, LANES)
    turn = lax.rem(head * hd, LANES)

    def own_half(value):
        return pltpu.roll(value, LANES - turn, 1)[:, :hd]

    pos_ref[...] = low(own_half(dot(table_ref[...], position_w[:, pair])))
    for copy in copies:
        copy.wait()
    weights = jnp.concatenate([query_w[:, pair], key_w[:, pair], value_w[:, pair]], axis=1)
    content_bias = cb_ref[pl.ds(head, 1), :]
    position_bias = pb_ref[pl.ds(head, 1), :]
    for unit in range(z.units):
        normed, _ = norm_rows(gather_ref[:, unit].reshape(z.length, width).astype(jnp.float32))
        attn_in_ref[unit] = low(normed * gain_ref[...] + bias_ref[...])
        qkv = dot(attn_in_ref[unit], weights)
        queries = own_half(qkv[:, :LANES])
        qc_ref[unit] = low(queries + content_bias)
        qp_ref[unit] = low(queries + position_bias)
        k_ref[unit] = low(own_half(qkv[:, LANES : 2 * LANES]))
        v_ref[unit] = low(own_half(qkv[:, 2 * LANES :]))
    for block in range(z.length // BLOCK):
        lo, hi = block * BLOCK, (block + 1) * BLOCK
        sides = []
        for unit in range(z.units):
            count = counts_ref[group * z.units + unit]
            content = dot_nt(qc_ref[unit, lo:hi, :], k_ref[unit, :hi, :])
            by_distance = dot_nt(qp_ref[unit, lo:hi, :], pos_ref[z.length - hi :, :])
            placed = pltpu.roll(by_distance, lo + 1, 1, stride=1, stride_axis=0)
            query_at = lo + lax.broadcasted_iota(jnp.int32, (BLOCK, hi), 0)
            key_at = lax.broadcasted_iota(jnp.int32, (BLOCK, hi), 1)
            valid = (key_at <= query_at) & (key_at < count)
            logits = jnp.where(valid, (content + placed) * hd**-0.5, masked_value)
            raised = jnp.exp(logits - jnp.max(logits, axis=-1, keepdims=True))
            probs = raised / jnp.sum(raised, axis=-1, keepdims=True)
            probs_ref[unit, lo:hi, :hi] = probs
            sides.append(low(dot(low(probs), v_ref[unit, :hi, :])))
        sides += [jnp.zeros((BLOCK, hd), jnp.bfloat16)] * (LANES // hd - z.units)
        per = BLOCK // r
        out_ref[block * per : (block + 1) * per] = jnp.concatenate(sides, axis=1).reshape(
            per, r, LANES
        )
    copies = send_all(n, me, lambda peer: out_ref.at[peer], recv_ref, out_send, out_recv)
    own = pltpu.make_async_copy(out_ref.at[me], recv_ref.at[me], own_sem)
    own.start()
    for copy in copies:
        copy.wait()
    own.wait()


def live_rows(z, me, length, part):
    at = lax.broadcasted_iota(jnp.int32, (z.r, 1), 0) * 3 + part + me * 3 * z.r
    return (at < length).astype(jnp.float32)


def middle_kernel(
    z,
    lengths_ref,
    att_recv_ref,
    pooled_ref,
    x_ref,
    og_ref,
    output_w,
    gain_ref,
    bias_ref,
    inner_w,
    outer_w,
    up_w,
    block_ref,
    recv_ref,
    hidden_grad_ref,
    up_grad_ref,
    outer_grad_ref,
    inner_grad_ref,
    output_grad_ref,
    norm_grad_ref,
    xf_ref,
    att_ref,
    act_ref,
    slope_ref,
    inner_low_ref,
    up_rows_ref,
    out_ref,
    out_send,
    out_recv,
    own_sem,
):
    n, r, width, hd = z.n, z.r, z.width, z.hd
    me = lax.axis_index("seq")
    greet(n, me)
    ff = inner_w.shape[1]
    step = min(512, ff)

    def live(part):
        return jnp.concatenate(
            [live_rows(z, me, lengths_ref[item], part) for item in range(z.items)], axis=0
        )

    rows_by_three(z, og_ref, xf_ref)
    for part in range(3):
        up_rows_ref[:, part * width : (part + 1) * width] = low(
            every_third(z, xf_ref, 8 + part) * live(part)
        )
    summed_grad = low(dot_nt(up_rows_ref[...], up_w[...]))
    for source in range(n):
        for unit in range(z.units):
            item = source // z.heads * z.units + unit
            head = source % z.heads
            att_ref[item * r : (item + 1) * r, head * hd : (head + 1) * hd] = att_recv_ref[
                source, :, unit * hd : (unit + 1) * hd
            ]
    short = pooled_ref[...].reshape(z.rows, width).astype(jnp.float32)
    hidden = short + dot(att_ref[...], output_w[...])
    normed, inverse = norm_rows(hidden)
    ffn_in = low(normed * gain_ref[...] + bias_ref[...])
    for lo in range(0, ff, step):
        inner = dot(ffn_in, inner_w[:, lo : lo + step])
        normal_cdf = 0.5 * (1.0 + lax.erf(inner * 0.7071067811865476))
        density = jnp.exp(-0.5 * inner * inner) * 0.3989422804014327
        act_ref[:, lo : lo + step] = low(inner * normal_cdf)
        slope_ref[:, lo : lo + step] = normal_cdf + inner * density
    for lo in range(0, ff, step):
        inner_low_ref[:, lo : lo + step] = low(
            dot_nt(summed_grad, outer_w[lo : lo + step, :]) * slope_ref[:, lo : lo + step]
        )
    ffn_grad = dot_nt(inner_low_ref[...], inner_w[...])
    norm_grad_ref[0:1, :] = jnp.sum(ffn_grad * normed, axis=0, keepdims=True)
    norm_grad_ref[1:2, :] = jnp.sum(ffn_grad, axis=0, keepdims=True)
    hidden_grad = summed_grad.astype(jnp.float32) + norm_backward(
        ffn_grad, normed, inverse, gain_ref[...]
    )
    hidden_grad_ref[...] = hidden_grad
    branch = low(hidden_grad)
    att_grad = low(dot_nt(branch, output_w[...]))
    for target in range(n):
        head = target % z.heads
        sides = []
        for unit in range(z.units):
            item = target // z.heads * z.units + unit
            sides.append(att_grad[item * r : (item + 1) * r, head * hd : (head + 1) * hd])
        sides += [jnp.zeros((r, hd), jnp.bfloat16)] * (LANES // hd - z.units)
        out_ref[target] = jnp.concatenate(sides, axis=1)
    copies = send_all(n, me, lambda peer: out_ref.at[peer], recv_ref, out_send, out_recv)
    own = pltpu.make_async_copy(out_ref.at[me], recv_ref.at[me], own_sem)
    own.start()
    summed = low(hidden + dot(act_ref[...], outer_w[...]))
    rows_by_three(z, x_ref, xf_ref)
    for part in range(3):
        up = dot(summed, up_w[:, part * width : (part + 1) * width])
        set_every_third(
            z, xf_ref, 8 + part, every_third(z, xf_ref, 8 + part) + up * live(part)
        )
    for item in range(z.items):
        for slab in range(width // LANES):
            block_ref[item, :, slab * LANES : (slab + 1) * LANES] = low(xf_ref[item, slab, 8:, :])
    for part in range(3):
        cut = slice(part * width, (part + 1) * width)
        up_grad_ref[:, cut] = low(dot_tn(summed, up_rows_ref[:, cut]))
    for lo in range(0, ff, step):
        cut = slice(lo, lo + step)
        outer_grad_ref[cut, :] = low(dot_tn(act_ref[:, cut], summed_grad))
        inner_grad_ref[:, cut] = low(dot_tn(ffn_in, inner_low_ref[:, cut]))
    output_grad_ref[...] = low(dot_tn(att_ref[...], branch))
    for copy in copies:
        copy.wait()
    own.wait()


def reversal():
    at = lax.broadcasted_iota(jnp.int32, (BLOCK, BLOCK), 0)
    across = lax.broadcasted_iota(jnp.int32, (BLOCK, BLOCK), 1)
    return low((at + across == BLOCK - 1).astype(jnp.float32))


def backward_kernel(
    z,
    grad_recv_ref,
    attn_in_ref,
    qc_ref,
    qp_ref,
    k_ref,
    v_ref,
    pos_ref,
    probs_ref,
    table_ref,
    recv_ref,
    head_grad_ref,
    bias_grad_ref,
    query_grad_ref,
    key_t_ref,
    value_t_ref,
    table_t_ref,
    out_ref,
    out_send,
    out_recv,
    own_sem,
):
    n, r, hd = z.n, z.r, z.hd
    length = z.length
    me = lax.axis_index("seq")
    greet(n, me)
    flip = reversal()
    content_sum = jnp.zeros((1, hd), jnp.float32)
    position_sum = jnp.zeros((1, hd), jnp.float32)
    key_t_ref[...] = jnp.zeros_like(key_t_ref)
    value_t_ref[...] = jnp.zeros_like(value_t_ref)
    table_t_ref[...] = jnp.zeros_like(table_t_ref)
    for unit in range(z.units):
        att_grad = grad_recv_ref[:, :, unit * hd : (unit + 1) * hd].reshape(length, hd)
        for block in range(length // BLOCK):
            lo, hi = block * BLOCK, (block + 1) * BLOCK
            block_grad = att_grad[lo:hi]
            probs = probs_ref[unit, lo:hi, :hi]
            prob_grad = dot_nt(block_grad, v_ref[unit, :hi, :])
            delta = jnp.sum(probs * prob_grad, axis=-1, keepdims=True)
            raw = low(probs * (prob_grad - delta) * hd**-0.5)
            content = dot(raw, k_ref[unit, :hi, :])
            key_t_ref[unit, :, :hi] += dot_tn(qc_ref[unit, lo:hi, :], raw)
            value_t_ref[unit, :, :hi] += dot_tn(block_grad, low(probs))
            by_distance = low(pltpu.roll(dot(flip, raw), 0, 1, stride=1, stride_axis=0))
            position = dot(by_distance, pos_ref[length - hi :, :])
            upper = low(position)
            lower = low(position - upper.astype(jnp.float32))
            position = dot(flip, upper) + dot(flip, lower)
            flipped_q = low(dot(flip, qp_ref[unit, lo:hi, :]))
            table_t_ref[unit, :, length - hi :] += dot_tn(flipped_q, by_distance)
            content_sum += jnp.sum(content, axis=0, keepdims=True)
            position_sum += jnp.sum(position, axis=0, keepdims=True)
            query_grad_ref[unit, lo:hi, :] = low(content + position)
    bias_grad_ref[0:1, :] = content_sum
    bias_grad_ref[1:2, :] = position_sum
    pad = [jnp.zeros((length, hd), jnp.bfloat16)] * (LANES // hd - z.units)
    sides = [query_grad_ref[unit] for unit in range(z.units)] + pad
    sides += [low(key_t_ref[unit].T) for unit in range(z.units)] + pad
    sides += [low(value_t_ref[unit].T) for unit in range(z.units)] + pad
    out_ref[...] = jnp.concatenate(sides, axis=1).reshape(n, r, 3 * LANES)
    copies = send_all(n, me, lambda peer: out_ref.at[peer], recv_ref, out_send, out_recv)
    own = pltpu.make_async_copy(out_ref.at[me], recv_ref.at[me], own_sem)
    own.start()
    query_sum = key_sum = value_sum = table_sum = 0.0
    for unit in range(z.units):
        query_sum += dot_tn(query_grad_ref[unit], attn_in_ref[unit])
        key_sum += dot(low(key_t_ref[unit]), attn_in_ref[unit])
        value_sum += dot(low(value_t_ref[unit]), attn_in_ref[unit])
        table_sum += dot(low(table_t_ref[unit]), table_ref[...])
    head_grad_ref[...] = jnp.concatenate([query_sum, key_sum, value_sum, table_sum], axis=0)
    for copy in copies:
        copy.wait()
    own.wait()


def last_kernel(
    z,
    recv_ref,
    hidden_grad_ref,
    pooled_ref,
    x_ref,
    og_ref,
    gain_ref,
    query_w,
    key_w,
    value_w,
    pool_w,
    input_grad_ref,
    pool_grad_ref,
    norm_grad_ref,
    xf_ref,
    of_ref,
    dq_ref,
    grad_ref,
    head_ref,
    halo_ref,
    halo_sems,
):
    n, r, width, hd = z.n, z.r, z.width, z.hd
    me = lax.axis_index("seq")
    greet(n, me)
    for source in range(n):
        for unit in range(z.units):
            item = source // z.heads * z.units + unit
            head = source % z.heads
            for which in range(3):
                dq_ref[which, item * r : (item + 1) * r, head * hd : (head + 1) * hd] = recv_ref[
                    source, :, which * LANES + unit * hd : which * LANES + (unit + 1) * hd
                ]
    attn_grad = (
        dot_nt(dq_ref[0], query_w[...])
        + dot_nt(dq_ref[1], key_w[...])
        + dot_nt(dq_ref[2], value_w[...])
    )
    normed, inverse = norm_rows(pooled_ref[...].reshape(z.rows, width).astype(jnp.float32))
    norm_grad_ref[0:1, :] = jnp.sum(attn_grad * normed, axis=0, keepdims=True)
    norm_grad_ref[1:2, :] = jnp.sum(attn_grad, axis=0, keepdims=True)
    short_grad = low(
        hidden_grad_ref[...] + norm_backward(attn_grad, normed, inverse, gain_ref[...])
    )
    for item in range(z.items):
        head_ref[item] = short_grad[item * r : item * r + 16, :]
        grad_ref[item, 0:r, :] = short_grad[item * r : (item + 1) * r, :].astype(jnp.float32)
    halo = pltpu.make_async_remote_copy(
        src_ref=head_ref,
        dst_ref=halo_ref,
        send_sem=halo_sems.at[0],
        recv_sem=halo_sems.at[1],
        device_id={"seq": lax.rem(me + n - 1, n)},
        device_id_type=MESH,
    )
    halo.start()
    rows_by_three(z, x_ref, xf_ref)
    rows_by_three(z, og_ref, of_ref)
    pool_grad_ref[2 * width :, :] = low(dot_tn(low(every_third(z, xf_ref, 8)), short_grad))
    own = dot_nt(short_grad, pool_w[2 * width :, :])
    set_every_third(z, of_ref, 8, every_third(z, of_ref, 8) + own)
    halo.wait()
    for item in range(z.items):
        after = jnp.where(me < n - 1, halo_ref[item].astype(jnp.float32), 0.0)
        grad_ref[item, r : r + 8, :] = after[0:8, :]
    later = low(
        jnp.concatenate([grad_ref[item, 1 : r + 1, :] for item in range(z.items)], axis=0)
    )
    for part in range(2):
        cut = slice(part * width, (part + 1) * width)
        first = 9 + part
        pool_grad_ref[cut, :] = low(dot_tn(low(every_third(z, xf_ref, first)), later))
        back = dot_nt(later, pool_w[cut, :])
        set_every_third(z, of_ref, first, every_third(z, of_ref, first) + back)
    for item in range(z.items):
        for slab in range(width // LANES):
            input_grad_ref[item, :, slab * LANES : (slab + 1) * LANES] = of_ref[item, slab, 8:, :]


def call(kernel, z, collective_id, ins, outs, scratch, args):
    return pl.pallas_call(
        functools.partial(kernel, z),
        out_shape=[jax.ShapeDtypeStruct(shape, dtype) for shape, dtype, _ in outs],
        in_specs=ins,
        out_specs=[space for _, _, space in outs],
        scratch_shapes=scratch,
        compiler_params=pltpu.CompilerParams(
            collective_id=collective_id, has_side_effects=True, vmem_limit_bytes=50 * 2**20
        ),
    )(*args)


def body(
    byte_rows,
    item_lengths,
    out_grad,
    pool_weight,
    norm1_gain,
    norm1_bias,
    query_weight,
    key_weight,
    value_weight,
    position_weight,
    content_bias,
    position_bias,
    output_weight,
    norm2_gain,
    norm2_bias,
    inner_weight,
    outer_weight,
    upsample_weight,
):
    items, full_rows, width = byte_rows.shape
    heads, hd = content_bias.shape
    n = lax.axis_size("seq")
    ff = inner_weight.shape[1]
    z = Sizes(n, items, full_rows, width, heads)
    r, units, length, rows = z.r, z.units, z.length, z.rows
    bf, f4 = jnp.bfloat16, jnp.float32
    slabs = width // LANES
    dma = pltpu.SemaphoreType.DMA
    counts = item_lengths // 3
    table = distance_table(length, width)
    gain1, bias1 = norm1_gain.reshape(1, width), norm1_bias.reshape(1, width)
    gain2, bias2 = norm2_gain.reshape(1, width), norm2_bias.reshape(1, width)
    xf = pltpu.VMEM((items, slabs, 3 * r + 8, LANES), f4)
    (pooled, att_recv, attn_in, qc, qp, keys, values, positions, probs) = call(
        forward_kernel,
        z,
        0,
        [SMEM] + [VMEM] * 11,
        [
            ((items, r, width), bf, VMEM),
            ((n, r, LANES), bf, ANY),
            ((units, length, width), bf, VMEM),
            ((units, length, hd), bf, VMEM),
            ((units, length, hd), bf, VMEM),
            ((units, length, hd), bf, VMEM),
            ((units, length, hd), bf, VMEM),
            ((length, hd), bf, VMEM),
            ((units, length, length), f4, VMEM),
        ],
        [
            xf,
            pltpu.VMEM((items, 16, width), bf),
            pltpu.VMEM((items, 16, width), bf),
            pltpu.VMEM((n, units, r, width), bf),
            pltpu.VMEM((n, r, LANES), bf),
            dma((2,)),
            dma((n,)),
            dma((n,)),
            dma((n,)),
            dma((n,)),
            dma,
        ],
        (
            counts,
            byte_rows,
            pool_weight,
            gain1,
            bias1,
            query_weight,
            key_weight,
            value_weight,
            position_weight,
            content_bias,
            position_bias,
            table,
        ),
    )
    (block_out, grad_recv, hidden_grad, up_g, outer_g, inner_g, output_g, norm2_g) = call(
        middle_kernel,
        z,
        1,
        [SMEM] + [VMEM] * 10,
        [
            ((items, full_rows, width), bf, VMEM),
            ((n, r, LANES), bf, ANY),
            ((rows, width), f4, VMEM),
            ((width, 3 * width), bf, VMEM),
            ((ff, width), bf, VMEM),
            ((width, ff), bf, VMEM),
            ((width, width), bf, VMEM),
            ((2, width), f4, VMEM),
        ],
        [
            xf,
            pltpu.VMEM((rows, width), bf),
            pltpu.VMEM((rows, ff), bf),
            pltpu.VMEM((rows, ff), f4),
            pltpu.VMEM((rows, ff), bf),
            pltpu.VMEM((rows, 3 * width), bf),
            pltpu.VMEM((n, r, LANES), bf),
            dma((n,)),
            dma((n,)),
            dma,
        ],
        (
            item_lengths,
            att_recv,
            pooled,
            byte_rows,
            out_grad,
            output_weight,
            gain2,
            bias2,
            inner_weight,
            outer_weight,
            upsample_weight,
        ),
    )
    qkv_recv, head_g, head_bias_g = call(
        backward_kernel,
        z,
        2,
        [VMEM] * 9,
        [
            ((n, r, 3 * LANES), bf, ANY),
            ((4 * hd, width), f4, VMEM),
            ((2, hd), f4, VMEM),
        ],
        [
            pltpu.VMEM((units, length, hd), bf),
            pltpu.VMEM((units, hd, length), f4),
            pltpu.VMEM((units, hd, length), f4),
            pltpu.VMEM((units, hd, length), f4),
            pltpu.VMEM((n, r, 3 * LANES), bf),
            dma((n,)),
            dma((n,)),
            dma,
        ],
        (grad_recv, attn_in, qc, qp, keys, values, positions, probs, table),
    )
    input_grad, pool_g, norm1_g = call(
        last_kernel,
        z,
        3,
        [VMEM] * 10,
        [
            ((items, full_rows, width), f4, VMEM),
            ((3 * width, width), bf, VMEM),
            ((2, width), f4, VMEM),
        ],
        [
            xf,
            xf,
            pltpu.VMEM((3, rows, width), bf),
            pltpu.VMEM((items, r + 8, width), f4),
            pltpu.VMEM((items, 16, width), bf),
            pltpu.VMEM((items, 16, width), bf),
            dma((2,)),
        ],
        (
            qkv_recv,
            hidden_grad,
            pooled,
            byte_rows,
            out_grad,
            gain1,
            query_weight,
            key_weight,
            value_weight,
            pool_weight,
        ),
    )
    dense = lax.psum((pool_g, up_g, outer_g, inner_g, output_g), ("batch", "seq"))
    pool_t, up_t, outer_t, inner_t, output_t = (value.astype(f4) for value in dense)
    norm_t = lax.psum(jnp.concatenate([norm1_g, norm2_g]), ("batch", "seq"))
    head_t = lax.all_gather(lax.psum(head_g.astype(bf), "batch"), "seq", axis=0)
    head_t = jnp.sum(head_t.reshape(n // heads, heads, 4, hd, width).astype(f4), axis=0)
    head_t = head_t.transpose(1, 3, 0, 2).reshape(4, width, width)
    bias_t = lax.all_gather(lax.psum(head_bias_g, "batch"), "seq", axis=0)
    bias_t = jnp.sum(bias_t.reshape(n // heads, heads, 2, hd), axis=0)
    return (
        block_out,
        input_grad,
        pool_t,
        norm_t[0],
        norm_t[1],
        head_t[0],
        head_t[1],
        head_t[2],
        head_t[3],
        bias_t[:, 0],
        bias_t[:, 1],
        output_t,
        norm_t[2],
        norm_t[3],
        inner_t,
        outer_t,
        up_t,
    )


def solution(mesh):
    split = P("batch", "seq", None)
    in_specs = (split, P("batch"), split) + (P(),) * 15
    out_specs = (split, split) + (P(),) * 15
    return jax.shard_map(body, mesh=mesh, in_specs=in_specs, out_specs=out_specs, check_vma=False)
```

```python
import functools

import jax
import jax.numpy as jnp
import numpy as np
from jax import lax
from jax.experimental import pallas as pl
from jax.experimental.pallas import tpu as pltpu
from jax.sharding import PartitionSpec as P

MESH = pl.DeviceIdType.MESH
epsilon = 1e-05
masked_value = -1e30
CHAIN_ROWS = [1024, 1536, 512, 512, 512, 1536, 512, 512, 512, 512, 512, 512, 512]
CHAIN_ORDER = [2, 1, 0, 8, 4, 0, 1, 3, 1, 0, 4, 9, 5]
BLOCK = 128
LANES = 128
VMEM = pl.BlockSpec(memory_space=pltpu.VMEM)
SMEM = pl.BlockSpec(memory_space=pltpu.SMEM)
ANY = pl.BlockSpec(memory_space=pl.ANY)


def dot(left, right):
    return jnp.dot(left, right, preferred_element_type=jnp.float32)


def dot_nt(left, right):
    return lax.dot_general(
        left, right, (((1,), (1,)), ((), ())), preferred_element_type=jnp.float32
    )


def dot_tn(left, right):
    return lax.dot_general(
        left, right, (((0,), (0,)), ((), ())), preferred_element_type=jnp.float32
    )


def low(value):
    return value.astype(jnp.bfloat16)


def distance_table(short_len, width):
    distance = (short_len - 1 - np.arange(short_len)).astype(np.float32)
    steps_in = np.arange(0, width, 2).astype(np.float32)
    frequency = np.exp(-np.log(np.float32(10000.0)) * steps_in / np.float32(width))
    angles = distance[:, None] * frequency[None, :].astype(np.float32)
    both = np.concatenate([np.sin(angles), np.cos(angles)], axis=1)
    return jnp.asarray(both.astype(jnp.bfloat16))


def norm_rows(rows):
    mean = jnp.mean(rows, axis=-1, keepdims=True)
    centered = rows - mean
    inverse = lax.rsqrt(jnp.mean(centered * centered, axis=-1, keepdims=True) + epsilon)
    return centered * inverse, inverse


def norm_backward(gradient, normed, inverse, gain):
    scaled = gradient * gain
    return inverse * (
        scaled
        - jnp.mean(scaled, axis=-1, keepdims=True)
        - normed * jnp.mean(scaled * normed, axis=-1, keepdims=True)
    )


class Sizes:
    def __init__(self, n, items, full_rows, width, heads):
        self.n = n
        self.items = items
        self.r = full_rows // 3
        self.width = width
        self.heads = heads
        self.hd = width // heads
        self.units = items * heads // n
        self.length = n * self.r
        self.rows = items * self.r
        assert n % heads == 0 and self.units * self.hd <= LANES


def greet(n, me):
    barrier = pltpu.get_barrier_semaphore()
    for step in range(1, n):
        pl.semaphore_signal(
            barrier, inc=1, device_id={"seq": lax.rem(me + step, n)}, device_id_type=MESH
        )
    pl.semaphore_wait(barrier, n - 1)


def send_all(n, me, source, target, send_sem, recv_sem):
    copies = []
    for step in range(1, n):
        peer = lax.rem(me + step, n)
        copies.append(
            pltpu.make_async_remote_copy(
                src_ref=source(peer),
                dst_ref=target.at[me],
                send_sem=send_sem.at[step],
                recv_sem=recv_sem.at[step],
                device_id={"seq": peer},
                device_id_type=MESH,
            )
        )
        copies[-1].start()
    return copies


def rows_by_three(z, x_ref, xf_ref):
    for item in range(z.items):
        for slab in range(z.width // LANES):
            xf_ref[item, slab, 8:, :] = x_ref[item, :, slab * LANES : (slab + 1) * LANES].astype(
                jnp.float32
            )


def every_third(z, xf_ref, first):
    items = []
    for item in range(z.items):
        slabs = [
            xf_ref[item, slab, pl.ds(first, z.r, stride=3), :] for slab in range(z.width // LANES)
        ]
        items.append(jnp.concatenate(slabs, axis=1))
    return jnp.concatenate(items, axis=0)


def set_every_third(z, xf_ref, first, value):
    for item in range(z.items):
        for slab in range(z.width // LANES):
            xf_ref[item, slab, pl.ds(first, z.r, stride=3), :] = value[
                item * z.r : (item + 1) * z.r, slab * LANES : (slab + 1) * LANES
            ]


def forward_kernel(
    z,
    counts_ref,
    x_ref,
    pool_w,
    gain_ref,
    bias_ref,
    query_w,
    key_w,
    value_w,
    position_w,
    cb_ref,
    pb_ref,
    table_ref,
    pooled_ref,
    recv_ref,
    qc_ref,
    qp_ref,
    k_ref,
    v_ref,
    pos_ref,
    probs_ref,
    xf_ref,
    tail_ref,
    halo_ref,
    qkv_out_ref,
    qkv_ref,
    out_ref,
    halo_sems,
    qkv_send,
    qkv_recv,
    out_send,
    out_recv,
    own_sem,
):
    n, r, width, hd = z.n, z.r, z.width, z.hd
    me = lax.axis_index("seq")
    head = lax.rem(me, z.heads)
    group = lax.div(me, z.heads)
    greet(n, me)
    tail_ref[...] = x_ref[:, 3 * r - 16 :, :]
    halo = pltpu.make_async_remote_copy(
        src_ref=tail_ref,
        dst_ref=halo_ref,
        send_sem=halo_sems.at[0],
        recv_sem=halo_sems.at[1],
        device_id={"seq": lax.rem(me + 1, n)},
        device_id_type=MESH,
    )
    halo.start()
    rows_by_three(z, x_ref, xf_ref)
    halo.wait()
    for item in range(z.items):
        before = jnp.where(me > 0, halo_ref[item].astype(jnp.float32), 0.0)
        for slab in range(width // LANES):
            xf_ref[item, slab, 0:8, :] = before[8:16, slab * LANES : (slab + 1) * LANES]
    pooled = jnp.zeros((z.rows, width), jnp.float32)
    for part in range(3):
        pooled += dot(
            low(every_third(z, xf_ref, 6 + part)), pool_w[part * width : (part + 1) * width, :]
        )
    short = low(pooled)
    pooled_ref[...] = short.reshape(z.items, r, width)
    normed, _ = norm_rows(short.astype(jnp.float32))
    attn_in = low(normed * gain_ref[...] + bias_ref[...])
    qkv = [low(dot(attn_in, w[...])) for w in (query_w, key_w, value_w)]
    pad = [jnp.zeros((r, hd), jnp.bfloat16)] * (LANES // hd - z.units)
    for target in range(n):
        sides = []
        lanes = slice(target % z.heads * hd, (target % z.heads + 1) * hd)
        for value in qkv:
            for unit in range(z.units):
                item = target // z.heads * z.units + unit
                sides.append(value[item * r : (item + 1) * r, lanes])
            sides += pad
        qkv_out_ref[target] = jnp.concatenate(sides, axis=1)
    copies = send_all(n, me, lambda peer: qkv_out_ref.at[peer], qkv_ref, qkv_send, qkv_recv)
    qkv_ref[me] = qkv_out_ref[me]
    lane_pair = pl.multiple_of(lax.div(head * hd, LANES) * LANES, LANES)
    turn = lax.rem(head * hd, LANES)
    both = dot(table_ref[...], position_w[:, pl.ds(lane_pair, LANES)])
    pos_ref[...] = low(pltpu.roll(both, LANES - turn, 1)[:, :hd])
    content_bias = cb_ref[pl.ds(head, 1), :]
    position_bias = pb_ref[pl.ds(head, 1), :]
    for copy in copies:
        copy.wait()
    for unit in range(z.units):
        queries, keys, values = (
            qkv_ref[:, :, which * LANES + unit * hd : which * LANES + (unit + 1) * hd].reshape(
                z.length, hd
            )
            for which in range(3)
        )
        qc_ref[unit] = low(queries.astype(jnp.float32) + content_bias)
        qp_ref[unit] = low(queries.astype(jnp.float32) + position_bias)
        k_ref[unit] = keys
        v_ref[unit] = values
    for block in range(z.length // BLOCK):
        lo, hi = block * BLOCK, (block + 1) * BLOCK
        sides = []
        for unit in range(z.units):
            count = counts_ref[group * z.units + unit]
            content = dot_nt(qc_ref[unit, lo:hi, :], k_ref[unit, :hi, :])
            by_distance = dot_nt(qp_ref[unit, lo:hi, :], pos_ref[z.length - hi :, :])
            placed = pltpu.roll(by_distance, lo + 1, 1, stride=1, stride_axis=0)
            query_at = lo + lax.broadcasted_iota(jnp.int32, (BLOCK, hi), 0)
            key_at = lax.broadcasted_iota(jnp.int32, (BLOCK, hi), 1)
            valid = (key_at <= query_at) & (key_at < count)
            logits = jnp.where(valid, (content + placed) * hd**-0.5, masked_value)
            raised = jnp.exp(logits - jnp.max(logits, axis=-1, keepdims=True))
            probs = raised / jnp.sum(raised, axis=-1, keepdims=True)
            probs_ref[unit, lo:hi, :hi] = probs
            sides.append(low(dot(low(probs), v_ref[unit, :hi, :])))
        sides += [jnp.zeros((BLOCK, hd), jnp.bfloat16)] * (LANES // hd - z.units)
        per = BLOCK // r
        out_ref[block * per : (block + 1) * per] = jnp.concatenate(sides, axis=1).reshape(
            per, r, LANES
        )
    copies = send_all(n, me, lambda peer: out_ref.at[peer], recv_ref, out_send, out_recv)
    own = pltpu.make_async_copy(out_ref.at[me], recv_ref.at[me], own_sem)
    own.start()
    for copy in copies:
        copy.wait()
    own.wait()


def live_rows(z, me, length, part):
    at = lax.broadcasted_iota(jnp.int32, (z.r, 1), 0) * 3 + part + me * 3 * z.r
    return (at < length).astype(jnp.float32)


def middle_kernel(
    z,
    lengths_ref,
    att_recv_ref,
    pooled_ref,
    x_ref,
    og_ref,
    output_w,
    gain_ref,
    bias_ref,
    inner_w,
    outer_w,
    up_w,
    block_ref,
    recv_ref,
    hidden_grad_ref,
    early_ref,
    norm_grad_ref,
    xf_ref,
    att_ref,
    act_ref,
    slope_ref,
    inner_low_ref,
    up_rows_ref,
    out_ref,
    out_send,
    out_recv,
    own_sem,
):
    n, r, width, hd = z.n, z.r, z.width, z.hd
    me = lax.axis_index("seq")
    greet(n, me)
    ff = inner_w.shape[1]
    step = min(512, ff)

    def live(part):
        return jnp.concatenate(
            [live_rows(z, me, lengths_ref[item], part) for item in range(z.items)], axis=0
        )

    rows_by_three(z, og_ref, xf_ref)
    for part in range(3):
        up_rows_ref[:, part * width : (part + 1) * width] = low(
            every_third(z, xf_ref, 8 + part) * live(part)
        )
    summed_grad = low(dot_nt(up_rows_ref[...], up_w[...]))
    for source in range(n):
        for unit in range(z.units):
            item = source // z.heads * z.units + unit
            head = source % z.heads
            att_ref[item * r : (item + 1) * r, head * hd : (head + 1) * hd] = att_recv_ref[
                source, :, unit * hd : (unit + 1) * hd
            ]
    short = pooled_ref[...].reshape(z.rows, width).astype(jnp.float32)
    hidden = short + dot(att_ref[...], output_w[...])
    normed, inverse = norm_rows(hidden)
    ffn_in = low(normed * gain_ref[...] + bias_ref[...])
    for lo in range(0, ff, step):
        inner = dot(ffn_in, inner_w[:, lo : lo + step])
        normal_cdf = 0.5 * (1.0 + lax.erf(inner * 0.7071067811865476))
        density = jnp.exp(-0.5 * inner * inner) * 0.3989422804014327
        act_ref[:, lo : lo + step] = low(inner * normal_cdf)
        slope_ref[:, lo : lo + step] = normal_cdf + inner * density
    for lo in range(0, ff, step):
        inner_low_ref[:, lo : lo + step] = low(
            dot_nt(summed_grad, outer_w[lo : lo + step, :]) * slope_ref[:, lo : lo + step]
        )
    ffn_grad = dot_nt(inner_low_ref[...], inner_w[...])
    norm_grad_ref[0:1, :] = jnp.sum(ffn_grad * normed, axis=0, keepdims=True)
    norm_grad_ref[1:2, :] = jnp.sum(ffn_grad, axis=0, keepdims=True)
    hidden_grad = summed_grad.astype(jnp.float32) + norm_backward(
        ffn_grad, normed, inverse, gain_ref[...]
    )
    hidden_grad_ref[...] = hidden_grad
    branch = low(hidden_grad)
    att_grad = low(dot_nt(branch, output_w[...]))
    for target in range(n):
        head = target % z.heads
        sides = []
        for unit in range(z.units):
            item = target // z.heads * z.units + unit
            sides.append(att_grad[item * r : (item + 1) * r, head * hd : (head + 1) * hd])
        sides += [jnp.zeros((r, hd), jnp.bfloat16)] * (LANES // hd - z.units)
        out_ref[target] = jnp.concatenate(sides, axis=1)
    copies = send_all(n, me, lambda peer: out_ref.at[peer], recv_ref, out_send, out_recv)
    own = pltpu.make_async_copy(out_ref.at[me], recv_ref.at[me], own_sem)
    own.start()
    summed = low(hidden + dot(act_ref[...], outer_w[...]))
    rows_by_three(z, x_ref, xf_ref)
    for part in range(3):
        up = dot(summed, up_w[:, part * width : (part + 1) * width])
        set_every_third(
            z, xf_ref, 8 + part, every_third(z, xf_ref, 8 + part) + up * live(part)
        )
    for item in range(z.items):
        for slab in range(width // LANES):
            block_ref[item, :, slab * LANES : (slab + 1) * LANES] = low(xf_ref[item, slab, 8:, :])
    for part in range(3):
        cut = slice(part * width, (part + 1) * width)
        early_ref[cut, :] = low(dot_tn(summed, up_rows_ref[:, cut]))
    for lo in range(0, ff, width):
        cut = slice(lo, lo + width)
        at = 3 * width + lo
        early_ref[at : at + width, :] = low(dot_tn(act_ref[:, cut], summed_grad))
        at += ff
        early_ref[at : at + width, :] = low(dot_tn(ffn_in, inner_low_ref[:, cut]))
    early_ref[3 * width + 2 * ff :, :] = low(dot_tn(att_ref[...], branch))
    for copy in copies:
        copy.wait()
    own.wait()


def reversal():
    at = lax.broadcasted_iota(jnp.int32, (BLOCK, BLOCK), 0)
    across = lax.broadcasted_iota(jnp.int32, (BLOCK, BLOCK), 1)
    return low((at + across == BLOCK - 1).astype(jnp.float32))


def backward_kernel(
    z,
    grad_recv_ref,
    qc_ref,
    qp_ref,
    k_ref,
    v_ref,
    pos_ref,
    probs_ref,
    table_ref,
    recv_ref,
    head_grad_ref,
    bias_grad_ref,
    query_grad_ref,
    key_t_ref,
    value_t_ref,
    table_t_ref,
    out_ref,
    out_send,
    out_recv,
    own_sem,
):
    n, r, hd = z.n, z.r, z.hd
    length = z.length
    me = lax.axis_index("seq")
    greet(n, me)
    flip = reversal()
    content_sum = jnp.zeros((1, hd), jnp.float32)
    position_sum = jnp.zeros((1, hd), jnp.float32)
    key_t_ref[...] = jnp.zeros_like(key_t_ref)
    value_t_ref[...] = jnp.zeros_like(value_t_ref)
    table_t_ref[...] = jnp.zeros_like(table_t_ref)
    for unit in range(z.units):
        att_grad = grad_recv_ref[:, :, unit * hd : (unit + 1) * hd].reshape(length, hd)
        for block in range(length // BLOCK):
            lo, hi = block * BLOCK, (block + 1) * BLOCK
            block_grad = att_grad[lo:hi]
            probs = probs_ref[unit, lo:hi, :hi]
            prob_grad = dot_nt(block_grad, v_ref[unit, :hi, :])
            delta = jnp.sum(probs * prob_grad, axis=-1, keepdims=True)
            raw = low(probs * (prob_grad - delta) * hd**-0.5)
            content = dot(raw, k_ref[unit, :hi, :])
            key_t_ref[unit, :, :hi] += dot_tn(qc_ref[unit, lo:hi, :], raw)
            value_t_ref[unit, :, :hi] += dot_tn(block_grad, low(probs))
            by_distance = low(pltpu.roll(dot(flip, raw), 0, 1, stride=1, stride_axis=0))
            position = dot(by_distance, pos_ref[length - hi :, :])
            upper = low(position)
            lower = low(position - upper.astype(jnp.float32))
            position = dot(flip, upper) + dot(flip, lower)
            flipped_q = low(dot(flip, qp_ref[unit, lo:hi, :]))
            table_t_ref[unit, :, length - hi :] += dot_tn(flipped_q, by_distance)
            content_sum += jnp.sum(content, axis=0, keepdims=True)
            position_sum += jnp.sum(position, axis=0, keepdims=True)
            query_grad_ref[unit, lo:hi, :] = low(content + position)
    bias_grad_ref[0:1, :] = content_sum
    bias_grad_ref[1:2, :] = position_sum
    pad = [jnp.zeros((length, hd), jnp.bfloat16)] * (LANES // hd - z.units)
    sides = [query_grad_ref[unit] for unit in range(z.units)] + pad
    sides += [low(key_t_ref[unit].T) for unit in range(z.units)] + pad
    sides += [low(value_t_ref[unit].T) for unit in range(z.units)] + pad
    out_ref[...] = jnp.concatenate(sides, axis=1).reshape(n, r, 3 * LANES)
    copies = send_all(n, me, lambda peer: out_ref.at[peer], recv_ref, out_send, out_recv)
    own = pltpu.make_async_copy(out_ref.at[me], recv_ref.at[me], own_sem)
    own.start()
    table_sum = 0.0
    for unit in range(z.units):
        table_sum += dot(low(table_t_ref[unit]), table_ref[...])
    head_grad_ref[...] = low(table_sum)
    for copy in copies:
        copy.wait()
    own.wait()


def last_kernel(
    z,
    recv_ref,
    hidden_grad_ref,
    pooled_ref,
    x_ref,
    og_ref,
    gain_ref,
    bias_ref,
    query_w,
    key_w,
    value_w,
    pool_w,
    input_grad_ref,
    late_ref,
    norm_grad_ref,
    xf_ref,
    of_ref,
    dq_ref,
    grad_ref,
    head_ref,
    halo_ref,
    halo_sems,
):
    n, r, width, hd = z.n, z.r, z.width, z.hd
    me = lax.axis_index("seq")
    greet(n, me)
    for source in range(n):
        for unit in range(z.units):
            item = source // z.heads * z.units + unit
            head = source % z.heads
            for which in range(3):
                dq_ref[which, item * r : (item + 1) * r, head * hd : (head + 1) * hd] = recv_ref[
                    source, :, which * LANES + unit * hd : which * LANES + (unit + 1) * hd
                ]
    attn_grad = (
        dot_nt(dq_ref[0], query_w[...])
        + dot_nt(dq_ref[1], key_w[...])
        + dot_nt(dq_ref[2], value_w[...])
    )
    normed, inverse = norm_rows(pooled_ref[...].reshape(z.rows, width).astype(jnp.float32))
    norm_grad_ref[0:1, :] = jnp.sum(attn_grad * normed, axis=0, keepdims=True)
    norm_grad_ref[1:2, :] = jnp.sum(attn_grad, axis=0, keepdims=True)
    short_grad = low(
        hidden_grad_ref[...] + norm_backward(attn_grad, normed, inverse, gain_ref[...])
    )
    for item in range(z.items):
        head_ref[item] = short_grad[item * r : item * r + 16, :]
        grad_ref[item, 0:r, :] = short_grad[item * r : (item + 1) * r, :].astype(jnp.float32)
    halo = pltpu.make_async_remote_copy(
        src_ref=head_ref,
        dst_ref=halo_ref,
        send_sem=halo_sems.at[0],
        recv_sem=halo_sems.at[1],
        device_id={"seq": lax.rem(me + n - 1, n)},
        device_id_type=MESH,
    )
    halo.start()
    attn_in = low(normed * gain_ref[...] + bias_ref[...])
    for which in range(3):
        at = (3 + which) * width
        late_ref[at : at + width, :] = low(dot_tn(attn_in, dq_ref[which]))
    rows_by_three(z, x_ref, xf_ref)
    rows_by_three(z, og_ref, of_ref)
    late_ref[2 * width : 3 * width, :] = low(dot_tn(low(every_third(z, xf_ref, 8)), short_grad))
    own = dot_nt(short_grad, pool_w[2 * width :, :])
    set_every_third(z, of_ref, 8, every_third(z, of_ref, 8) + own)
    halo.wait()
    for item in range(z.items):
        after = jnp.where(me < n - 1, halo_ref[item].astype(jnp.float32), 0.0)
        grad_ref[item, r : r + 8, :] = after[0:8, :]
    later = low(
        jnp.concatenate([grad_ref[item, 1 : r + 1, :] for item in range(z.items)], axis=0)
    )
    for part in range(2):
        cut = slice(part * width, (part + 1) * width)
        first = 9 + part
        late_ref[cut, :] = low(dot_tn(low(every_third(z, xf_ref, first)), later))
        back = dot_nt(later, pool_w[cut, :])
        set_every_third(z, of_ref, first, every_third(z, of_ref, first) + back)
    for item in range(z.items):
        for slab in range(width // LANES):
            input_grad_ref[item, :, slab * LANES : (slab + 1) * LANES] = of_ref[item, slab, 8:, :]


class Copies:
    def __init__(self, batch_size, seq_size):
        self.core = [("batch", 1)]
        self.chips = [("batch", 1 << k) for k in range(1, batch_size.bit_length() - 1)]
        self.line = [("seq", 1 << k) for k in range(seq_size.bit_length() - 1)]
        self.bits = self.core + self.chips + self.line

    def cost(self, bit, size):
        axis, mask = bit
        if bit in self.core:
            return {"core": size / 428e3}
        near = 2 * size / 92e3
        if bit in self.line[:1] or axis == "batch":
            return {bit: near}
        return {"line": near, bit: near * (mask // 2)}

    def orders(self):
        if len(self.bits) != 5:
            links = self.chips + self.line
            return [self.core + links[k:] + links[:k] for k in range(len(links))] * 4
        c, x, y, z0, z1 = self.bits
        names = (
            "xyz0z1",
            "yxz0z1",
            "yz0xz1",
            "z0xyz1",
            "z1xz0y",
            "yxz1z0",
            "xyz1z0",
            "yz0z1x",
            "xz0yz1",
            "z0z1xy",
        )
        found = []
        for name in names:
            order = [c]
            while name:
                for key, bit in (("x", x), ("y", y), ("z0", z0), ("z1", z1)):
                    if name.startswith(key):
                        order.append(bit)
                        name = name[len(key) :]
            found.append(order)
        return found

    def halving(self, rows, order, base):
        down, up = [], []
        for bit in order:
            if rows % 32 == 0:
                rows //= 2
                down.append(("sum", bit, rows, rows))
                up.append(("spread", bit, rows, rows))
            else:
                down.append(("sum", bit, 0, rows))
        return {"base": base, "fixed": [], "steps": down + up[::-1], "rows": rows}

    def by_head(self, heads, hd, base):
        head_bits = self.line[: heads.bit_length() - 1]
        batch_bits = self.core + self.chips
        rest = self.line[len(head_bits) :]
        rows, parts = hd, []
        for bit in batch_bits + rest:
            if rows % 32 == 0:
                rows //= 2
                parts.append((bit, rows))
            else:
                parts.append((bit, 0))
        split = [bit for bit, size in parts if size]
        inner = split[1:]
        stride, strides = rows, {}
        for bit in inner[::-1] + head_bits + split[:1]:
            strides[bit] = stride
            stride *= 2
        down = [("sum", bit, strides.get(bit, 0), size or rows) for bit, size in parts]
        up = [("spread", bit, strides[bit], strides[bit]) for bit in strides]
        fixed = [(bit, strides[bit]) for bit in head_bits]
        return {"base": base, "fixed": fixed, "steps": down + up, "rows": rows, "strides": strides}

    def schedule(self, chains, width):
        chains = [(chain, start) for chain, start in chains]
        left = []
        for chain, _ in chains:
            total = [0.0]
            for _, bit, _, rows in chain["steps"][::-1]:
                busy = max(self.cost(bit, 2 * rows * width).values())
                total.append(total[-1] + busy + 2.0)
            left.append(total[::-1])
        free, ready = {}, [start for _, start in chains]
        at = [0] * len(chains)
        plan = []
        while True:
            best = None
            for c, (chain, _) in enumerate(chains):
                if at[c] < len(chain["steps"]):
                    _, bit, _, rows = chain["steps"][at[c]]
                    cost = self.cost(bit, 2 * rows * width)
                    start = max([ready[c]] + [free.get(link, 0.0) for link in cost])
                    key = (round(start, 1), -left[c][at[c]], c)
                    if best is None or key < best[0]:
                        best = (key, c, cost, start)
            if best is None:
                return plan
            _, c, cost, start = best
            for link, busy in cost.items():
                free[link] = start + busy
            step = chains[c][0]["steps"][at[c]]
            lag = 0.7 if step[1] in self.core else 2.0
            lag += 1e-6 * 2 * step[3] * width if step[0] == "sum" else 0.0
            ready[c] = start + max(cost.values()) + lag
            plan.append((start, c, at[c]))
            at[c] += 1


class Sums:
    def __init__(self, chains, work, landing, total, send_sems, recv_sems):
        self.chains = chains
        self.work, self.landing, self.total = work, landing, total
        self.send_sems, self.recv_sems = send_sems, recv_sems
        self.index = {"batch": lax.axis_index("batch"), "seq": lax.axis_index("seq")}
        self.open = {}
        self.offset = {}
        sem = land = 0
        self.sem, self.land = {}, {}
        for c, chain in enumerate(chains):
            self.offset[c] = chain["base"] + sum(
                self.bit(bit) * stride for bit, stride in chain["fixed"]
            )
            for k, (phase, _, _, rows) in enumerate(chain["steps"]):
                self.sem[c, k] = sem
                sem += 1
                if phase == "sum":
                    self.land[c, k] = land
                    land += rows

    @staticmethod
    def needs(chains):
        steps = [step for chain in chains for step in chain["steps"]]
        return len(steps), sum(step[3] for step in steps if step[0] == "sum")

    def bit(self, bit):
        axis, mask = bit
        return lax.rem(lax.div(self.index[axis], mask), 2)

    def partner(self, bit):
        axis, mask = bit
        return {axis: self.index[axis] + mask - 2 * mask * self.bit(bit)}

    def start(self, c, k):
        if k:
            self.finish(c, k - 1)
        phase, bit, stride, rows = self.chains[c]["steps"][k]
        side = self.bit(bit)
        offset = self.offset[c]
        if phase == "sum":
            other = offset + (1 - side) * stride if stride else offset
            source = self.work.at[pl.ds(pl.multiple_of(other, 16), rows)]
            target = self.landing.at[pl.ds(self.land[c, k], rows)]
            if stride:
                self.offset[c] = offset + side * stride
        else:
            here = pl.ds(pl.multiple_of(offset, 16), rows)
            source, target = self.total.at[here], self.total.at[here]
            self.offset[c] = offset - side * stride
        copy = pltpu.make_async_remote_copy(
            src_ref=source,
            dst_ref=target,
            send_sem=self.send_sems.at[self.sem[c, k]],
            recv_sem=self.recv_sems.at[self.sem[c, k]],
            device_id=self.partner(bit),
            device_id_type=MESH,
        )
        copy.start()
        self.open[c] = copy

    def finish(self, c, k):
        self.open.pop(c).wait()
        steps = self.chains[c]["steps"]
        phase, _, _, rows = steps[k]
        if phase == "sum":
            last = k + 1 == len(steps) or steps[k + 1][0] == "spread"
            held = pl.ds(pl.multiple_of(self.offset[c], 16), rows)
            landed = self.landing[self.land[c, k] : self.land[c, k] + rows, :]
            both = self.work[held, :].astype(jnp.float32) + landed.astype(jnp.float32)
            (self.total if last else self.work)[held, :] = low(both)


def sum_kernel(
    z,
    plan,
    chains,
    bits,
    terms_ref,
    small_ref,
    total_ref,
    small_total_ref,
    work,
    landing,
    total,
    small_work,
    small_landing,
    send_sems,
    recv_sems,
    small_send,
    small_recv,
    load_sems,
    store_sems,
):
    sums = Sums(chains, work, landing, total, send_sems, recv_sems)
    loads = []
    for c, chain in enumerate(chains):
        at, size = chain["base"], chain["all"]
        loads.append(
            pltpu.make_async_copy(
                terms_ref.at[at : at + size], work.at[at : at + size], load_sems.at[c]
            )
        )
        loads[-1].start()
    barrier = pltpu.get_barrier_semaphore()
    for bit in bits:
        pl.semaphore_signal(barrier, inc=1, device_id=sums.partner(bit), device_id_type=MESH)
    pl.semaphore_wait(barrier, len(bits))
    small_work[0] = small_ref[...]
    small = []

    def small_start(k):
        copy = pltpu.make_async_remote_copy(
            src_ref=small_work.at[k],
            dst_ref=small_landing.at[k],
            send_sem=small_send.at[k],
            recv_sem=small_recv.at[k],
            device_id=sums.partner(bits[k]),
            device_id_type=MESH,
        )
        copy.start()
        small.append(copy)

    def small_finish(k):
        small[k].wait()
        small_work[k + 1] = small_work[k] + small_landing[k]

    stores = []
    small_start(0)
    small_at = [plan[len(plan) * (k + 1) // (len(bits) + 1)][1:] for k in range(len(bits))]
    for _, c, k in plan:
        if k == 0:
            loads[c].wait()
        sums.start(c, k)
        if (c, k) in small_at:
            done = small_at.index((c, k))
            small_finish(done)
            if done + 1 < len(bits):
                small_start(done + 1)
    small_total_ref[...] = small_work[len(bits)]
    ends = {}
    for order, (_, c, k) in enumerate(plan):
        ends[c] = order
    for c in sorted(ends, key=ends.get):
        sums.finish(c, len(chains[c]["steps"]) - 1)
        at, size = chains[c]["base"], chains[c]["all"]
        stores.append(
            pltpu.make_async_copy(
                total.at[at : at + size], total_ref.at[at : at + size], store_sems.at[c]
            )
        )
        stores[-1].start()
    for store in stores:
        store.wait()


def sum_all(z, nb, terms, head_term, small, early_rows):
    width = z.width
    copies = Copies(nb, z.n)
    orders = copies.orders()
    chains, base = [], 0
    sizes = CHAIN_ROWS if sum(CHAIN_ROWS) == terms.shape[0] else [512] * (terms.shape[0] // 512)
    for c, rows in enumerate(sizes):
        chains.append(copies.halving(rows, orders[CHAIN_ORDER[c % len(CHAIN_ORDER)] % len(orders)], base))
        chains[-1]["all"] = rows
        base += rows
    total_rows = base + z.heads * z.hd
    chains.append(copies.by_head(z.heads, z.hd, base))
    chains[-1]["all"] = z.heads * z.hd
    half = z.hd // 2
    head = lax.rem(lax.axis_index("seq"), z.heads)
    placed = jnp.zeros((2, z.heads, half, width), jnp.bfloat16)
    placed = lax.dynamic_update_slice(
        placed, head_term.reshape(2, 1, half, width), (0, head, 0, 0)
    )
    terms = jnp.concatenate([terms, placed.reshape(z.heads * z.hd, width)], axis=0)
    plan = copies.schedule([(chain, 0.0) for chain in chains], width)
    count, landing = Sums.needs(chains)
    bits = copies.bits
    bf, f4, dma = jnp.bfloat16, jnp.float32, pltpu.SemaphoreType.DMA
    total, small_total = pl.pallas_call(
        functools.partial(sum_kernel, z, plan, chains, bits),
        out_shape=[
            jax.ShapeDtypeStruct((total_rows, width), bf),
            jax.ShapeDtypeStruct(small.shape, f4),
        ],
        in_specs=[ANY, VMEM],
        out_specs=[ANY, VMEM],
        scratch_shapes=[
            pltpu.VMEM((total_rows, width), bf),
            pltpu.VMEM((landing, width), bf),
            pltpu.VMEM((total_rows, width), bf),
            pltpu.VMEM((len(bits) + 1,) + small.shape, f4),
            pltpu.VMEM((len(bits),) + small.shape, f4),
            dma((count,)),
            dma((count,)),
            dma((len(bits),)),
            dma((len(bits),)),
            dma((len(chains),)),
            dma((len(chains),)),
        ],
        compiler_params=pltpu.CompilerParams(
            collective_id=4, has_side_effects=True, vmem_limit_bytes=58 * 2**20
        ),
    )(terms, small)
    heads_total = total[base:].reshape(2, z.heads, half, width).transpose(1, 0, 2, 3)
    return total, heads_total.reshape(z.heads * z.hd, width).T, small_total


def call(kernel, z, collective_id, ins, outs, scratch, args):
    return pl.pallas_call(
        functools.partial(kernel, z),
        out_shape=[jax.ShapeDtypeStruct(shape, dtype) for shape, dtype, _ in outs],
        in_specs=ins,
        out_specs=[space for _, _, space in outs],
        scratch_shapes=scratch,
        compiler_params=pltpu.CompilerParams(
            collective_id=collective_id, has_side_effects=True, vmem_limit_bytes=50 * 2**20
        ),
    )(*args)


def body(
    byte_rows,
    item_lengths,
    out_grad,
    pool_weight,
    norm1_gain,
    norm1_bias,
    query_weight,
    key_weight,
    value_weight,
    position_weight,
    content_bias,
    position_bias,
    output_weight,
    norm2_gain,
    norm2_bias,
    inner_weight,
    outer_weight,
    upsample_weight,
):
    items, full_rows, width = byte_rows.shape
    heads, hd = content_bias.shape
    n = lax.axis_size("seq")
    ff = inner_weight.shape[1]
    z = Sizes(n, items, full_rows, width, heads)
    r, units, length, rows = z.r, z.units, z.length, z.rows
    bf, f4 = jnp.bfloat16, jnp.float32
    slabs = width // LANES
    dma = pltpu.SemaphoreType.DMA
    counts = item_lengths // 3
    table = distance_table(length, width)
    gain1, bias1 = norm1_gain.reshape(1, width), norm1_bias.reshape(1, width)
    gain2, bias2 = norm2_gain.reshape(1, width), norm2_bias.reshape(1, width)
    xf = pltpu.VMEM((items, slabs, 3 * r + 8, LANES), f4)
    (pooled, att_recv, qc, qp, keys, values, positions, probs) = call(
        forward_kernel,
        z,
        0,
        [SMEM] + [VMEM] * 11,
        [
            ((items, r, width), bf, VMEM),
            ((n, r, LANES), bf, ANY),
            ((units, length, hd), bf, VMEM),
            ((units, length, hd), bf, VMEM),
            ((units, length, hd), bf, VMEM),
            ((units, length, hd), bf, VMEM),
            ((length, hd), bf, VMEM),
            ((units, length, length), f4, VMEM),
        ],
        [
            xf,
            pltpu.VMEM((items, 16, width), bf),
            pltpu.VMEM((items, 16, width), bf),
            pltpu.VMEM((n, r, 3 * LANES), bf),
            pltpu.VMEM((n, r, 3 * LANES), bf),
            pltpu.VMEM((n, r, LANES), bf),
            dma((2,)),
            dma((n,)),
            dma((n,)),
            dma((n,)),
            dma((n,)),
            dma,
        ],
        (
            counts,
            byte_rows,
            pool_weight,
            gain1,
            bias1,
            query_weight,
            key_weight,
            value_weight,
            position_weight,
            content_bias,
            position_bias,
            table,
        ),
    )
    early_rows = 3 * width + 2 * ff + width
    block_out, grad_recv, hidden_grad, early, norm2_g = call(
        middle_kernel,
        z,
        1,
        [SMEM] + [VMEM] * 10,
        [
            ((items, full_rows, width), bf, VMEM),
            ((n, r, LANES), bf, ANY),
            ((rows, width), f4, VMEM),
            ((early_rows, width), bf, VMEM),
            ((2, width), f4, VMEM),
        ],
        [
            xf,
            pltpu.VMEM((rows, width), bf),
            pltpu.VMEM((rows, ff), bf),
            pltpu.VMEM((rows, ff), f4),
            pltpu.VMEM((rows, ff), bf),
            pltpu.VMEM((rows, 3 * width), bf),
            pltpu.VMEM((n, r, LANES), bf),
            dma((n,)),
            dma((n,)),
            dma,
        ],
        (
            item_lengths,
            att_recv,
            pooled,
            byte_rows,
            out_grad,
            output_weight,
            gain2,
            bias2,
            inner_weight,
            outer_weight,
            upsample_weight,
        ),
    )
    qkv_recv, head_g, head_bias_g = call(
        backward_kernel,
        z,
        2,
        [VMEM] * 8,
        [
            ((n, r, 3 * LANES), bf, ANY),
            ((hd, width), bf, VMEM),
            ((2, hd), f4, VMEM),
        ],
        [
            pltpu.VMEM((units, length, hd), bf),
            pltpu.VMEM((units, hd, length), f4),
            pltpu.VMEM((units, hd, length), f4),
            pltpu.VMEM((units, hd, length), f4),
            pltpu.VMEM((n, r, 3 * LANES), bf),
            dma((n,)),
            dma((n,)),
            dma,
        ],
        (grad_recv, qc, qp, keys, values, positions, probs, table),
    )
    input_grad, late, norm1_g = call(
        last_kernel,
        z,
        3,
        [VMEM] * 11,
        [
            ((items, full_rows, width), f4, VMEM),
            ((6 * width, width), bf, VMEM),
            ((2, width), f4, VMEM),
        ],
        [
            xf,
            xf,
            pltpu.VMEM((3, rows, width), bf),
            pltpu.VMEM((items, r + 8, width), f4),
            pltpu.VMEM((items, 16, width), bf),
            pltpu.VMEM((items, 16, width), bf),
            dma((2,)),
        ],
        (
            qkv_recv,
            hidden_grad,
            pooled,
            byte_rows,
            out_grad,
            gain1,
            bias1,
            query_weight,
            key_weight,
            value_weight,
            pool_weight,
        ),
    )
    own_head = lax.rem(lax.axis_index("seq"), heads)
    mine = (lax.broadcasted_iota(jnp.int32, (1, heads, 1), 1) == own_head).astype(f4)
    small = jnp.concatenate(
        [norm1_g, norm2_g, (head_bias_g[:, None, :] * mine).reshape(2, width)], axis=0
    )
    small = jnp.concatenate([small, jnp.zeros((2, width), f4)], axis=0)
    total, position_t, small_t = sum_all(
        z,
        lax.axis_size("batch"),
        jnp.concatenate([early, late], axis=0),
        head_g,
        small,
        early_rows,
    )

    def rows_at(first, count):
        return total[first * width : (first + count) * width].astype(f4)

    def side_by_side(first, count):
        stacked = rows_at(first, count).reshape(count, width, width)
        return stacked.transpose(1, 0, 2).reshape(width, count * width)

    wide = ff // width
    up_t = side_by_side(0, 3)
    outer_t = rows_at(3, wide)
    inner_t = side_by_side(3 + wide, wide)
    output_t = rows_at(3 + 2 * wide, 1)
    pool_t = rows_at(4 + 2 * wide, 3)
    query_t, key_t, value_t = (rows_at(7 + 2 * wide + which, 1) for which in range(3))
    bias_t = small_t[4:6].reshape(2, heads, hd)
    return (
        block_out,
        input_grad,
        pool_t,
        small_t[0],
        small_t[1],
        query_t,
        key_t,
        value_t,
        position_t.astype(f4),
        bias_t[0],
        bias_t[1],
        output_t,
        small_t[2],
        small_t[3],
        inner_t,
        outer_t,
        up_t,
    )


def solution(mesh):
    split = P("batch", "seq", None)
    in_specs = (split, P("batch"), split) + (P(),) * 15
    out_specs = (split, split) + (P(),) * 15
    return jax.shard_map(body, mesh=mesh, in_specs=in_specs, out_specs=out_specs, check_vma=False)
```

```python
import functools

import jax
import jax.numpy as jnp
import numpy as np
from jax import lax
from jax.experimental import pallas as pl
from jax.experimental.pallas import tpu as pltpu
from jax.sharding import PartitionSpec as P

MESH = pl.DeviceIdType.MESH
epsilon = 1e-05
masked_value = -1e30
CHAIN_ROWS = [1024, 1536, 512, 512, 512, 1536, 512, 512, 512, 512, 512, 512, 512]
CHAIN_ORDER = [2, 1, 0, 8, 4, 0, 1, 3, 1, 0, 4, 9, 5]
BLOCK = 128
LANES = 128
VMEM = pl.BlockSpec(memory_space=pltpu.VMEM)
SMEM = pl.BlockSpec(memory_space=pltpu.SMEM)
ANY = pl.BlockSpec(memory_space=pl.ANY)


def dot(left, right):
    return jnp.dot(left, right, preferred_element_type=jnp.float32)


def dot_nt(left, right):
    return lax.dot_general(
        left, right, (((1,), (1,)), ((), ())), preferred_element_type=jnp.float32
    )


def dot_tn(left, right):
    return lax.dot_general(
        left, right, (((0,), (0,)), ((), ())), preferred_element_type=jnp.float32
    )


def low(value):
    return value.astype(jnp.bfloat16)


def distance_table(short_len, width):
    distance = (short_len - 1 - np.arange(short_len)).astype(np.float32)
    steps_in = np.arange(0, width, 2).astype(np.float32)
    frequency = np.exp(-np.log(np.float32(10000.0)) * steps_in / np.float32(width))
    angles = distance[:, None] * frequency[None, :].astype(np.float32)
    both = np.concatenate([np.sin(angles), np.cos(angles)], axis=1)
    return jnp.asarray(both.astype(jnp.bfloat16))


def norm_rows(rows):
    mean = jnp.mean(rows, axis=-1, keepdims=True)
    centered = rows - mean
    inverse = lax.rsqrt(jnp.mean(centered * centered, axis=-1, keepdims=True) + epsilon)
    return centered * inverse, inverse


def norm_backward(gradient, normed, inverse, gain):
    scaled = gradient * gain
    return inverse * (
        scaled
        - jnp.mean(scaled, axis=-1, keepdims=True)
        - normed * jnp.mean(scaled * normed, axis=-1, keepdims=True)
    )


class Sizes:
    def __init__(self, n, items, full_rows, width, heads):
        self.n = n
        self.items = items
        self.r = full_rows // 3
        self.width = width
        self.heads = heads
        self.hd = width // heads
        self.units = items * heads // n
        self.length = n * self.r
        self.rows = items * self.r
        assert n % heads == 0 and self.units * self.hd <= LANES


def greet(n, me):
    barrier = pltpu.get_barrier_semaphore()
    for step in range(1, n):
        pl.semaphore_signal(
            barrier, inc=1, device_id={"seq": lax.rem(me + step, n)}, device_id_type=MESH
        )
    pl.semaphore_wait(barrier, n - 1)


def send_all(n, me, source, target, send_sem, recv_sem):
    copies = []
    for step in range(1, n):
        peer = lax.rem(me + step, n)
        copies.append(
            pltpu.make_async_remote_copy(
                src_ref=source(peer),
                dst_ref=target.at[me],
                send_sem=send_sem.at[step],
                recv_sem=recv_sem.at[step],
                device_id={"seq": peer},
                device_id_type=MESH,
            )
        )
        copies[-1].start()
    return copies


def rows_by_three(z, x_ref, xf_ref):
    for item in range(z.items):
        for slab in range(z.width // LANES):
            xf_ref[item, slab, 8:, :] = x_ref[item, :, slab * LANES : (slab + 1) * LANES].astype(
                jnp.float32
            )


def every_third(z, xf_ref, first):
    items = []
    for item in range(z.items):
        slabs = [
            xf_ref[item, slab, pl.ds(first, z.r, stride=3), :] for slab in range(z.width // LANES)
        ]
        items.append(jnp.concatenate(slabs, axis=1))
    return jnp.concatenate(items, axis=0)


def set_every_third(z, xf_ref, first, value):
    for item in range(z.items):
        for slab in range(z.width // LANES):
            xf_ref[item, slab, pl.ds(first, z.r, stride=3), :] = value[
                item * z.r : (item + 1) * z.r, slab * LANES : (slab + 1) * LANES
            ]


def forward_kernel(
    z,
    counts_ref,
    x_ref,
    pool_w,
    gain_ref,
    bias_ref,
    query_w,
    key_w,
    value_w,
    position_w,
    cb_ref,
    pb_ref,
    table_ref,
    pooled_ref,
    recv_ref,
    qc_ref,
    qp_ref,
    k_ref,
    v_ref,
    pos_ref,
    probs_ref,
    xf_ref,
    tail_ref,
    halo_ref,
    qkv_out_ref,
    qkv_ref,
    out_ref,
    halo_sems,
    qkv_send,
    qkv_recv,
    out_send,
    out_recv,
    own_sem,
):
    n, r, width, hd = z.n, z.r, z.width, z.hd
    me = lax.axis_index("seq")
    head = lax.rem(me, z.heads)
    group = lax.div(me, z.heads)
    greet(n, me)
    tail_ref[...] = x_ref[:, 3 * r - 16 :, :]
    halo = pltpu.make_async_remote_copy(
        src_ref=tail_ref,
        dst_ref=halo_ref,
        send_sem=halo_sems.at[0],
        recv_sem=halo_sems.at[1],
        device_id={"seq": lax.rem(me + 1, n)},
        device_id_type=MESH,
    )
    halo.start()
    rows_by_three(z, x_ref, xf_ref)
    halo.wait()
    for item in range(z.items):
        before = jnp.where(me > 0, halo_ref[item].astype(jnp.float32), 0.0)
        for slab in range(width // LANES):
            xf_ref[item, slab, 0:8, :] = before[8:16, slab * LANES : (slab + 1) * LANES]
    pooled = jnp.zeros((z.rows, width), jnp.float32)
    for part in range(3):
        pooled += dot(
            low(every_third(z, xf_ref, 6 + part)), pool_w[part * width : (part + 1) * width, :]
        )
    short = low(pooled)
    pooled_ref[...] = short.reshape(z.items, r, width)
    normed, _ = norm_rows(short.astype(jnp.float32))
    attn_in = low(normed * gain_ref[...] + bias_ref[...])
    qkv = [low(dot(attn_in, w[...])) for w in (query_w, key_w, value_w)]
    pad = [jnp.zeros((r, hd), jnp.bfloat16)] * (LANES // hd - z.units)
    for target in range(n):
        sides = []
        lanes = slice(target % z.heads * hd, (target % z.heads + 1) * hd)
        for value in qkv:
            for unit in range(z.units):
                item = target // z.heads * z.units + unit
                sides.append(value[item * r : (item + 1) * r, lanes])
            sides += pad
        qkv_out_ref[target] = jnp.concatenate(sides, axis=1)
    copies = send_all(n, me, lambda peer: qkv_out_ref.at[peer], qkv_ref, qkv_send, qkv_recv)
    qkv_ref[me] = qkv_out_ref[me]
    lane_pair = pl.multiple_of(lax.div(head * hd, LANES) * LANES, LANES)
    turn = lax.rem(head * hd, LANES)
    both = dot(table_ref[...], position_w[:, pl.ds(lane_pair, LANES)])
    pos_ref[...] = low(pltpu.roll(both, LANES - turn, 1)[:, :hd])
    content_bias = cb_ref[pl.ds(head, 1), :]
    position_bias = pb_ref[pl.ds(head, 1), :]
    for copy in copies:
        copy.wait()
    for unit in range(z.units):
        queries, keys, values = (
            qkv_ref[:, :, which * LANES + unit * hd : which * LANES + (unit + 1) * hd].reshape(
                z.length, hd
            )
            for which in range(3)
        )
        qc_ref[unit] = low(queries.astype(jnp.float32) + content_bias)
        qp_ref[unit] = low(queries.astype(jnp.float32) + position_bias)
        k_ref[unit] = keys
        v_ref[unit] = values
    for block in range(z.length // BLOCK):
        lo, hi = block * BLOCK, (block + 1) * BLOCK
        sides = []
        for unit in range(z.units):
            count = counts_ref[group * z.units + unit]
            content = dot_nt(qc_ref[unit, lo:hi, :], k_ref[unit, :hi, :])
            by_distance = dot_nt(qp_ref[unit, lo:hi, :], pos_ref[z.length - hi :, :])
            placed = pltpu.roll(by_distance, lo + 1, 1, stride=1, stride_axis=0)
            query_at = lo + lax.broadcasted_iota(jnp.int32, (BLOCK, hi), 0)
            key_at = lax.broadcasted_iota(jnp.int32, (BLOCK, hi), 1)
            valid = (key_at <= query_at) & (key_at < count)
            logits = jnp.where(valid, (content + placed) * hd**-0.5, masked_value)
            raised = jnp.exp(logits - jnp.max(logits, axis=-1, keepdims=True))
            probs = raised / jnp.sum(raised, axis=-1, keepdims=True)
            probs_ref[unit, lo:hi, :hi] = probs
            sides.append(low(dot(low(probs), v_ref[unit, :hi, :])))
        sides += [jnp.zeros((BLOCK, hd), jnp.bfloat16)] * (LANES // hd - z.units)
        per = BLOCK // r
        out_ref[block * per : (block + 1) * per] = jnp.concatenate(sides, axis=1).reshape(
            per, r, LANES
        )
    copies = send_all(n, me, lambda peer: out_ref.at[peer], recv_ref, out_send, out_recv)
    own = pltpu.make_async_copy(out_ref.at[me], recv_ref.at[me], own_sem)
    own.start()
    for copy in copies:
        copy.wait()
    own.wait()


def live_rows(z, me, length, part):
    at = lax.broadcasted_iota(jnp.int32, (z.r, 1), 0) * 3 + part + me * 3 * z.r
    return (at < length).astype(jnp.float32)


def middle_kernel(
    z,
    lengths_ref,
    att_recv_ref,
    pooled_ref,
    x_ref,
    og_ref,
    output_w,
    gain_ref,
    bias_ref,
    inner_w,
    outer_w,
    up_w,
    block_ref,
    recv_ref,
    hidden_grad_ref,
    early_ref,
    norm_grad_ref,
    xf_ref,
    att_ref,
    act_ref,
    slope_ref,
    inner_low_ref,
    up_rows_ref,
    out_ref,
    out_send,
    out_recv,
    own_sem,
):
    n, r, width, hd = z.n, z.r, z.width, z.hd
    me = lax.axis_index("seq")
    greet(n, me)
    ff = inner_w.shape[1]
    step = min(512, ff)

    def live(part):
        return jnp.concatenate(
            [live_rows(z, me, lengths_ref[item], part) for item in range(z.items)], axis=0
        )

    rows_by_three(z, og_ref, xf_ref)
    for part in range(3):
        up_rows_ref[:, part * width : (part + 1) * width] = low(
            every_third(z, xf_ref, 8 + part) * live(part)
        )
    summed_grad = low(dot_nt(up_rows_ref[...], up_w[...]))
    for source in range(n):
        for unit in range(z.units):
            item = source // z.heads * z.units + unit
            head = source % z.heads
            att_ref[item * r : (item + 1) * r, head * hd : (head + 1) * hd] = att_recv_ref[
                source, :, unit * hd : (unit + 1) * hd
            ]
    short = pooled_ref[...].reshape(z.rows, width).astype(jnp.float32)
    hidden = short + dot(att_ref[...], output_w[...])
    normed, inverse = norm_rows(hidden)
    ffn_in = low(normed * gain_ref[...] + bias_ref[...])
    for lo in range(0, ff, step):
        inner = dot(ffn_in, inner_w[:, lo : lo + step])
        normal_cdf = 0.5 * (1.0 + lax.erf(inner * 0.7071067811865476))
        density = jnp.exp(-0.5 * inner * inner) * 0.3989422804014327
        act_ref[:, lo : lo + step] = low(inner * normal_cdf)
        slope_ref[:, lo : lo + step] = normal_cdf + inner * density
    for lo in range(0, ff, step):
        inner_low_ref[:, lo : lo + step] = low(
            dot_nt(summed_grad, outer_w[lo : lo + step, :]) * slope_ref[:, lo : lo + step]
        )
    ffn_grad = dot_nt(inner_low_ref[...], inner_w[...])
    norm_grad_ref[0:1, :] = jnp.sum(ffn_grad * normed, axis=0, keepdims=True)
    norm_grad_ref[1:2, :] = jnp.sum(ffn_grad, axis=0, keepdims=True)
    hidden_grad = summed_grad.astype(jnp.float32) + norm_backward(
        ffn_grad, normed, inverse, gain_ref[...]
    )
    hidden_grad_ref[...] = hidden_grad
    branch = low(hidden_grad)
    att_grad = low(dot_nt(branch, output_w[...]))
    for target in range(n):
        head = target % z.heads
        sides = []
        for unit in range(z.units):
            item = target // z.heads * z.units + unit
            sides.append(att_grad[item * r : (item + 1) * r, head * hd : (head + 1) * hd])
        sides += [jnp.zeros((r, hd), jnp.bfloat16)] * (LANES // hd - z.units)
        out_ref[target] = jnp.concatenate(sides, axis=1)
    copies = send_all(n, me, lambda peer: out_ref.at[peer], recv_ref, out_send, out_recv)
    own = pltpu.make_async_copy(out_ref.at[me], recv_ref.at[me], own_sem)
    own.start()
    summed = low(hidden + dot(act_ref[...], outer_w[...]))
    rows_by_three(z, x_ref, xf_ref)
    for part in range(3):
        up = dot(summed, up_w[:, part * width : (part + 1) * width])
        set_every_third(
            z, xf_ref, 8 + part, every_third(z, xf_ref, 8 + part) + up * live(part)
        )
    for item in range(z.items):
        for slab in range(width // LANES):
            block_ref[item, :, slab * LANES : (slab + 1) * LANES] = low(xf_ref[item, slab, 8:, :])
    for part in range(3):
        cut = slice(part * width, (part + 1) * width)
        early_ref[cut, :] = low(dot_tn(summed, up_rows_ref[:, cut]))
    for lo in range(0, ff, width):
        cut = slice(lo, lo + width)
        at = 3 * width + lo
        early_ref[at : at + width, :] = low(dot_tn(act_ref[:, cut], summed_grad))
        at += ff
        early_ref[at : at + width, :] = low(dot_tn(ffn_in, inner_low_ref[:, cut]))
    early_ref[3 * width + 2 * ff :, :] = low(dot_tn(att_ref[...], branch))
    for copy in copies:
        copy.wait()
    own.wait()


def reversal():
    at = lax.broadcasted_iota(jnp.int32, (BLOCK, BLOCK), 0)
    across = lax.broadcasted_iota(jnp.int32, (BLOCK, BLOCK), 1)
    return low((at + across == BLOCK - 1).astype(jnp.float32))


def backward_kernel(
    z,
    grad_recv_ref,
    qc_ref,
    qp_ref,
    k_ref,
    v_ref,
    pos_ref,
    probs_ref,
    table_ref,
    recv_ref,
    head_grad_ref,
    bias_grad_ref,
    query_grad_ref,
    key_t_ref,
    value_t_ref,
    table_t_ref,
    out_ref,
    out_send,
    out_recv,
    own_sem,
):
    n, r, hd = z.n, z.r, z.hd
    length = z.length
    me = lax.axis_index("seq")
    greet(n, me)
    flip = reversal()
    content_sum = jnp.zeros((1, hd), jnp.float32)
    position_sum = jnp.zeros((1, hd), jnp.float32)
    key_t_ref[...] = jnp.zeros_like(key_t_ref)
    value_t_ref[...] = jnp.zeros_like(value_t_ref)
    table_t_ref[...] = jnp.zeros_like(table_t_ref)
    for unit in range(z.units):
        att_grad = grad_recv_ref[:, :, unit * hd : (unit + 1) * hd].reshape(length, hd)
        for block in range(length // BLOCK):
            lo, hi = block * BLOCK, (block + 1) * BLOCK
            block_grad = att_grad[lo:hi]
            probs = probs_ref[unit, lo:hi, :hi]
            prob_grad = dot_nt(block_grad, v_ref[unit, :hi, :])
            delta = jnp.sum(probs * prob_grad, axis=-1, keepdims=True)
            raw = low(probs * (prob_grad - delta) * hd**-0.5)
            content = dot(raw, k_ref[unit, :hi, :])
            key_t_ref[unit, :, :hi] += dot_tn(qc_ref[unit, lo:hi, :], raw)
            value_t_ref[unit, :, :hi] += dot_tn(block_grad, low(probs))
            by_distance = low(pltpu.roll(dot(flip, raw), 0, 1, stride=1, stride_axis=0))
            position = dot(by_distance, pos_ref[length - hi :, :])
            upper = low(position)
            lower = low(position - upper.astype(jnp.float32))
            position = dot(flip, upper) + dot(flip, lower)
            flipped_q = low(dot(flip, qp_ref[unit, lo:hi, :]))
            table_t_ref[unit, :, length - hi :] += dot_tn(flipped_q, by_distance)
            content_sum += jnp.sum(content, axis=0, keepdims=True)
            position_sum += jnp.sum(position, axis=0, keepdims=True)
            query_grad_ref[unit, lo:hi, :] = low(content + position)
    bias_grad_ref[0:1, :] = content_sum
    bias_grad_ref[1:2, :] = position_sum
    pad = [jnp.zeros((length, hd), jnp.bfloat16)] * (LANES // hd - z.units)
    sides = [query_grad_ref[unit] for unit in range(z.units)] + pad
    sides += [low(key_t_ref[unit].T) for unit in range(z.units)] + pad
    sides += [low(value_t_ref[unit].T) for unit in range(z.units)] + pad
    out_ref[...] = jnp.concatenate(sides, axis=1).reshape(n, r, 3 * LANES)
    copies = send_all(n, me, lambda peer: out_ref.at[peer], recv_ref, out_send, out_recv)
    own = pltpu.make_async_copy(out_ref.at[me], recv_ref.at[me], own_sem)
    own.start()
    table_sum = 0.0
    for unit in range(z.units):
        table_sum += dot(low(table_t_ref[unit]), table_ref[...])
    head_grad_ref[...] = low(table_sum)
    for copy in copies:
        copy.wait()
    own.wait()


def last_kernel(
    z,
    recv_ref,
    hidden_grad_ref,
    pooled_ref,
    x_ref,
    og_ref,
    gain_ref,
    bias_ref,
    query_w,
    key_w,
    value_w,
    pool_w,
    input_grad_ref,
    late_ref,
    norm_grad_ref,
    xf_ref,
    of_ref,
    dq_ref,
    grad_ref,
    head_ref,
    halo_ref,
    halo_sems,
):
    n, r, width, hd = z.n, z.r, z.width, z.hd
    me = lax.axis_index("seq")
    greet(n, me)
    for source in range(n):
        for unit in range(z.units):
            item = source // z.heads * z.units + unit
            head = source % z.heads
            for which in range(3):
                dq_ref[which, item * r : (item + 1) * r, head * hd : (head + 1) * hd] = recv_ref[
                    source, :, which * LANES + unit * hd : which * LANES + (unit + 1) * hd
                ]
    attn_grad = (
        dot_nt(dq_ref[0], query_w[...])
        + dot_nt(dq_ref[1], key_w[...])
        + dot_nt(dq_ref[2], value_w[...])
    )
    normed, inverse = norm_rows(pooled_ref[...].reshape(z.rows, width).astype(jnp.float32))
    norm_grad_ref[0:1, :] = jnp.sum(attn_grad * normed, axis=0, keepdims=True)
    norm_grad_ref[1:2, :] = jnp.sum(attn_grad, axis=0, keepdims=True)
    short_grad = low(
        hidden_grad_ref[...] + norm_backward(attn_grad, normed, inverse, gain_ref[...])
    )
    for item in range(z.items):
        head_ref[item] = short_grad[item * r : item * r + 16, :]
        grad_ref[item, 0:r, :] = short_grad[item * r : (item + 1) * r, :].astype(jnp.float32)
    halo = pltpu.make_async_remote_copy(
        src_ref=head_ref,
        dst_ref=halo_ref,
        send_sem=halo_sems.at[0],
        recv_sem=halo_sems.at[1],
        device_id={"seq": lax.rem(me + n - 1, n)},
        device_id_type=MESH,
    )
    halo.start()
    attn_in = low(normed * gain_ref[...] + bias_ref[...])
    for which in range(3):
        at = (3 + which) * width
        late_ref[at : at + width, :] = low(dot_tn(attn_in, dq_ref[which]))
    rows_by_three(z, x_ref, xf_ref)
    rows_by_three(z, og_ref, of_ref)
    late_ref[2 * width : 3 * width, :] = low(dot_tn(low(every_third(z, xf_ref, 8)), short_grad))
    own = dot_nt(short_grad, pool_w[2 * width :, :])
    set_every_third(z, of_ref, 8, every_third(z, of_ref, 8) + own)
    halo.wait()
    for item in range(z.items):
        after = jnp.where(me < n - 1, halo_ref[item].astype(jnp.float32), 0.0)
        grad_ref[item, r : r + 8, :] = after[0:8, :]
    later = low(
        jnp.concatenate([grad_ref[item, 1 : r + 1, :] for item in range(z.items)], axis=0)
    )
    for part in range(2):
        cut = slice(part * width, (part + 1) * width)
        first = 9 + part
        late_ref[cut, :] = low(dot_tn(low(every_third(z, xf_ref, first)), later))
        back = dot_nt(later, pool_w[cut, :])
        set_every_third(z, of_ref, first, every_third(z, of_ref, first) + back)
    for item in range(z.items):
        for slab in range(width // LANES):
            input_grad_ref[item, :, slab * LANES : (slab + 1) * LANES] = of_ref[item, slab, 8:, :]


class Copies:
    def __init__(self, batch_size, seq_size):
        self.core = [("batch", 1)]
        self.chips = [("batch", 1 << k) for k in range(1, batch_size.bit_length() - 1)]
        self.line = [("seq", 1 << k) for k in range(seq_size.bit_length() - 1)]
        self.bits = self.core + self.chips + self.line

    def cost(self, bit, size):
        axis, mask = bit
        if bit in self.core:
            return {"core": size / 428e3}
        near = 2 * size / 92e3
        if bit in self.line[:1] or axis == "batch":
            return {bit: near}
        return {"line": near, bit: near * (mask // 2)}

    def orders(self):
        if len(self.bits) != 5:
            links = self.chips + self.line
            return [self.core + links[k:] + links[:k] for k in range(len(links))] * 4
        c, x, y, z0, z1 = self.bits
        names = (
            "xyz0z1",
            "yxz0z1",
            "yz0xz1",
            "z0xyz1",
            "z1xz0y",
            "yxz1z0",
            "xyz1z0",
            "yz0z1x",
            "xz0yz1",
            "z0z1xy",
        )
        found = []
        for name in names:
            order = [c]
            while name:
                for key, bit in (("x", x), ("y", y), ("z0", z0), ("z1", z1)):
                    if name.startswith(key):
                        order.append(bit)
                        name = name[len(key) :]
            found.append(order)
        return found

    def halving(self, rows, order, base):
        down, up = [], []
        for bit in order:
            if rows % 32 == 0:
                rows //= 2
                down.append(("sum", bit, rows, rows))
                up.append(("spread", bit, rows, rows))
            else:
                down.append(("sum", bit, 0, rows))
        return {"base": base, "fixed": [], "steps": down + up[::-1], "rows": rows}

    def by_head(self, heads, hd, base):
        head_bits = self.line[: heads.bit_length() - 1]
        batch_bits = self.core + self.chips
        rest = self.line[len(head_bits) :]
        rows, parts = hd, []
        for bit in batch_bits + rest:
            if rows % 32 == 0:
                rows //= 2
                parts.append((bit, rows))
            else:
                parts.append((bit, 0))
        split = [bit for bit, size in parts if size]
        inner = split[1:]
        stride, strides = rows, {}
        for bit in inner[::-1] + head_bits + split[:1]:
            strides[bit] = stride
            stride *= 2
        down = [("sum", bit, strides.get(bit, 0), size or rows) for bit, size in parts]
        up = [("spread", bit, strides[bit], strides[bit]) for bit in strides]
        fixed = [(bit, strides[bit]) for bit in head_bits]
        return {"base": base, "fixed": fixed, "steps": down + up, "rows": rows, "strides": strides}

    def schedule(self, chains, width):
        chains = [(chain, start) for chain, start in chains]
        left = []
        for chain, _ in chains:
            total = [0.0]
            for _, bit, _, rows in chain["steps"][::-1]:
                busy = max(self.cost(bit, 2 * rows * width).values())
                total.append(total[-1] + busy + 2.0)
            left.append(total[::-1])
        free, ready = {}, [start for _, start in chains]
        at = [0] * len(chains)
        plan = []
        while True:
            best = None
            for c, (chain, _) in enumerate(chains):
                if at[c] < len(chain["steps"]):
                    _, bit, _, rows = chain["steps"][at[c]]
                    cost = self.cost(bit, 2 * rows * width)
                    start = max([ready[c]] + [free.get(link, 0.0) for link in cost])
                    key = (round(start, 1), -left[c][at[c]], c)
                    if best is None or key < best[0]:
                        best = (key, c, cost, start)
            if best is None:
                return plan
            _, c, cost, start = best
            for link, busy in cost.items():
                free[link] = start + busy
            step = chains[c][0]["steps"][at[c]]
            lag = 0.7 if step[1] in self.core else 2.0
            lag += 1e-6 * 2 * step[3] * width if step[0] == "sum" else 0.0
            ready[c] = start + max(cost.values()) + lag
            plan.append((start, c, at[c]))
            at[c] += 1


class Sums:
    def __init__(self, chains, work, landing, total, send_sems, recv_sems):
        self.chains = chains
        self.work, self.landing, self.total = work, landing, total
        self.send_sems, self.recv_sems = send_sems, recv_sems
        self.index = {"batch": lax.axis_index("batch"), "seq": lax.axis_index("seq")}
        self.open = {}
        self.offset = {}
        sem = land = 0
        self.sem, self.land = {}, {}
        for c, chain in enumerate(chains):
            self.offset[c] = chain["base"] + sum(
                self.bit(bit) * stride for bit, stride in chain["fixed"]
            )
            for k, (phase, _, _, rows) in enumerate(chain["steps"]):
                self.sem[c, k] = sem
                sem += 1
                if phase == "sum":
                    self.land[c, k] = land
                    land += rows

    @staticmethod
    def needs(chains):
        steps = [step for chain in chains for step in chain["steps"]]
        return len(steps), sum(step[3] for step in steps if step[0] == "sum")

    def bit(self, bit):
        axis, mask = bit
        return lax.rem(lax.div(self.index[axis], mask), 2)

    def partner(self, bit):
        axis, mask = bit
        return {axis: self.index[axis] + mask - 2 * mask * self.bit(bit)}

    def start(self, c, k):
        if k:
            self.finish(c, k - 1)
        phase, bit, stride, rows = self.chains[c]["steps"][k]
        side = self.bit(bit)
        offset = self.offset[c]
        if phase == "sum":
            other = offset + (1 - side) * stride if stride else offset
            source = self.work.at[pl.ds(pl.multiple_of(other, 16), rows)]
            target = self.landing.at[pl.ds(self.land[c, k], rows)]
            if stride:
                self.offset[c] = offset + side * stride
        else:
            here = pl.ds(pl.multiple_of(offset, 16), rows)
            source, target = self.total.at[here], self.total.at[here]
            self.offset[c] = offset - side * stride
        copy = pltpu.make_async_remote_copy(
            src_ref=source,
            dst_ref=target,
            send_sem=self.send_sems.at[self.sem[c, k]],
            recv_sem=self.recv_sems.at[self.sem[c, k]],
            device_id=self.partner(bit),
            device_id_type=MESH,
        )
        copy.start()
        self.open[c] = copy

    def finish(self, c, k):
        self.open.pop(c).wait()
        steps = self.chains[c]["steps"]
        phase, _, _, rows = steps[k]
        if phase == "sum":
            last = k + 1 == len(steps) or steps[k + 1][0] == "spread"
            held = pl.ds(pl.multiple_of(self.offset[c], 16), rows)
            landed = self.landing[self.land[c, k] : self.land[c, k] + rows, :]
            both = self.work[held, :].astype(jnp.float32) + landed.astype(jnp.float32)
            (self.total if last else self.work)[held, :] = low(both)


def sum_kernel(
    z,
    plan,
    chains,
    bits,
    early_ref,
    late_ref,
    head_ref,
    small_ref,
    total_ref,
    small_total_ref,
    work,
    landing,
    total,
    small_work,
    small_landing,
    send_sems,
    recv_sems,
    small_send,
    small_recv,
    load_sems,
    store_sems,
):
    sums = Sums(chains, work, landing, total, send_sems, recv_sems)
    loads = []
    for c, chain in enumerate(chains):
        at, size = chain["base"], chain["all"]
        early_rows = early_ref.shape[0]
        if "strides" in chain:
            half = z.hd // 2
            head = lax.rem(lax.axis_index("seq"), z.heads)
            parts = []
            for side in range(2):
                to = pl.multiple_of(at + side * z.heads * half + head * half, 16)
                parts.append((head_ref.at[side * half : (side + 1) * half], to, half))
        elif at < early_rows:
            parts = [(early_ref.at[at : at + size], at, size)]
        else:
            parts = [(late_ref.at[at - early_rows : at - early_rows + size], at, size)]
        loads.append(
            [
                pltpu.make_async_copy(
                    source, work.at[pl.ds(to, count)], load_sems.at[c, which]
                )
                for which, (source, to, count) in enumerate(parts)
            ]
        )
        for load in loads[-1]:
            load.start()
    barrier = pltpu.get_barrier_semaphore()
    for bit in bits:
        pl.semaphore_signal(barrier, inc=1, device_id=sums.partner(bit), device_id_type=MESH)
    pl.semaphore_wait(barrier, len(bits))
    small_work[0] = small_ref[...]
    small = []

    def small_start(k):
        copy = pltpu.make_async_remote_copy(
            src_ref=small_work.at[k],
            dst_ref=small_landing.at[k],
            send_sem=small_send.at[k],
            recv_sem=small_recv.at[k],
            device_id=sums.partner(bits[k]),
            device_id_type=MESH,
        )
        copy.start()
        small.append(copy)

    def small_finish(k):
        small[k].wait()
        small_work[k + 1] = small_work[k] + small_landing[k]

    stores = []
    small_start(0)
    small_at = [plan[len(plan) * (k + 1) // (len(bits) + 1)][1:] for k in range(len(bits))]
    for _, c, k in plan:
        if k == 0:
            for load in loads[c]:
                load.wait()
        sums.start(c, k)
        if (c, k) in small_at:
            done = small_at.index((c, k))
            small_finish(done)
            if done + 1 < len(bits):
                small_start(done + 1)
    small_total_ref[...] = small_work[len(bits)]
    ends = {}
    for order, (_, c, k) in enumerate(plan):
        ends[c] = order
    for c in sorted(ends, key=ends.get):
        sums.finish(c, len(chains[c]["steps"]) - 1)
        at, size = chains[c]["base"], chains[c]["all"]
        stores.append(
            pltpu.make_async_copy(
                total.at[at : at + size], total_ref.at[at : at + size], store_sems.at[c]
            )
        )
        stores[-1].start()
    for store in stores:
        store.wait()


def sum_all(z, nb, early, late, head_term, small):
    width = z.width
    copies = Copies(nb, z.n)
    orders = copies.orders()
    chains, base = [], 0
    term_rows = early.shape[0] + late.shape[0]
    sizes = CHAIN_ROWS if sum(CHAIN_ROWS) == term_rows else [512] * (term_rows // 512)
    for c, rows in enumerate(sizes):
        chains.append(copies.halving(rows, orders[CHAIN_ORDER[c % len(CHAIN_ORDER)] % len(orders)], base))
        chains[-1]["all"] = rows
        base += rows
    total_rows = base + z.heads * z.hd
    chains.append(copies.by_head(z.heads, z.hd, base))
    chains[-1]["all"] = z.heads * z.hd
    plan = copies.schedule([(chain, 0.0) for chain in chains], width)
    count, landing = Sums.needs(chains)
    bits = copies.bits
    bf, f4, dma = jnp.bfloat16, jnp.float32, pltpu.SemaphoreType.DMA
    total, small_total = pl.pallas_call(
        functools.partial(sum_kernel, z, plan, chains, bits),
        out_shape=[
            jax.ShapeDtypeStruct((total_rows, width), bf),
            jax.ShapeDtypeStruct(small.shape, f4),
        ],
        in_specs=[ANY, ANY, ANY, VMEM],
        out_specs=[ANY, VMEM],
        scratch_shapes=[
            pltpu.VMEM((total_rows, width), bf),
            pltpu.VMEM((landing, width), bf),
            pltpu.VMEM((total_rows, width), bf),
            pltpu.VMEM((len(bits) + 1,) + small.shape, f4),
            pltpu.VMEM((len(bits),) + small.shape, f4),
            dma((count,)),
            dma((count,)),
            dma((len(bits),)),
            dma((len(bits),)),
            dma((len(chains), 2)),
            dma((len(chains),)),
        ],
        compiler_params=pltpu.CompilerParams(
            collective_id=4, has_side_effects=True, vmem_limit_bytes=58 * 2**20
        ),
    )(early, late, head_term, small)
    return total, small_total


def result_kernel(
    z,
    ff,
    total_ref,
    small_ref,
    block_in_ref,
    input_in_ref,
    block_ref,
    input_ref,
    pool_ref,
    gain1_ref,
    bias1_ref,
    query_ref,
    key_ref,
    value_ref,
    position_ref,
    content_bias_ref,
    position_bias_ref,
    output_ref,
    gain2_ref,
    bias2_ref,
    inner_ref,
    outer_ref,
    up_ref,
    held,
    wide,
    load_sems,
    store_sems,
    pass_sems,
):
    width = z.width
    through = [
        pltpu.make_async_copy(block_in_ref, block_ref, pass_sems.at[0]),
        pltpu.make_async_copy(input_in_ref, input_ref, pass_sems.at[1]),
    ]
    blocks = held.shape[0]
    loads = [
        pltpu.make_async_copy(
            total_ref.at[k * width : (k + 1) * width], held.at[k], load_sems.at[k]
        )
        for k in range(blocks)
    ]
    for copy in loads + through:
        copy.start()
    places = [up_ref.at[:, k * width : (k + 1) * width] for k in range(3)]
    places += [outer_ref.at[k * width : (k + 1) * width] for k in range(ff // width)]
    places += [inner_ref.at[:, k * width : (k + 1) * width] for k in range(ff // width)]
    places += [output_ref]
    places += [pool_ref.at[k * width : (k + 1) * width] for k in range(3)]
    places += [query_ref, key_ref, value_ref, position_ref]
    gain1_ref[...] = small_ref[0:1, :]
    bias1_ref[...] = small_ref[1:2, :]
    gain2_ref[...] = small_ref[2:3, :]
    bias2_ref[...] = small_ref[3:4, :]
    for head in range(z.heads):
        lanes = slice(head * z.hd, (head + 1) * z.hd)
        content_bias_ref[head : head + 1, :] = small_ref[4:5, lanes]
        position_bias_ref[head : head + 1, :] = small_ref[5:6, lanes]
    stores = []
    for k in range(blocks):
        loads[k].wait()
        if k + 1 < blocks:
            wide[k] = held[k].astype(jnp.float32)
        else:
            half = z.hd // 2
            for head in range(z.heads):
                rows = [
                    held[k, side * z.heads * half + head * half :][:half] for side in range(2)
                ]
                both = jnp.concatenate(rows, axis=0).astype(jnp.float32)
                wide[k, :, head * z.hd : (head + 1) * z.hd] = both.T
        stores.append(pltpu.make_async_copy(wide.at[k], places[k], store_sems.at[k]))
        stores[-1].start()
    for copy in stores + through:
        copy.wait()


def call(kernel, z, collective_id, ins, outs, scratch, args):
    return pl.pallas_call(
        functools.partial(kernel, z),
        out_shape=[jax.ShapeDtypeStruct(shape, dtype) for shape, dtype, _ in outs],
        in_specs=ins,
        out_specs=[space for _, _, space in outs],
        scratch_shapes=scratch,
        compiler_params=pltpu.CompilerParams(
            collective_id=collective_id, has_side_effects=True, vmem_limit_bytes=50 * 2**20
        ),
    )(*args)


def body(
    byte_rows,
    item_lengths,
    out_grad,
    pool_weight,
    norm1_gain,
    norm1_bias,
    query_weight,
    key_weight,
    value_weight,
    position_weight,
    content_bias,
    position_bias,
    output_weight,
    norm2_gain,
    norm2_bias,
    inner_weight,
    outer_weight,
    upsample_weight,
):
    items, full_rows, width = byte_rows.shape
    heads, hd = content_bias.shape
    n = lax.axis_size("seq")
    ff = inner_weight.shape[1]
    z = Sizes(n, items, full_rows, width, heads)
    r, units, length, rows = z.r, z.units, z.length, z.rows
    bf, f4 = jnp.bfloat16, jnp.float32
    slabs = width // LANES
    dma = pltpu.SemaphoreType.DMA
    counts = item_lengths // 3
    table = distance_table(length, width)
    gain1, bias1 = norm1_gain.reshape(1, width), norm1_bias.reshape(1, width)
    gain2, bias2 = norm2_gain.reshape(1, width), norm2_bias.reshape(1, width)
    xf = pltpu.VMEM((items, slabs, 3 * r + 8, LANES), f4)
    (pooled, att_recv, qc, qp, keys, values, positions, probs) = call(
        forward_kernel,
        z,
        0,
        [SMEM] + [VMEM] * 11,
        [
            ((items, r, width), bf, VMEM),
            ((n, r, LANES), bf, ANY),
            ((units, length, hd), bf, VMEM),
            ((units, length, hd), bf, VMEM),
            ((units, length, hd), bf, VMEM),
            ((units, length, hd), bf, VMEM),
            ((length, hd), bf, VMEM),
            ((units, length, length), f4, VMEM),
        ],
        [
            xf,
            pltpu.VMEM((items, 16, width), bf),
            pltpu.VMEM((items, 16, width), bf),
            pltpu.VMEM((n, r, 3 * LANES), bf),
            pltpu.VMEM((n, r, 3 * LANES), bf),
            pltpu.VMEM((n, r, LANES), bf),
            dma((2,)),
            dma((n,)),
            dma((n,)),
            dma((n,)),
            dma((n,)),
            dma,
        ],
        (
            counts,
            byte_rows,
            pool_weight,
            gain1,
            bias1,
            query_weight,
            key_weight,
            value_weight,
            position_weight,
            content_bias,
            position_bias,
            table,
        ),
    )
    early_rows = 3 * width + 2 * ff + width
    block_out, grad_recv, hidden_grad, early, norm2_g = call(
        middle_kernel,
        z,
        1,
        [SMEM] + [VMEM] * 10,
        [
            ((items, full_rows, width), bf, VMEM),
            ((n, r, LANES), bf, ANY),
            ((rows, width), f4, VMEM),
            ((early_rows, width), bf, VMEM),
            ((2, width), f4, VMEM),
        ],
        [
            xf,
            pltpu.VMEM((rows, width), bf),
            pltpu.VMEM((rows, ff), bf),
            pltpu.VMEM((rows, ff), f4),
            pltpu.VMEM((rows, ff), bf),
            pltpu.VMEM((rows, 3 * width), bf),
            pltpu.VMEM((n, r, LANES), bf),
            dma((n,)),
            dma((n,)),
            dma,
        ],
        (
            item_lengths,
            att_recv,
            pooled,
            byte_rows,
            out_grad,
            output_weight,
            gain2,
            bias2,
            inner_weight,
            outer_weight,
            upsample_weight,
        ),
    )
    qkv_recv, head_g, head_bias_g = call(
        backward_kernel,
        z,
        2,
        [VMEM] * 8,
        [
            ((n, r, 3 * LANES), bf, ANY),
            ((hd, width), bf, VMEM),
            ((2, hd), f4, VMEM),
        ],
        [
            pltpu.VMEM((units, length, hd), bf),
            pltpu.VMEM((units, hd, length), f4),
            pltpu.VMEM((units, hd, length), f4),
            pltpu.VMEM((units, hd, length), f4),
            pltpu.VMEM((n, r, 3 * LANES), bf),
            dma((n,)),
            dma((n,)),
            dma,
        ],
        (grad_recv, qc, qp, keys, values, positions, probs, table),
    )
    input_grad, late, norm1_g = call(
        last_kernel,
        z,
        3,
        [VMEM] * 11,
        [
            ((items, full_rows, width), f4, VMEM),
            ((6 * width, width), bf, VMEM),
            ((2, width), f4, VMEM),
        ],
        [
            xf,
            xf,
            pltpu.VMEM((3, rows, width), bf),
            pltpu.VMEM((items, r + 8, width), f4),
            pltpu.VMEM((items, 16, width), bf),
            pltpu.VMEM((items, 16, width), bf),
            dma((2,)),
        ],
        (
            qkv_recv,
            hidden_grad,
            pooled,
            byte_rows,
            out_grad,
            gain1,
            bias1,
            query_weight,
            key_weight,
            value_weight,
            pool_weight,
        ),
    )
    own_head = lax.rem(lax.axis_index("seq"), heads)
    mine = (lax.broadcasted_iota(jnp.int32, (1, heads, 1), 1) == own_head).astype(f4)
    small = jnp.concatenate(
        [norm1_g, norm2_g, (head_bias_g[:, None, :] * mine).reshape(2, width)], axis=0
    )
    small = jnp.concatenate([small, jnp.zeros((2, width), f4)], axis=0)
    total, small_t = sum_all(z, lax.axis_size("batch"), early, late, head_g, small)
    blocks = total.shape[0] // width
    shapes = [
        ((items, full_rows, width), bf, ANY),
        ((items, full_rows, width), f4, ANY),
        ((3 * width, width), f4, ANY),
        ((1, width), f4, VMEM),
        ((1, width), f4, VMEM),
        ((width, width), f4, ANY),
        ((width, width), f4, ANY),
        ((width, width), f4, ANY),
        ((width, width), f4, ANY),
        ((heads, hd), f4, VMEM),
        ((heads, hd), f4, VMEM),
        ((width, width), f4, ANY),
        ((1, width), f4, VMEM),
        ((1, width), f4, VMEM),
        ((width, ff), f4, ANY),
        ((ff, width), f4, ANY),
        ((width, 3 * width), f4, ANY),
    ]
    results = pl.pallas_call(
        functools.partial(result_kernel, z, ff),
        out_shape=[jax.ShapeDtypeStruct(shape, dtype) for shape, dtype, _ in shapes],
        in_specs=[ANY, VMEM, ANY, ANY],
        out_specs=[space for _, _, space in shapes],
        scratch_shapes=[
            pltpu.VMEM((blocks, width, width), bf),
            pltpu.VMEM((blocks, width, width), f4),
            dma((blocks,)),
            dma((blocks,)),
            dma((2,)),
        ],
        compiler_params=pltpu.CompilerParams(vmem_limit_bytes=50 * 2**20),
    )(total, small_t, block_out, input_grad)
    return tuple(
        value.reshape(width) if value.shape == (1, width) else value for value in results
    )


def solution(mesh):
    split = P("batch", "seq", None)
    in_specs = (split, P("batch"), split) + (P(),) * 15
    out_specs = (split, split) + (P(),) * 15
    return jax.shard_map(body, mesh=mesh, in_specs=in_specs, out_specs=out_specs, check_vma=False)
```

```python
import functools

import jax
import jax.numpy as jnp
import numpy as np
from jax import lax
from jax.experimental import pallas as pl
from jax.experimental.pallas import tpu as pltpu
from jax.sharding import PartitionSpec as P

MESH = pl.DeviceIdType.MESH
epsilon = 1e-05
masked_value = -1e30
CHAINS = [(2, 0), (2, 1), (1, 2), (1, 3), (2, 0), (1, 1), (1, 8), (1, 4), (1, 5), (1, 0), (1, 1), (1, 3), (1, 9), (1, 2), (1, 4)]
EARLY_DONE = 9.0
BACK_DONE = 21.0
LATE = (31.0, 34.0)
BLOCK = 128
LANES = 128
VMEM = pl.BlockSpec(memory_space=pltpu.VMEM)
SMEM = pl.BlockSpec(memory_space=pltpu.SMEM)
ANY = pl.BlockSpec(memory_space=pl.ANY)


def dot(left, right):
    return jnp.dot(left, right, preferred_element_type=jnp.float32)


def dot_nt(left, right):
    return lax.dot_general(
        left, right, (((1,), (1,)), ((), ())), preferred_element_type=jnp.float32
    )


def dot_tn(left, right):
    return lax.dot_general(
        left, right, (((0,), (0,)), ((), ())), preferred_element_type=jnp.float32
    )


def low(value):
    return value.astype(jnp.bfloat16)


def distance_table(short_len, width):
    distance = (short_len - 1 - np.arange(short_len)).astype(np.float32)
    steps_in = np.arange(0, width, 2).astype(np.float32)
    frequency = np.exp(-np.log(np.float32(10000.0)) * steps_in / np.float32(width))
    angles = distance[:, None] * frequency[None, :].astype(np.float32)
    both = np.concatenate([np.sin(angles), np.cos(angles)], axis=1)
    return jnp.asarray(both.astype(jnp.bfloat16))


def norm_rows(rows):
    mean = jnp.mean(rows, axis=-1, keepdims=True)
    centered = rows - mean
    inverse = lax.rsqrt(jnp.mean(centered * centered, axis=-1, keepdims=True) + epsilon)
    return centered * inverse, inverse


def norm_backward(gradient, normed, inverse, gain):
    scaled = gradient * gain
    return inverse * (
        scaled
        - jnp.mean(scaled, axis=-1, keepdims=True)
        - normed * jnp.mean(scaled * normed, axis=-1, keepdims=True)
    )


class Sizes:
    def __init__(self, n, items, full_rows, width, heads):
        self.n = n
        self.items = items
        self.r = full_rows // 3
        self.width = width
        self.heads = heads
        self.hd = width // heads
        self.units = items * heads // n
        self.length = n * self.r
        self.rows = items * self.r
        assert n % heads == 0 and self.units * self.hd <= LANES


def send_all(n, me, source, target, send_sem, recv_sem):
    copies = []
    for step in range(1, n):
        peer = lax.rem(me + step, n)
        copies.append(
            pltpu.make_async_remote_copy(
                src_ref=source(peer),
                dst_ref=target.at[me],
                send_sem=send_sem.at[step],
                recv_sem=recv_sem.at[step],
                device_id={"seq": peer},
                device_id_type=MESH,
            )
        )
        copies[-1].start()
    return copies


def rows_by_three(z, x_ref, xf_ref):
    for item in range(z.items):
        for slab in range(z.width // LANES):
            xf_ref[item, slab, 8:, :] = x_ref[item, :, slab * LANES : (slab + 1) * LANES].astype(
                jnp.float32
            )


def every_third(z, xf_ref, first):
    items = []
    for item in range(z.items):
        slabs = [
            xf_ref[item, slab, pl.ds(first, z.r, stride=3), :] for slab in range(z.width // LANES)
        ]
        items.append(jnp.concatenate(slabs, axis=1))
    return jnp.concatenate(items, axis=0)


def set_every_third(z, xf_ref, first, value):
    for item in range(z.items):
        for slab in range(z.width // LANES):
            xf_ref[item, slab, pl.ds(first, z.r, stride=3), :] = value[
                item * z.r : (item + 1) * z.r, slab * LANES : (slab + 1) * LANES
            ]


def live_rows(z, me, length, part):
    at = lax.broadcasted_iota(jnp.int32, (z.r, 1), 0) * 3 + part + me * 3 * z.r
    return (at < length).astype(jnp.float32)


def reversal():
    at = lax.broadcasted_iota(jnp.int32, (BLOCK, BLOCK), 0)
    across = lax.broadcasted_iota(jnp.int32, (BLOCK, BLOCK), 1)
    return low((at + across == BLOCK - 1).astype(jnp.float32))


class Copies:
    def __init__(self, batch_size, seq_size):
        self.core = [("batch", 1)]
        self.chips = [("batch", 1 << k) for k in range(1, batch_size.bit_length() - 1)]
        self.line = [("seq", 1 << k) for k in range(seq_size.bit_length() - 1)]
        self.bits = self.core + self.chips + self.line

    def cost(self, bit, size):
        axis, mask = bit
        if bit in self.core:
            return {"core": size / 428e3}
        near = 2 * size / 92e3
        if bit in self.line[:1] or axis == "batch":
            return {bit: near}
        return {"line": near, bit: near * (mask // 2)}

    def orders(self):
        if len(self.bits) != 5:
            links = self.chips + self.line
            return [self.core + links[k:] + links[:k] for k in range(len(links))] * 4
        c, x, y, z0, z1 = self.bits
        names = (
            "xyz0z1",
            "yxz0z1",
            "yz0xz1",
            "z0xyz1",
            "z1xz0y",
            "yxz1z0",
            "xyz1z0",
            "yz0z1x",
            "xz0yz1",
            "z0z1xy",
        )
        found = []
        for name in names:
            order = [c]
            while name:
                for key, bit in (("x", x), ("y", y), ("z0", z0), ("z1", z1)):
                    if name.startswith(key):
                        order.append(bit)
                        name = name[len(key) :]
            found.append(order)
        return found

    def halving(self, rows, order, base):
        down, up = [], []
        for bit in order:
            if rows % 32 == 0:
                rows //= 2
                down.append(("sum", bit, rows, rows))
                up.append(("spread", bit, rows, rows))
            else:
                down.append(("sum", bit, 0, rows))
        return {"base": base, "fixed": [], "steps": down + up[::-1], "rows": rows}

    def by_head(self, heads, hd, base):
        head_bits = self.line[: heads.bit_length() - 1]
        batch_bits = self.core + self.chips
        rest = self.line[len(head_bits) :]
        rows, parts = hd, []
        for bit in batch_bits + rest:
            if rows % 32 == 0:
                rows //= 2
                parts.append((bit, rows))
            else:
                parts.append((bit, 0))
        split = [bit for bit, size in parts if size]
        inner = split[1:]
        stride, strides = rows, {}
        for bit in inner[::-1] + head_bits + split[:1]:
            strides[bit] = stride
            stride *= 2
        down = [("sum", bit, strides.get(bit, 0), size or rows) for bit, size in parts]
        up = [("spread", bit, strides[bit], strides[bit]) for bit in strides]
        fixed = [(bit, strides[bit]) for bit in head_bits]
        return {"base": base, "fixed": fixed, "steps": down + up, "rows": rows, "strides": strides}

    def schedule(self, chains, width, holds=()):
        left = []
        for chain in chains:
            total = [0.0]
            for _, bit, _, rows in chain["steps"][::-1]:
                busy = max(self.cost(bit, 2 * rows * width).values())
                total.append(total[-1] + busy + 2.0)
            left.append(total[::-1])
        free, ready = {}, [chain["ready"] for chain in chains]
        at = [0] * len(chains)
        plan, holds = [], sorted(holds, key=lambda hold: hold[0])
        self.end = 0.0
        while True:
            best = None
            for c, chain in enumerate(chains):
                if at[c] < len(chain["steps"]):
                    _, bit, _, rows = chain["steps"][at[c]]
                    cost = self.cost(bit, 2 * rows * width)
                    start = max([ready[c]] + [free.get(link, 0.0) for link in cost])
                    key = (round(start, 1), -left[c][at[c]], c)
                    if best is None or key < best[0]:
                        best = (key, c, cost, start)
            if best is None:
                return sorted(plan)
            _, c, cost, start = best
            if holds and start >= holds[0][0]:
                since, taken = holds.pop(0)
                for link, busy in taken.items():
                    free[link] = max(free.get(link, 0.0), since) + busy
                continue
            for link, busy in cost.items():
                free[link] = start + busy
            step = chains[c]["steps"][at[c]]
            lag = 0.7 if step[1] in self.core else 2.0
            lag += 1e-6 * 2 * step[3] * width if step[0] == "sum" else 0.0
            ready[c] = start + max(cost.values()) + lag
            self.end = max(self.end, ready[c])
            plan.append((start, c, at[c]))
            at[c] += 1


class Sums:
    def __init__(self, chains, work, landing, total, send_sems, recv_sems):
        self.chains = chains
        self.work, self.landing, self.total = work, landing, total
        self.send_sems, self.recv_sems = send_sems, recv_sems
        self.index = {"batch": lax.axis_index("batch"), "seq": lax.axis_index("seq")}
        self.open = {}
        self.offset = {}
        sem = land = 0
        self.sem, self.land = {}, {}
        for c, chain in enumerate(chains):
            self.offset[c] = chain["base"] + sum(
                self.bit(bit) * stride for bit, stride in chain["fixed"]
            )
            for k, (phase, _, _, rows) in enumerate(chain["steps"]):
                self.sem[c, k] = sem
                sem += 1
                if phase == "sum":
                    self.land[c, k] = land
                    land += rows

    @staticmethod
    def needs(chains):
        steps = [step for chain in chains for step in chain["steps"]]
        return len(steps), sum(step[3] for step in steps if step[0] == "sum")

    def bit(self, bit):
        axis, mask = bit
        return lax.rem(lax.div(self.index[axis], mask), 2)

    def partner(self, bit):
        axis, mask = bit
        return {axis: self.index[axis] + mask - 2 * mask * self.bit(bit)}

    def start(self, c, k):
        if k:
            self.finish(c, k - 1)
        phase, bit, stride, rows = self.chains[c]["steps"][k]
        side = self.bit(bit)
        offset = self.offset[c]
        if phase == "sum":
            other = offset + (1 - side) * stride if stride else offset
            source = self.work.at[pl.ds(pl.multiple_of(other, 16), rows)]
            target = self.landing.at[pl.ds(self.land[c, k], rows)]
            if stride:
                self.offset[c] = offset + side * stride
        else:
            here = pl.ds(pl.multiple_of(offset, 16), rows)
            source, target = self.total.at[here], self.total.at[here]
            self.offset[c] = offset - side * stride
        copy = pltpu.make_async_remote_copy(
            src_ref=source,
            dst_ref=target,
            send_sem=self.send_sems.at[self.sem[c, k]],
            recv_sem=self.recv_sems.at[self.sem[c, k]],
            device_id=self.partner(bit),
            device_id_type=MESH,
        )
        copy.start()
        self.open[c] = copy

    def finish(self, c, k):
        self.open.pop(c).wait()
        steps = self.chains[c]["steps"]
        phase, _, _, rows = steps[k]
        if phase == "sum":
            last = k + 1 == len(steps) or steps[k + 1][0] == "spread"
            held = pl.ds(pl.multiple_of(self.offset[c], 16), rows)
            landed = self.landing[self.land[c, k] : self.land[c, k] + rows, :]
            both = self.work[held, :].astype(jnp.float32) + landed.astype(jnp.float32)
            (self.total if last else self.work)[held, :] = low(both)


OPERANDS = (
    "x",
    "pool_w",
    "gain1",
    "bias1",
    "query_w",
    "key_w",
    "value_w",
    "og",
    "up_w",
    "outer_w",
    "table",
    "position_w",
    "content_bias",
    "position_bias",
    "output_w",
    "gain2",
    "bias2",
    "inner_w",
)


class Pass:
    def __init__(self, z, plan, chains, bits, names, refs):
        self.z = z
        self.__dict__.update(zip(names, refs))
        self.plan, self.chains, self.bits = plan, chains, bits
        self.me = lax.axis_index("seq")
        self.head = lax.rem(self.me, z.heads)
        self.group = lax.div(self.me, z.heads)
        self.sums = Sums(
            chains, self.work, self.landing, self.total, self.sum_send, self.sum_recv
        )
        self.at = 0
        self.loads = {}

    def run(self):
        self.enter()
        self.project()
        self.attend()
        self.feed_forward()
        self.attend_back()
        self.finish_rows()
        self.finish_sums()

    def enter(self):
        z, me = self.z, self.me
        for k, name in enumerate(OPERANDS):
            self.loads[name] = pltpu.make_async_copy(
                getattr(self, name), getattr(self, name + "_v"), self.load_sems.at[k]
            )
            self.loads[name].start()
        barrier = pltpu.get_barrier_semaphore()
        batch = [bit for bit in self.bits if bit[0] == "batch"]
        for step in range(1, z.n):
            pl.semaphore_signal(
                barrier,
                inc=1,
                device_id={"seq": lax.rem(me + step, z.n)},
                device_id_type=MESH,
            )
        for bit in batch:
            pl.semaphore_signal(
                barrier, inc=1, device_id=self.sums.partner(bit), device_id_type=MESH
            )
        self.have("x")
        rows_by_three(z, self.x_v, self.xf)
        pl.semaphore_wait(barrier, z.n - 1 + len(batch))

    def have(self, *names):
        for name in names:
            if name in self.loads:
                self.loads.pop(name).wait()

    def neighbour(self, source, target, sems, step):
        copy = pltpu.make_async_remote_copy(
            src_ref=source,
            dst_ref=target,
            send_sem=sems.at[0],
            recv_sem=sems.at[1],
            device_id={"seq": lax.rem(self.me + step, self.z.n)},
            device_id_type=MESH,
        )
        copy.start()
        return copy

    def exchange(self, source, target, send, recv):
        copies = send_all(self.z.n, self.me, lambda peer: source.at[peer], target, send, recv)
        target[self.me] = source[self.me]
        return copies

    def by_head(self, target, values):
        z = self.z
        pad = [jnp.zeros((z.r, z.hd), jnp.bfloat16)] * (LANES // z.hd - z.units)
        lanes = slice(target % z.heads * z.hd, (target % z.heads + 1) * z.hd)
        sides = []
        for value in values:
            for unit in range(z.units):
                item = target // z.heads * z.units + unit
                sides.append(value[item * z.r : (item + 1) * z.r, lanes])
            sides += pad
        return jnp.concatenate(sides, axis=1)

    def to_rows(self, source_ref, which, target_ref):
        z = self.z
        for source in range(z.n):
            for unit in range(z.units):
                item = source // z.heads * z.units + unit
                head = source % z.heads
                first = which * LANES + unit * z.hd
                target_ref[item * z.r : (item + 1) * z.r, head * z.hd : (head + 1) * z.hd] = (
                    source_ref[source, :, first : first + z.hd]
                )

    def live(self, part):
        z = self.z
        rows = [live_rows(z, self.me, self.lengths[item], part) for item in range(z.items)]
        return jnp.concatenate(rows, axis=0)

    def project(self):
        z, me, r, width = self.z, self.me, self.z.r, self.z.width
        halo = self.neighbour(
            self.x_v.at[:, 3 * r - 16 :, :], self.halo, self.halo_sems, 1
        )
        self.have("pool_w")
        pooled = dot(low(every_third(z, self.xf, 8)), self.pool_w_v[2 * width :, :])
        halo.wait()
        for item in range(z.items):
            before = jnp.where(me > 0, self.halo[item].astype(jnp.float32), 0.0)
            for slab in range(width // LANES):
                self.xf[item, slab, 0:8, :] = before[8:16, slab * LANES : (slab + 1) * LANES]
        for part in range(2):
            pooled += dot(
                low(every_third(z, self.xf, 6 + part)),
                self.pool_w_v[part * width : (part + 1) * width, :],
            )
        self.short[...] = low(pooled)
        normed, inverse = norm_rows(self.short[...].astype(jnp.float32))
        self.normed1[...] = normed
        self.inverse1[...] = inverse
        self.have("gain1", "bias1", "query_w", "key_w", "value_w")
        self.attn_in[...] = low(normed * self.gain1_v[...] + self.bias1_v[...])
        attn_in = self.attn_in[...]
        qkv = [low(dot(attn_in, w[...])) for w in (self.query_w_v, self.key_w_v, self.value_w_v)]
        for target in range(z.n):
            self.qkv_out[target] = self.by_head(target, qkv)
        copies = self.exchange(self.qkv_out, self.qkv_in, self.qkv_send, self.qkv_recv)
        self.have("og", "up_w", "outer_w")
        rows_by_three(z, self.og_v, self.of)
        for part in range(3):
            self.up_rows[:, part * width : (part + 1) * width] = low(
                every_third(z, self.of, 8 + part) * self.live(part)
            )
        self.summed_grad[...] = low(dot_nt(self.up_rows[...], self.up_w_v[...]))
        ff = self.outer_w_v.shape[0]
        for lo in range(0, ff, width):
            self.act_grad[:, lo : lo + width] = dot_nt(
                self.summed_grad[...], self.outer_w_v[lo : lo + width, :]
            )
        self.have("table", "position_w", "content_bias", "position_bias")
        first = self.head * z.hd
        pair = pl.ds(pl.multiple_of(lax.div(first, LANES) * LANES, LANES), LANES)
        both = dot(self.table_v[...], self.position_w_v[:, pair])
        self.pos[...] = low(pltpu.roll(both, LANES - lax.rem(first, LANES), 1)[:, : z.hd])
        for copy in copies:
            copy.wait()

    def attend(self):
        z, r, hd = self.z, self.z.r, self.z.hd
        content_bias = self.content_bias_v[pl.ds(self.head, 1), :]
        position_bias = self.position_bias_v[pl.ds(self.head, 1), :]
        for unit in range(z.units):
            queries, keys, values = (
                self.qkv_in[:, :, which * LANES + unit * hd : which * LANES + (unit + 1) * hd]
                .reshape(z.length, hd)
                for which in range(3)
            )
            self.qc[unit] = low(queries.astype(jnp.float32) + content_bias)
            self.qp[unit] = low(queries.astype(jnp.float32) + position_bias)
            self.keys[unit] = keys
            self.values[unit] = values
        for block in range(z.length // BLOCK):
            lo, hi = block * BLOCK, (block + 1) * BLOCK
            sides = []
            for unit in range(z.units):
                length = self.lengths[self.group * z.units + unit]
                content = dot_nt(self.qc[unit, lo:hi, :], self.keys[unit, :hi, :])
                by_distance = dot_nt(self.qp[unit, lo:hi, :], self.pos[z.length - hi :, :])
                placed = pltpu.roll(by_distance, lo + 1, 1, stride=1, stride_axis=0)
                query_at = lo + lax.broadcasted_iota(jnp.int32, (BLOCK, hi), 0)
                key_at = lax.broadcasted_iota(jnp.int32, (BLOCK, hi), 1)
                valid = (key_at <= query_at) & (3 * key_at < length)
                logits = jnp.where(valid, (content + placed) * hd**-0.5, masked_value)
                raised = jnp.exp(logits - jnp.max(logits, axis=-1, keepdims=True))
                probs = raised / jnp.sum(raised, axis=-1, keepdims=True)
                self.probs[unit, lo:hi, :hi] = probs
                sides.append(low(dot(low(probs), self.values[unit, :hi, :])))
            sides += [jnp.zeros((BLOCK, hd), jnp.bfloat16)] * (LANES // hd - z.units)
            per = BLOCK // r
            self.att_out[block * per : (block + 1) * per] = jnp.concatenate(
                sides, axis=1
            ).reshape(per, r, LANES)
        copies = self.exchange(self.att_out, self.att_in, self.att_send, self.att_recv)
        self.have("output_w", "gain2", "bias2", "inner_w")
        for copy in copies:
            copy.wait()

    def feed_forward(self):
        z, width = self.z, self.z.width
        ff = self.outer_w_v.shape[0]
        self.to_rows(self.att_in, 0, self.att)
        hidden = self.short[...].astype(jnp.float32) + dot(self.att[...], self.output_w_v[...])
        normed, inverse = norm_rows(hidden)
        self.hidden[...] = hidden
        self.ffn_in[...] = low(normed * self.gain2_v[...] + self.bias2_v[...])
        ffn_in = self.ffn_in[...]
        ffn_grad = jnp.zeros((z.rows, width), jnp.float32)
        for lo in range(0, ff, width):
            cut = slice(lo, lo + width)
            inner = dot(ffn_in, self.inner_w_v[:, cut])
            normal_cdf = 0.5 * (1.0 + lax.erf(inner * 0.7071067811865476))
            density = jnp.exp(-0.5 * inner * inner) * 0.3989422804014327
            self.act[:, cut] = low(inner * normal_cdf)
            inner_grad = low(self.act_grad[:, cut] * (normal_cdf + inner * density))
            self.inner_grad[:, cut] = inner_grad
            ffn_grad += dot_nt(inner_grad, self.inner_w_v[:, cut])
        self.small_work[0, 2:3, :] = jnp.sum(ffn_grad * normed, axis=0, keepdims=True)
        self.small_work[0, 3:4, :] = jnp.sum(ffn_grad, axis=0, keepdims=True)
        hidden_grad = self.summed_grad[...].astype(jnp.float32) + norm_backward(
            ffn_grad, normed, inverse, self.gain2_v[...]
        )
        self.hidden_grad[...] = hidden_grad
        self.branch[...] = low(hidden_grad)
        att_grad = low(dot_nt(self.branch[...], self.output_w_v[...]))
        for target in range(z.n):
            self.grad_out[target] = self.by_head(target, [att_grad])
        self.copies = self.exchange(self.grad_out, self.grad_in, self.grad_send, self.grad_recv)
        row = 0
        for lo in range(0, ff, width):
            self.work[row : row + width, :] = low(
                dot_tn(self.act[:, lo : lo + width], self.summed_grad[...])
            )
            row += width
            self.advance(0.6 * row / width)
        for lo in range(0, ff, width):
            self.work[row : row + width, :] = low(
                dot_tn(self.ffn_in[...], self.inner_grad[:, lo : lo + width])
            )
            row += width
            self.advance(0.6 * row / width)
        self.work[row : row + width, :] = low(dot_tn(self.att[...], self.branch[...]))
        row += width
        self.summed[...] = low(self.hidden[...] + dot(self.act[...], self.outer_w_v[...]))
        for lo in range(0, 3 * width, width):
            self.work[row : row + width, :] = low(
                dot_tn(self.summed[...], self.up_rows[:, lo : lo + width])
            )
            row += width
            self.advance(1.8 + 0.6 * row / width)
        self.row = row
        for copy in self.copies:
            copy.wait()

    def upsample(self):
        z, width = self.z, self.z.width
        for part in range(3):
            up = dot(self.summed[...], self.up_w_v[:, part * width : (part + 1) * width])
            set_every_third(
                z, self.bf, 8 + part, every_third(z, self.xf, 8 + part) + up * self.live(part)
            )
        for item in range(z.items):
            for slab in range(width // LANES):
                self.block_low[item, :, slab * LANES : (slab + 1) * LANES] = low(
                    self.bf[item, slab, 8:, :]
                )
        self.block_store = pltpu.make_async_copy(
            self.block_low, self.block_out, self.out_sems.at[0]
        )
        self.block_store.start()

    def attend_back(self):
        z, r, hd, length = self.z, self.z.r, self.z.hd, self.z.length
        flip = reversal()
        content_sum = jnp.zeros((1, hd), jnp.float32)
        position_sum = jnp.zeros((1, hd), jnp.float32)
        self.key_t[...] = jnp.zeros_like(self.key_t)
        self.value_t[...] = jnp.zeros_like(self.value_t)
        self.table_t[...] = jnp.zeros_like(self.table_t)
        now = EARLY_DONE
        for unit in range(z.units):
            att_grad = self.grad_in[:, :, unit * hd : (unit + 1) * hd].reshape(length, hd)
            for block in range(length // BLOCK):
                lo, hi = block * BLOCK, (block + 1) * BLOCK
                block_grad = att_grad[lo:hi]
                probs = self.probs[unit, lo:hi, :hi]
                prob_grad = dot_nt(block_grad, self.values[unit, :hi, :])
                delta = jnp.sum(probs * prob_grad, axis=-1, keepdims=True)
                raw = low(probs * (prob_grad - delta) * hd**-0.5)
                content = dot(raw, self.keys[unit, :hi, :])
                self.key_t[unit, :, :hi] += dot_tn(self.qc[unit, lo:hi, :], raw)
                self.value_t[unit, :, :hi] += dot_tn(block_grad, low(probs))
                by_distance = low(pltpu.roll(dot(flip, raw), 0, 1, stride=1, stride_axis=0))
                position = dot(by_distance, self.pos[length - hi :, :])
                upper = low(position)
                lower = low(position - upper.astype(jnp.float32))
                position = dot(flip, upper) + dot(flip, lower)
                flipped_q = low(dot(flip, self.qp[unit, lo:hi, :]))
                self.table_t[unit, :, length - hi :] += dot_tn(flipped_q, by_distance)
                content_sum += jnp.sum(content, axis=0, keepdims=True)
                position_sum += jnp.sum(position, axis=0, keepdims=True)
                self.query_grad[unit, lo:hi, :] = low(content + position)
                now += 1.2
                self.advance(now)
        own = lax.broadcasted_iota(jnp.int32, (1, z.width), 1) // hd == self.head
        for row, value in ((4, content_sum), (5, position_sum)):
            spread = jnp.concatenate([value] * z.heads, axis=1)
            self.small_work[0, row : row + 1, :] = jnp.where(own, spread, 0.0)
        pad = [jnp.zeros((length, hd), jnp.bfloat16)] * (LANES // hd - z.units)
        sides = [self.query_grad[unit] for unit in range(z.units)] + pad
        sides += [low(self.key_t[unit].T) for unit in range(z.units)] + pad
        sides += [low(self.value_t[unit].T) for unit in range(z.units)] + pad
        self.back_out[...] = jnp.concatenate(sides, axis=1).reshape(z.n, r, 3 * LANES)
        copies = self.exchange(self.back_out, self.back_in, self.back_send, self.back_recv)
        table_sum = 0.0
        for unit in range(z.units):
            table_sum += dot(low(self.table_t[unit]), self.table_v[...])
        half = hd // 2
        base = self.chains[-1]["base"]
        for side in range(2):
            at = pl.multiple_of(base + side * z.heads * half + self.head * half, 16)
            self.work[pl.ds(at, half), :] = low(table_sum[side * half : (side + 1) * half])
        self.advance(BACK_DONE)
        self.upsample()
        self.advance(BACK_DONE + 4.0)
        for copy in copies:
            copy.wait()

    def finish_rows(self):
        z, me, r, width = self.z, self.me, self.z.r, self.z.width
        for which in range(3):
            self.to_rows(self.back_in, which, self.row_grad.at[which])
        attn_grad = (
            dot_nt(self.row_grad[0], self.query_w_v[...])
            + dot_nt(self.row_grad[1], self.key_w_v[...])
            + dot_nt(self.row_grad[2], self.value_w_v[...])
        )
        normed = self.normed1[...]
        self.small_work[0, 0:1, :] = jnp.sum(attn_grad * normed, axis=0, keepdims=True)
        self.small_work[0, 1:2, :] = jnp.sum(attn_grad, axis=0, keepdims=True)
        self.small_work[0, 6:8, :] = jnp.zeros((2, width), jnp.float32)
        short_grad = low(
            self.hidden_grad[...]
            + norm_backward(attn_grad, normed, self.inverse1[...], self.gain1_v[...])
        )
        for item in range(z.items):
            self.first_rows[item] = short_grad[item * r : item * r + 16, :]
            self.later[item, 0:r, :] = short_grad[item * r : (item + 1) * r, :].astype(jnp.float32)
        halo = self.neighbour(self.first_rows, self.next_rows, self.next_sems, z.n - 1)
        self.small_start(0)
        row = self.row
        for which in range(3):
            self.work[row : row + width, :] = low(dot_tn(self.attn_in[...], self.row_grad[which]))
            row += width
        self.advance(LATE[0])
        own = dot_nt(short_grad, self.pool_w_v[2 * width :, :])
        set_every_third(z, self.of, 8, every_third(z, self.of, 8) + own)
        self.work[row + 2 * width : row + 3 * width, :] = low(
            dot_tn(low(every_third(z, self.xf, 8)), short_grad)
        )
        halo.wait()
        for item in range(z.items):
            after = jnp.where(me < z.n - 1, self.next_rows[item].astype(jnp.float32), 0.0)
            self.later[item, r : r + 8, :] = after[0:8, :]
        later = low(
            jnp.concatenate([self.later[item, 1 : r + 1, :] for item in range(z.items)], axis=0)
        )
        for part in range(2):
            cut = slice(row + part * width, row + (part + 1) * width)
            self.work[cut, :] = low(dot_tn(low(every_third(z, self.xf, 9 + part)), later))
        self.advance(LATE[1])
        for part in range(2):
            back = dot_nt(later, self.pool_w_v[part * width : (part + 1) * width, :])
            first = 9 + part
            set_every_third(z, self.of, first, every_third(z, self.of, first) + back)
        for item in range(z.items):
            for slab in range(width // LANES):
                self.input_rows[item, :, slab * LANES : (slab + 1) * LANES] = self.of[
                    item, slab, 8:, :
                ]
        self.input_store = pltpu.make_async_copy(
            self.input_rows, self.input_grad, self.out_sems.at[1]
        )
        self.input_store.start()

    def advance(self, now):
        while self.at < len(self.plan) and self.plan[self.at][0] <= now:
            _, c, k = self.plan[self.at]
            self.sums.start(c, k)
            self.at += 1

    def small_start(self, k):
        self.small_copy = pltpu.make_async_remote_copy(
            src_ref=self.small_work.at[k],
            dst_ref=self.small_landing.at[k],
            send_sem=self.small_send.at[k],
            recv_sem=self.small_recv.at[k],
            device_id=self.sums.partner(self.bits[k]),
            device_id_type=MESH,
        )
        self.small_copy.start()

    def finish_sums(self):
        steps = len(self.bits)
        first = self.plan[self.at][0] if self.at < len(self.plan) else 0.0
        for k in range(steps):
            self.advance(first + 3.0 * (k + 1))
            self.small_copy.wait()
            self.small_work[k + 1] = self.small_work[k] + self.small_landing[k]
            if k + 1 < steps:
                self.small_start(k + 1)
        self.small_total[...] = self.small_work[steps]
        ends = {}
        for order, (_, c, k) in enumerate(self.plan):
            ends[c] = order
        stores = []
        for c in sorted(ends, key=ends.get):
            while self.at <= ends[c]:
                self.sums.start(*self.plan[self.at][1:])
                self.at += 1
            self.sums.finish(c, len(self.chains[c]["steps"]) - 1)
            at, size = self.chains[c]["base"], self.chains[c]["all"]
            stores.append(
                pltpu.make_async_copy(
                    self.total.at[at : at + size],
                    self.total_out.at[at : at + size],
                    self.store_sems.at[c],
                )
            )
            stores[-1].start()
        for store in stores + [self.block_store, self.input_store]:
            store.wait()


def block_kernel(z, plan, chains, bits, names, *refs):
    Pass(z, plan, chains, bits, names, refs).run()


def chains_of(z, ff, nb):
    width = z.width
    copies = Copies(nb, z.n)
    orders = copies.orders()
    units = 3 * (ff * 2 + width * 10) // width // 3
    early = 2 * ff // width + 4
    chosen = CHAINS if len(copies.bits) == 5 and sum(rows for rows, _ in CHAINS) == units else None
    if chosen is None:
        chosen = [(1, k) for k in range(units)]
    chains, base = [], 0
    for rows, order in chosen:
        chains.append(copies.halving(rows * width, orders[order % len(orders)], base * width))
        chains[-1]["all"] = rows * width
        base += rows
        if base <= early - 3:
            chains[-1]["ready"] = 0.6 * base
        elif base <= early:
            chains[-1]["ready"] = 1.8 + 0.6 * base
        else:
            chains[-1]["ready"] = LATE[0] if base <= early + 3 else LATE[1]
    chains.append(copies.by_head(z.heads, z.hd, base * width))
    chains[-1]["all"] = z.heads * z.hd
    chains[-1]["ready"] = BACK_DONE
    return copies, chains


def result_kernel(
    z,
    ff,
    total_ref,
    small_ref,
    block_in_ref,
    input_in_ref,
    block_ref,
    input_ref,
    pool_ref,
    gain1_ref,
    bias1_ref,
    query_ref,
    key_ref,
    value_ref,
    position_ref,
    content_bias_ref,
    position_bias_ref,
    output_ref,
    gain2_ref,
    bias2_ref,
    inner_ref,
    outer_ref,
    up_ref,
    held,
    wide,
    load_sems,
    store_sems,
    pass_sems,
):
    width = z.width
    through = [
        pltpu.make_async_copy(block_in_ref, block_ref, pass_sems.at[0]),
        pltpu.make_async_copy(input_in_ref, input_ref, pass_sems.at[1]),
    ]
    blocks = held.shape[0]
    loads = [
        pltpu.make_async_copy(
            total_ref.at[k * width : (k + 1) * width], held.at[k], load_sems.at[k]
        )
        for k in range(blocks)
    ]
    for copy in loads + through:
        copy.start()
    places = [outer_ref.at[k * width : (k + 1) * width] for k in range(ff // width)]
    places += [inner_ref.at[:, k * width : (k + 1) * width] for k in range(ff // width)]
    places += [output_ref]
    places += [up_ref.at[:, k * width : (k + 1) * width] for k in range(3)]
    places += [query_ref, key_ref, value_ref]
    places += [pool_ref.at[k * width : (k + 1) * width] for k in range(3)]
    places += [position_ref]
    gain1_ref[...] = small_ref[0:1, :]
    bias1_ref[...] = small_ref[1:2, :]
    gain2_ref[...] = small_ref[2:3, :]
    bias2_ref[...] = small_ref[3:4, :]
    for head in range(z.heads):
        lanes = slice(head * z.hd, (head + 1) * z.hd)
        content_bias_ref[head : head + 1, :] = small_ref[4:5, lanes]
        position_bias_ref[head : head + 1, :] = small_ref[5:6, lanes]
    stores = []
    for k in range(blocks):
        loads[k].wait()
        if k + 1 < blocks:
            wide[k] = held[k].astype(jnp.float32)
        else:
            half = z.hd // 2
            for head in range(z.heads):
                rows = [
                    held[k, side * z.heads * half + head * half :][:half] for side in range(2)
                ]
                both = jnp.concatenate(rows, axis=0).astype(jnp.float32)
                wide[k, :, head * z.hd : (head + 1) * z.hd] = both.T
        stores.append(pltpu.make_async_copy(wide.at[k], places[k], store_sems.at[k]))
        stores[-1].start()
    for copy in stores + through:
        copy.wait()


def body(
    byte_rows,
    item_lengths,
    out_grad,
    pool_weight,
    norm1_gain,
    norm1_bias,
    query_weight,
    key_weight,
    value_weight,
    position_weight,
    content_bias,
    position_bias,
    output_weight,
    norm2_gain,
    norm2_bias,
    inner_weight,
    outer_weight,
    upsample_weight,
):
    items, full_rows, width = byte_rows.shape
    heads, hd = content_bias.shape
    n = lax.axis_size("seq")
    ff = inner_weight.shape[1]
    z = Sizes(n, items, full_rows, width, heads)
    r, units, length, rows = z.r, z.units, z.length, z.rows
    bf, f4 = jnp.bfloat16, jnp.float32
    slabs = width // LANES
    dma = pltpu.SemaphoreType.DMA
    copies, chains = chains_of(z, ff, lax.axis_size("batch"))
    near = 16 * n * 0.001
    holds = [
        (0.0, {("seq", 1): 0.7 * near * 16, "line": 1.4 * near * 16}),
        (BACK_DONE - 2.0, {("seq", 1): 2.1 * near * 16, "line": 4.2 * near * 16}),
    ]
    plan = copies.schedule(chains, width, holds)
    bits = copies.bits
    count, landing = Sums.needs(chains)
    total_rows = chains[-1]["base"] + chains[-1]["all"]
    operands = {
        "x": byte_rows,
        "pool_w": pool_weight,
        "gain1": norm1_gain.reshape(1, width),
        "bias1": norm1_bias.reshape(1, width),
        "query_w": query_weight,
        "key_w": key_weight,
        "value_w": value_weight,
        "og": out_grad,
        "up_w": upsample_weight,
        "outer_w": outer_weight,
        "table": distance_table(length, width),
        "position_w": position_weight,
        "content_bias": content_bias,
        "position_bias": position_bias,
        "output_w": output_weight,
        "gain2": norm2_gain.reshape(1, width),
        "bias2": norm2_bias.reshape(1, width),
        "inner_w": inner_weight,
    }
    outs = {
        "block_out": (byte_rows.shape, bf, ANY),
        "input_grad": (byte_rows.shape, f4, ANY),
        "total_out": ((total_rows, width), bf, ANY),
        "small_total": ((8, width), f4, VMEM),
    }
    slab_rows = pltpu.VMEM((items, slabs, 3 * r + 8, LANES), f4)
    scratch = {name + "_v": pltpu.VMEM(operands[name].shape, operands[name].dtype) for name in OPERANDS}
    scratch.update(
        xf=slab_rows,
        of=slab_rows,
        bf=slab_rows,
        block_low=pltpu.VMEM(byte_rows.shape, bf),
        input_rows=pltpu.VMEM(byte_rows.shape, f4),
        halo=pltpu.VMEM((items, 16, width), bf),
        first_rows=pltpu.VMEM((items, 16, width), bf),
        next_rows=pltpu.VMEM((items, 16, width), bf),
        later=pltpu.VMEM((items, r + 8, width), f4),
        short=pltpu.VMEM((rows, width), bf),
        normed1=pltpu.VMEM((rows, width), f4),
        inverse1=pltpu.VMEM((rows, 1), f4),
        attn_in=pltpu.VMEM((rows, width), bf),
        qkv_out=pltpu.VMEM((n, r, 3 * LANES), bf),
        qkv_in=pltpu.VMEM((n, r, 3 * LANES), bf),
        att_out=pltpu.VMEM((n, r, LANES), bf),
        att_in=pltpu.VMEM((n, r, LANES), bf),
        grad_out=pltpu.VMEM((n, r, LANES), bf),
        grad_in=pltpu.VMEM((n, r, LANES), bf),
        back_out=pltpu.VMEM((n, r, 3 * LANES), bf),
        back_in=pltpu.VMEM((n, r, 3 * LANES), bf),
        qc=pltpu.VMEM((units, length, hd), bf),
        qp=pltpu.VMEM((units, length, hd), bf),
        keys=pltpu.VMEM((units, length, hd), bf),
        values=pltpu.VMEM((units, length, hd), bf),
        pos=pltpu.VMEM((length, hd), bf),
        probs=pltpu.VMEM((units, length, length), f4),
        query_grad=pltpu.VMEM((units, length, hd), bf),
        key_t=pltpu.VMEM((units, hd, length), f4),
        value_t=pltpu.VMEM((units, hd, length), f4),
        table_t=pltpu.VMEM((units, hd, length), f4),
        att=pltpu.VMEM((rows, width), bf),
        hidden=pltpu.VMEM((rows, width), f4),
        ffn_in=pltpu.VMEM((rows, width), bf),
        act=pltpu.VMEM((rows, ff), bf),
        act_grad=pltpu.VMEM((rows, ff), f4),
        inner_grad=pltpu.VMEM((rows, ff), bf),
        up_rows=pltpu.VMEM((rows, 3 * width), bf),
        summed=pltpu.VMEM((rows, width), bf),
        summed_grad=pltpu.VMEM((rows, width), bf),
        hidden_grad=pltpu.VMEM((rows, width), f4),
        branch=pltpu.VMEM((rows, width), bf),
        row_grad=pltpu.VMEM((3, rows, width), bf),
        work=pltpu.VMEM((total_rows, width), bf),
        landing=pltpu.VMEM((landing, width), bf),
        total=pltpu.VMEM((total_rows, width), bf),
        small_work=pltpu.VMEM((len(bits) + 1, 8, width), f4),
        small_landing=pltpu.VMEM((len(bits), 8, width), f4),
        load_sems=dma((len(OPERANDS),)),
        halo_sems=dma((2,)),
        next_sems=dma((2,)),
        qkv_send=dma((n,)),
        qkv_recv=dma((n,)),
        att_send=dma((n,)),
        att_recv=dma((n,)),
        grad_send=dma((n,)),
        grad_recv=dma((n,)),
        back_send=dma((n,)),
        back_recv=dma((n,)),
        sum_send=dma((count,)),
        sum_recv=dma((count,)),
        small_send=dma((len(bits),)),
        small_recv=dma((len(bits),)),
        store_sems=dma((len(chains),)),
        out_sems=dma((2,)),
    )
    names = ("lengths",) + OPERANDS + tuple(outs) + tuple(scratch)
    block_out, input_grad, total, small_t = pl.pallas_call(
        functools.partial(block_kernel, z, plan, chains, bits, names),
        out_shape=[jax.ShapeDtypeStruct(shape, dtype) for shape, dtype, _ in outs.values()],
        in_specs=[SMEM] + [ANY] * len(OPERANDS),
        out_specs=[space for _, _, space in outs.values()],
        scratch_shapes=list(scratch.values()),
        compiler_params=pltpu.CompilerParams(
            collective_id=0, has_side_effects=True, vmem_limit_bytes=60 * 2**20
        ),
    )(item_lengths, *(operands[name] for name in OPERANDS))
    blocks = total.shape[0] // width
    shapes = [
        ((items, full_rows, width), bf, ANY),
        ((items, full_rows, width), f4, ANY),
        ((3 * width, width), f4, ANY),
        ((1, width), f4, VMEM),
        ((1, width), f4, VMEM),
        ((width, width), f4, ANY),
        ((width, width), f4, ANY),
        ((width, width), f4, ANY),
        ((width, width), f4, ANY),
        ((heads, hd), f4, VMEM),
        ((heads, hd), f4, VMEM),
        ((width, width), f4, ANY),
        ((1, width), f4, VMEM),
        ((1, width), f4, VMEM),
        ((width, ff), f4, ANY),
        ((ff, width), f4, ANY),
        ((width, 3 * width), f4, ANY),
    ]
    results = pl.pallas_call(
        functools.partial(result_kernel, z, ff),
        out_shape=[jax.ShapeDtypeStruct(shape, dtype) for shape, dtype, _ in shapes],
        in_specs=[ANY, VMEM, ANY, ANY],
        out_specs=[space for _, _, space in shapes],
        scratch_shapes=[
            pltpu.VMEM((blocks, width, width), bf),
            pltpu.VMEM((blocks, width, width), f4),
            dma((blocks,)),
            dma((blocks,)),
            dma((2,)),
        ],
        compiler_params=pltpu.CompilerParams(vmem_limit_bytes=50 * 2**20),
    )(total, small_t, block_out, input_grad)
    return tuple(
        value.reshape(width) if value.shape == (1, width) else value for value in results
    )


def solution(mesh):
    split = P("batch", "seq", None)
    in_specs = (split, P("batch"), split) + (P(),) * 15
    out_specs = (split, split) + (P(),) * 15
    return jax.shard_map(body, mesh=mesh, in_specs=in_specs, out_specs=out_specs, check_vma=False)
```

```python
import functools

import jax
import jax.numpy as jnp
import numpy as np
from jax import lax
from jax.experimental import pallas as pl
from jax.experimental.pallas import tpu as pltpu
from jax.sharding import PartitionSpec as P

MESH = pl.DeviceIdType.MESH
epsilon = 1e-05
masked_value = -1e30
CHAINS = (
    (1, "z1xyz0"),
    (2, "xyz0z1"),
    (1, "z0z1yx"),
    (2, "yxz0z1"),
    (1, "z0yz1x"),
    (1, "yxz0z1"),
    (2, "xyz0z1"),
    (1, "yxz1z0"),
    (1, "z0xyz1"),
    (1, "xyz0z1"),
    (1, "yxz0z1"),
    (1, "yxz1z0"),
    (1, "yxz0z1"),
    (1, "xyz1z0"),
    (1, "xyz0z1"),
)
LAG, CORE_LAG, ISSUE, MARGIN = 2.8, 1.0, 0.15, 0.3
UNIT, BLOCK_STEP, SEND, TABLE, UP, ROWS, QKV, POOL, INPUT = 0.33, 0.7, 0.3, 0.4, 1.5, 2.2, 0.9, 1.6, 1.2
BLOCK = 128
LANES = 128
VMEM = pl.BlockSpec(memory_space=pltpu.VMEM)
SMEM = pl.BlockSpec(memory_space=pltpu.SMEM)
ANY = pl.BlockSpec(memory_space=pl.ANY)


def dot(left, right):
    return jnp.dot(left, right, preferred_element_type=jnp.float32)


def dot_nt(left, right):
    return lax.dot_general(
        left, right, (((1,), (1,)), ((), ())), preferred_element_type=jnp.float32
    )


def dot_tn(left, right):
    return lax.dot_general(
        left, right, (((0,), (0,)), ((), ())), preferred_element_type=jnp.float32
    )


def low(value):
    return value.astype(jnp.bfloat16)


def distance_table(short_len, width):
    distance = (short_len - 1 - np.arange(short_len)).astype(np.float32)
    steps_in = np.arange(0, width, 2).astype(np.float32)
    frequency = np.exp(-np.log(np.float32(10000.0)) * steps_in / np.float32(width))
    angles = distance[:, None] * frequency[None, :].astype(np.float32)
    both = np.concatenate([np.sin(angles), np.cos(angles)], axis=1)
    return jnp.asarray(both.astype(jnp.bfloat16))


def norm_rows(rows):
    mean = jnp.mean(rows, axis=-1, keepdims=True)
    centered = rows - mean
    inverse = lax.rsqrt(jnp.mean(centered * centered, axis=-1, keepdims=True) + epsilon)
    return centered * inverse, inverse


def norm_backward(gradient, normed, inverse, gain):
    scaled = gradient * gain
    return inverse * (
        scaled
        - jnp.mean(scaled, axis=-1, keepdims=True)
        - normed * jnp.mean(scaled * normed, axis=-1, keepdims=True)
    )


class Sizes:
    def __init__(self, n, items, full_rows, width, heads):
        self.n = n
        self.items = items
        self.r = full_rows // 3
        self.width = width
        self.heads = heads
        self.hd = width // heads
        self.units = items * heads // n
        self.length = n * self.r
        self.rows = items * self.r
        assert n % heads == 0 and self.units * self.hd <= LANES


class Exchange:
    def __init__(self, n, me, source, target, sems):
        target[me] = source[me]
        for step in range(1, n):
            peer = lax.rem(me + step, n)
            pltpu.make_async_remote_copy(
                src_ref=source.at[peer],
                dst_ref=target.at[me],
                send_sem=sems.at[0],
                recv_sem=sems.at[1],
                device_id={"seq": peer},
                device_id_type=MESH,
            ).start()
        self.all = pltpu.make_async_remote_copy(
            src_ref=source.at[1:],
            dst_ref=target.at[1:],
            send_sem=sems.at[0],
            recv_sem=sems.at[1],
            device_id={"seq": lax.rem(me + 1, n)},
            device_id_type=MESH,
        )

    def wait(self):
        self.all.wait()


def rows_by_three(z, x_ref, xf_ref):
    for item in range(z.items):
        for slab in range(z.width // LANES):
            xf_ref[item, slab, 8:, :] = x_ref[item, :, slab * LANES : (slab + 1) * LANES].astype(
                jnp.float32
            )


def every_third(z, xf_ref, first):
    items = []
    for item in range(z.items):
        slabs = [
            xf_ref[item, slab, pl.ds(first, z.r, stride=3), :] for slab in range(z.width // LANES)
        ]
        items.append(jnp.concatenate(slabs, axis=1))
    return jnp.concatenate(items, axis=0)


def set_every_third(z, xf_ref, first, value):
    for item in range(z.items):
        for slab in range(z.width // LANES):
            xf_ref[item, slab, pl.ds(first, z.r, stride=3), :] = value[
                item * z.r : (item + 1) * z.r, slab * LANES : (slab + 1) * LANES
            ]


def live_rows(z, me, length, part):
    at = lax.broadcasted_iota(jnp.int32, (z.r, 1), 0) * 3 + part + me * 3 * z.r
    return (at < length).astype(jnp.float32)


def reversal():
    at = lax.broadcasted_iota(jnp.int32, (BLOCK, BLOCK), 0)
    across = lax.broadcasted_iota(jnp.int32, (BLOCK, BLOCK), 1)
    return low((at + across == BLOCK - 1).astype(jnp.float32))


class Copies:
    def __init__(self, batch_size, seq_size):
        self.core = [("batch", 1)]
        self.chips = [("batch", 1 << k) for k in range(1, batch_size.bit_length() - 1)]
        self.line = [("seq", 1 << k) for k in range(seq_size.bit_length() - 1)]
        self.bits = self.core + self.chips + self.line

    def cost(self, bit, size):
        axis, mask = bit
        if bit in self.core:
            return {"core": size / 428e3}
        near = 2 * size / 92e3
        if bit in self.line[:1] or axis == "batch":
            return {bit: near}
        return {"line": near, bit: near * (mask // 2)}

    def order(self, name):
        order = list(self.core)
        links = {"x": self.chips[0], "y": self.line[0], "z0": self.line[1], "z1": self.line[2]}
        while name:
            for key, bit in links.items():
                if name.startswith(key):
                    order.append(bit)
                    name = name[len(key) :]
        return order

    def rotated(self, k):
        links = self.chips + self.line
        k %= len(links)
        return self.core + links[k:] + links[:k]

    def hold(self, size):
        count = 1 << len(self.line)
        y = 2 * size * count / 2 / 92e3
        return {self.line[0]: y, "line": 1.5 * y, self.line[-1]: 2 * y}

    def halving(self, rows, order, base):
        down, up = [], []
        for bit in order:
            if rows % 32 == 0:
                rows //= 2
                down.append(("sum", bit, rows, rows))
                up.append(("spread", bit, rows, rows))
            else:
                down.append(("sum", bit, 0, rows))
        return {"base": base, "fixed": [], "steps": down + up[::-1], "rows": rows}

    def by_head(self, heads, hd, base):
        head_bits = self.line[: heads.bit_length() - 1]
        batch_bits = self.core + self.chips
        rest = self.line[len(head_bits) :]
        rows, parts = hd, []
        for bit in batch_bits + rest:
            if rows % 32 == 0:
                rows //= 2
                parts.append((bit, rows))
            else:
                parts.append((bit, 0))
        split = [bit for bit, size in parts if size]
        inner = split[1:]
        stride, strides = rows, {}
        for bit in inner[::-1] + head_bits + split[:1]:
            strides[bit] = stride
            stride *= 2
        down = [("sum", bit, strides.get(bit, 0), size or rows) for bit, size in parts]
        up = [("spread", bit, strides[bit], strides[bit]) for bit in strides]
        fixed = [(bit, strides[bit]) for bit in head_bits]
        return {"base": base, "fixed": fixed, "steps": down + up, "rows": rows, "strides": strides}

    def schedule(self, chains, width, segments, size):
        left = []
        for chain in chains:
            total = [0.0]
            for _, bit, _, rows in chain["steps"][::-1]:
                busy = max(self.cost(bit, 2 * rows * width).values())
                total.append(total[-1] + busy + LAG)
            left.append(total[::-1])
        free, at, plan = {}, [0] * len(chains), []
        ready = [None] * len(chains)
        now, segment, sent = 0.0, 0, {}

        def hold(name, times):
            for link, busy in self.hold(times * size).items():
                free[link] = max(free.get(link, 0.0), now) + busy
            sent[name] = max(free[link] for link in self.hold(size)) + LAG + 0.5

        hold("grad", 1)
        while True:
            best, later = None, []
            for c, chain in enumerate(chains):
                if ready[c] is None or at[c] > len(chain["steps"]):
                    continue
                if at[c] == len(chain["steps"]):
                    start = ready[c] + MARGIN
                else:
                    _, bit, _, rows = chain["steps"][at[c]]
                    cost = self.cost(bit, 2 * rows * width)
                    start = max([ready[c] + (MARGIN if at[c] else 0.0)] + [free.get(link, 0.0) - 0.3 for link in cost])
                if start <= now:
                    key = (-left[c][at[c]], c)
                    best = key if best is None or key < best else best
                else:
                    later.append(start)
            if best is not None:
                c = best[1]
                k = at[c]
                at[c] += 1
                steps = chains[c]["steps"]
                now += ISSUE
                if k and steps[k - 1][0] == "sum":
                    now += 0.4e-6 * 2 * steps[k - 1][3] * width
                if k == len(steps):
                    plan.append(("end", c, k))
                    continue
                _, bit, _, rows = steps[k]
                cost = self.cost(bit, 2 * rows * width)
                start = max([now] + [free.get(link, 0.0) for link in cost])
                for link, busy in cost.items():
                    free[link] = start + busy
                lag = CORE_LAG if bit in self.core else LAG
                ready[c] = start + max(cost.values()) + lag
                plan.append(("sum", c, k))
                continue
            if segment < len(segments):
                name, busy, releases = segments[segment]
                due = sent.get(name, 0.0)
                if due <= now:
                    plan.append(("seg", segment, name))
                    now += busy
                    for c in releases:
                        ready[c] = now
                    if name == "send":
                        hold("back", 3)
                    segment += 1
                    continue
                later.append(due)
            if not later:
                self.end = now
                return plan
            now = max(now + 0.01, min(later))


class Sums:
    def __init__(self, chains, work, landing, total, send_sems, recv_sems):
        self.chains = chains
        self.work, self.landing, self.total = work, landing, total
        self.send_sems, self.recv_sems = send_sems, recv_sems
        self.index = {"batch": lax.axis_index("batch"), "seq": lax.axis_index("seq")}
        self.open = {}
        self.offset = {}
        sem = land = 0
        self.sem, self.land = {}, {}
        for c, chain in enumerate(chains[:-1]):
            self.offset[c] = chain["base"] + sum(
                self.bit(bit) * stride for bit, stride in chain["fixed"]
            )
            for k, (phase, _, _, rows) in enumerate(chain["steps"]):
                self.sem[c, k] = sem
                sem += 1
                if phase == "sum":
                    self.land[c, k] = land
                    land += rows

    @staticmethod
    def needs(chains):
        steps = [step for chain in chains[:-1] for step in chain["steps"]]
        return len(steps), sum(step[3] for step in steps if step[0] == "sum")

    def bit(self, bit):
        axis, mask = bit
        return lax.rem(lax.div(self.index[axis], mask), 2)

    def partner(self, bit):
        axis, mask = bit
        return {axis: self.index[axis] + mask - 2 * mask * self.bit(bit)}

    def start(self, c, k):
        if k:
            self.finish(c, k - 1)
        phase, bit, stride, rows = self.chains[c]["steps"][k]
        side = self.bit(bit)
        offset = self.offset[c]
        if phase == "sum":
            other = offset + (1 - side) * stride if stride else offset
            source = self.work.at[pl.ds(pl.multiple_of(other, 16), rows)]
            target = self.landing.at[pl.ds(self.land[c, k], rows)]
            if stride:
                self.offset[c] = offset + side * stride
        else:
            here = pl.ds(pl.multiple_of(offset, 16), rows)
            source, target = self.total.at[here], self.total.at[here]
            self.offset[c] = offset - side * stride
        copy = pltpu.make_async_remote_copy(
            src_ref=source,
            dst_ref=target,
            send_sem=self.send_sems.at[c],
            recv_sem=self.recv_sems.at[self.sem[c, k]],
            device_id=self.partner(bit),
            device_id_type=MESH,
        )
        copy.start()
        self.open[c] = copy

    def finish(self, c, k):
        self.open.pop(c).wait()
        steps = self.chains[c]["steps"]
        phase, _, _, rows = steps[k]
        if phase == "sum":
            last = k + 1 == len(steps) or steps[k + 1][0] == "spread"
            held = pl.ds(pl.multiple_of(self.offset[c], 16), rows)
            landed = self.landing[self.land[c, k] : self.land[c, k] + rows, :]
            both = self.work[held, :].astype(jnp.float32) + landed.astype(jnp.float32)
            (self.total if last else self.work)[held, :] = low(both)


OPERANDS = (
    "x",
    "pool_w",
    "gain1",
    "bias1",
    "query_w",
    "key_w",
    "value_w",
    "og",
    "up_w",
    "outer_w",
    "table",
    "position_w",
    "content_bias",
    "position_bias",
    "output_w",
    "gain2",
    "bias2",
    "inner_w",
)


class Pass:
    def __init__(self, z, plan, chains, bits, names, refs):
        self.z = z
        self.__dict__.update(zip(names, refs))
        self.plan, self.chains, self.bits = plan, chains, bits
        self.me = lax.axis_index("seq")
        self.head = lax.rem(self.me, z.heads)
        self.group = lax.div(self.me, z.heads)
        self.sums = Sums(
            chains, self.work, self.landing, self.total, self.sum_send, self.sum_recv
        )
        self.at = 0
        self.loads, self.stores = {}, []

    def run(self):
        self.enter()
        self.project()
        self.attend()
        self.feed_forward()
        self.attend_back()
        self.finish_rows()
        self.finish_sums()

    def enter(self):
        z, me = self.z, self.me
        for k, name in enumerate(OPERANDS):
            self.loads[name] = pltpu.make_async_copy(
                getattr(self, name), getattr(self, name + "_v"), self.load_sems.at[k]
            )
            self.loads[name].start()
        barrier = pltpu.get_barrier_semaphore()
        batch = [bit for bit in self.bits if bit[0] == "batch"]
        for step in range(1, z.n):
            pl.semaphore_signal(
                barrier,
                inc=1,
                device_id={"seq": lax.rem(me + step, z.n)},
                device_id_type=MESH,
            )
        for bit in batch:
            pl.semaphore_signal(
                barrier, inc=1, device_id=self.sums.partner(bit), device_id_type=MESH
            )
        self.have("x")
        rows_by_three(z, self.x_v, self.xf)
        self.xf[:, :, 0:8, :] = jnp.zeros((z.items, z.width // LANES, 8, LANES), jnp.float32)
        self.have("pool_w")
        self.pooled[...] = self.pool(2)
        pl.semaphore_wait(barrier, z.n - 1 + len(batch))

    def pool(self, part):
        width = self.z.width
        return dot(
            low(every_third(self.z, self.xf, 6 + part)),
            self.pool_w_v[part * width : (part + 1) * width, :],
        )

    def have(self, *names):
        for name in names:
            if name in self.loads:
                self.loads.pop(name).wait()

    def neighbour(self, source, target, sems, step):
        copy = pltpu.make_async_remote_copy(
            src_ref=source,
            dst_ref=target,
            send_sem=sems.at[0],
            recv_sem=sems.at[1],
            device_id={"seq": lax.rem(self.me + step, self.z.n)},
            device_id_type=MESH,
        )
        copy.start()
        return copy

    def exchange(self, source, target, sems):
        return Exchange(self.z.n, self.me, source, target, sems)

    def by_head(self, target, values):
        z = self.z
        pad = [jnp.zeros((z.r, z.hd), jnp.bfloat16)] * (LANES // z.hd - z.units)
        lanes = slice(target % z.heads * z.hd, (target % z.heads + 1) * z.hd)
        sides = []
        for value in values:
            for unit in range(z.units):
                item = target // z.heads * z.units + unit
                sides.append(value[item * z.r : (item + 1) * z.r, lanes])
            sides += pad
        return jnp.concatenate(sides, axis=1)

    def to_rows(self, source_ref, which, target_ref):
        z = self.z
        for source in range(z.n):
            for unit in range(z.units):
                item = source // z.heads * z.units + unit
                head = source % z.heads
                first = which * LANES + unit * z.hd
                target_ref[item * z.r : (item + 1) * z.r, head * z.hd : (head + 1) * z.hd] = (
                    source_ref[source, :, first : first + z.hd]
                )

    def live(self, part):
        z = self.z
        rows = [live_rows(z, self.me, self.lengths[item], part) for item in range(z.items)]
        return jnp.concatenate(rows, axis=0)

    def project(self):
        z, me, r, width = self.z, self.me, self.z.r, self.z.width
        halo = self.neighbour(
            self.x_v.at[:, 3 * r - 16 :, :], self.halo, self.halo_sems, 1
        )
        pooled = self.pooled[...] + self.pool(0) + self.pool(1)
        halo.wait()
        before = jnp.where(me > 0, self.halo[...].astype(jnp.float32), 0.0)
        before = low(before.reshape(z.items * 16, width))
        parts = [dot(before, self.pool_w_v[part * width : (part + 1) * width, :]) for part in (0, 1)]
        row = lax.broadcasted_iota(jnp.int32, (z.rows, 1), 0)
        for item in range(z.items):
            at = item * 16 + 14
            extra = parts[0][at : at + 1, :] + parts[1][at + 1 : at + 2, :]
            pooled += jnp.where(row == item * r, extra, 0.0)
        self.short[...] = low(pooled)
        normed, inverse = norm_rows(self.short[...].astype(jnp.float32))
        self.normed1[...] = normed
        self.inverse1[...] = inverse
        self.have("gain1", "bias1", "query_w", "key_w", "value_w")
        self.attn_in[...] = low(normed * self.gain1_v[...] + self.bias1_v[...])
        attn_in = self.attn_in[...]
        qkv = [low(dot(attn_in, w[...])) for w in (self.query_w_v, self.key_w_v, self.value_w_v)]
        for target in range(z.n):
            self.qkv_out[target] = self.by_head(target, qkv)
        copies = self.exchange(self.qkv_out, self.qkv_in, self.qkv_sems)
        self.have("og", "up_w", "outer_w")
        rows_by_three(z, self.og_v, self.of)
        for part in range(3):
            self.up_rows[:, part * width : (part + 1) * width] = low(
                every_third(z, self.of, 8 + part) * self.live(part)
            )
        self.summed_grad[...] = low(dot_nt(self.up_rows[...], self.up_w_v[...]))
        ff = self.outer_w_v.shape[0]
        for lo in range(0, ff, width):
            self.act_grad[:, lo : lo + width] = dot_nt(
                self.summed_grad[...], self.outer_w_v[lo : lo + width, :]
            )
        self.have("table", "position_w", "content_bias", "position_bias")
        first = self.head * z.hd
        pair = pl.ds(pl.multiple_of(lax.div(first, LANES) * LANES, LANES), LANES)
        both = dot(self.table_v[...], self.position_w_v[:, pair])
        self.pos[...] = low(pltpu.roll(both, LANES - lax.rem(first, LANES), 1)[:, : z.hd])
        copies.wait()

    def attend(self):
        z, r, hd = self.z, self.z.r, self.z.hd
        content_bias = self.content_bias_v[pl.ds(self.head, 1), :]
        position_bias = self.position_bias_v[pl.ds(self.head, 1), :]
        for unit in range(z.units):
            queries, keys, values = (
                self.qkv_in[:, :, which * LANES + unit * hd : which * LANES + (unit + 1) * hd]
                .reshape(z.length, hd)
                for which in range(3)
            )
            self.qc[unit] = low(queries.astype(jnp.float32) + content_bias)
            self.qp[unit] = low(queries.astype(jnp.float32) + position_bias)
            self.keys[unit] = keys
            self.values[unit] = values
        for block in range(z.length // BLOCK):
            lo, hi = block * BLOCK, (block + 1) * BLOCK
            sides = []
            for unit in range(z.units):
                length = self.lengths[self.group * z.units + unit]
                content = dot_nt(self.qc[unit, lo:hi, :], self.keys[unit, :hi, :])
                by_distance = dot_nt(self.qp[unit, lo:hi, :], self.pos[z.length - hi :, :])
                placed = pltpu.roll(by_distance, lo + 1, 1, stride=1, stride_axis=0)
                query_at = lo + lax.broadcasted_iota(jnp.int32, (BLOCK, hi), 0)
                key_at = lax.broadcasted_iota(jnp.int32, (BLOCK, hi), 1)
                valid = (key_at <= query_at) & (3 * key_at < length)
                logits = jnp.where(valid, (content + placed) * hd**-0.5, masked_value)
                raised = jnp.exp(logits - jnp.max(logits, axis=-1, keepdims=True))
                probs = raised / jnp.sum(raised, axis=-1, keepdims=True)
                self.probs[unit, lo:hi, :hi] = probs
                sides.append(low(dot(low(probs), self.values[unit, :hi, :])))
            sides += [jnp.zeros((BLOCK, hd), jnp.bfloat16)] * (LANES // hd - z.units)
            per = BLOCK // r
            self.att_out[block * per : (block + 1) * per] = jnp.concatenate(
                sides, axis=1
            ).reshape(per, r, LANES)
        copies = self.exchange(self.att_out, self.att_in, self.att_sems)
        self.have("output_w", "gain2", "bias2", "inner_w")
        copies.wait()

    def feed_forward(self):
        z, width = self.z, self.z.width
        ff = self.outer_w_v.shape[0]
        self.to_rows(self.att_in, 0, self.att)
        hidden = self.short[...].astype(jnp.float32) + dot(self.att[...], self.output_w_v[...])
        normed, inverse = norm_rows(hidden)
        self.hidden[...] = hidden
        self.ffn_in[...] = low(normed * self.gain2_v[...] + self.bias2_v[...])
        ffn_in = self.ffn_in[...]
        ffn_grad = jnp.zeros((z.rows, width), jnp.float32)
        for lo in range(0, ff, width):
            cut = slice(lo, lo + width)
            inner = dot(ffn_in, self.inner_w_v[:, cut])
            normal_cdf = 0.5 * (1.0 + lax.erf(inner * 0.7071067811865476))
            density = jnp.exp(-0.5 * inner * inner) * 0.3989422804014327
            self.act[:, cut] = low(inner * normal_cdf)
            inner_grad = low(self.act_grad[:, cut] * (normal_cdf + inner * density))
            self.inner_grad[:, cut] = inner_grad
            ffn_grad += dot_nt(inner_grad, self.inner_w_v[:, cut])
        self.small_work[0, 2:3, :] = jnp.sum(ffn_grad * normed, axis=0, keepdims=True)
        self.small_work[0, 3:4, :] = jnp.sum(ffn_grad, axis=0, keepdims=True)
        hidden_grad = self.summed_grad[...].astype(jnp.float32) + norm_backward(
            ffn_grad, normed, inverse, self.gain2_v[...]
        )
        self.hidden_grad[...] = hidden_grad
        self.branch[...] = low(hidden_grad)
        att_grad = low(dot_nt(self.branch[...], self.output_w_v[...]))
        for target in range(z.n):
            self.grad_out[target] = self.by_head(target, [att_grad])
        self.copies = self.exchange(self.grad_out, self.grad_in, self.grad_sems)
        row = 0
        for lo in range(0, ff, width):
            self.reach("unit")
            self.work[row : row + width, :] = low(
                dot_tn(self.act[:, lo : lo + width], self.summed_grad[...])
            )
            row += width
        for lo in range(0, ff, width):
            self.reach("unit")
            self.work[row : row + width, :] = low(
                dot_tn(self.ffn_in[...], self.inner_grad[:, lo : lo + width])
            )
            row += width
        self.reach("unit")
        self.work[row : row + width, :] = low(dot_tn(self.att[...], self.branch[...]))
        row += width
        self.summed[...] = low(self.hidden[...] + dot(self.act[...], self.outer_w_v[...]))
        for lo in range(0, 3 * width, width):
            self.reach("unit")
            self.work[row : row + width, :] = low(
                dot_tn(self.summed[...], self.up_rows[:, lo : lo + width])
            )
            row += width
        self.row = row
        self.reach("grad")
        self.copies.wait()

    def upsample(self):
        z, width = self.z, self.z.width
        for part in range(3):
            up = dot(self.summed[...], self.up_w_v[:, part * width : (part + 1) * width])
            set_every_third(
                z, self.bf, 8 + part, every_third(z, self.xf, 8 + part) + up * self.live(part)
            )
        for item in range(z.items):
            for slab in range(width // LANES):
                self.block_low[item, :, slab * LANES : (slab + 1) * LANES] = low(
                    self.bf[item, slab, 8:, :]
                )
        self.block_store = pltpu.make_async_copy(
            self.block_low, self.block_out, self.out_sems.at[0]
        )
        self.block_store.start()

    def attend_back(self):
        z, r, hd, length = self.z, self.z.r, self.z.hd, self.z.length
        flip = reversal()
        content_sum = jnp.zeros((1, hd), jnp.float32)
        position_sum = jnp.zeros((1, hd), jnp.float32)
        self.key_t[...] = jnp.zeros_like(self.key_t)
        self.value_t[...] = jnp.zeros_like(self.value_t)
        self.table_t[...] = jnp.zeros_like(self.table_t)
        for unit in range(z.units):
            att_grad = self.grad_in[:, :, unit * hd : (unit + 1) * hd].reshape(length, hd)
            for block in range(length // BLOCK):
                self.reach("block")
                lo, hi = block * BLOCK, (block + 1) * BLOCK
                block_grad = att_grad[lo:hi]
                probs = self.probs[unit, lo:hi, :hi]
                prob_grad = dot_nt(block_grad, self.values[unit, :hi, :])
                delta = jnp.sum(probs * prob_grad, axis=-1, keepdims=True)
                raw = low(probs * (prob_grad - delta) * hd**-0.5)
                content = dot(raw, self.keys[unit, :hi, :])
                self.key_t[unit, :, :hi] += dot_tn(self.qc[unit, lo:hi, :], raw)
                self.value_t[unit, :, :hi] += dot_tn(block_grad, low(probs))
                by_distance = low(pltpu.roll(dot(flip, raw), 0, 1, stride=1, stride_axis=0))
                position = dot(by_distance, self.pos[length - hi :, :])
                upper = low(position)
                lower = low(position - upper.astype(jnp.float32))
                position = dot(flip, upper) + dot(flip, lower)
                flipped_q = low(dot(flip, self.qp[unit, lo:hi, :]))
                self.table_t[unit, :, length - hi :] += dot_tn(flipped_q, by_distance)
                content_sum += jnp.sum(content, axis=0, keepdims=True)
                position_sum += jnp.sum(position, axis=0, keepdims=True)
                self.query_grad[unit, lo:hi, :] = low(content + position)
        self.reach("send")
        own = lax.broadcasted_iota(jnp.int32, (1, z.width), 1) // hd == self.head
        for row, value in ((4, content_sum), (5, position_sum)):
            spread = jnp.concatenate([value] * z.heads, axis=1)
            self.small_work[0, row : row + 1, :] = jnp.where(own, spread, 0.0)
        pad = [jnp.zeros((length, hd), jnp.bfloat16)] * (LANES // hd - z.units)
        sides = [self.query_grad[unit] for unit in range(z.units)] + pad
        sides += [low(self.key_t[unit].T) for unit in range(z.units)] + pad
        sides += [low(self.value_t[unit].T) for unit in range(z.units)] + pad
        self.back_out[...] = jnp.concatenate(sides, axis=1).reshape(z.n, r, 3 * LANES)
        copies = self.exchange(self.back_out, self.back_in, self.back_sems)
        self.reach("table")
        table_sum = 0.0
        for unit in range(z.units):
            table_sum += dot(low(self.table_t[unit]), self.table_v[...])
        half = hd // 2
        base = self.chains[-2]["base"]
        for side in range(2):
            at = pl.multiple_of(base + side * z.heads * half + self.head * half, 16)
            self.work[pl.ds(at, half), :] = low(table_sum[side * half : (side + 1) * half])
        self.reach("up")
        self.upsample()
        self.reach("back")
        copies.wait()

    def finish_rows(self):
        z, me, r, width = self.z, self.me, self.z.r, self.z.width
        self.reach("rows")
        for which in range(3):
            self.to_rows(self.back_in, which, self.row_grad.at[which])
        attn_grad = (
            dot_nt(self.row_grad[0], self.query_w_v[...])
            + dot_nt(self.row_grad[1], self.key_w_v[...])
            + dot_nt(self.row_grad[2], self.value_w_v[...])
        )
        normed = self.normed1[...]
        self.small_work[0, 0:1, :] = jnp.sum(attn_grad * normed, axis=0, keepdims=True)
        self.small_work[0, 1:2, :] = jnp.sum(attn_grad, axis=0, keepdims=True)
        self.small_work[0, 6:8, :] = jnp.zeros((2, width), jnp.float32)
        short_grad = low(
            self.hidden_grad[...]
            + norm_backward(attn_grad, normed, self.inverse1[...], self.gain1_v[...])
        )
        for item in range(z.items):
            self.first_rows[item] = short_grad[item * r : item * r + 16, :]
            self.later[item, 0:r, :] = short_grad[item * r : (item + 1) * r, :].astype(jnp.float32)
        halo = self.neighbour(self.first_rows, self.next_rows, self.next_sems, z.n - 1)
        row = self.row
        self.reach("qkv")
        for which in range(3):
            self.work[row : row + width, :] = low(dot_tn(self.attn_in[...], self.row_grad[which]))
            row += width
        self.reach("pool")
        own = dot_nt(short_grad, self.pool_w_v[2 * width :, :])
        set_every_third(z, self.of, 8, every_third(z, self.of, 8) + own)
        self.work[row + 2 * width : row + 3 * width, :] = low(
            dot_tn(low(every_third(z, self.xf, 8)), short_grad)
        )
        halo.wait()
        for item in range(z.items):
            after = jnp.where(me < z.n - 1, self.next_rows[item].astype(jnp.float32), 0.0)
            self.later[item, r : r + 8, :] = after[0:8, :]
        later = low(
            jnp.concatenate([self.later[item, 1 : r + 1, :] for item in range(z.items)], axis=0)
        )
        for part in range(2):
            cut = slice(row + part * width, row + (part + 1) * width)
            self.work[cut, :] = low(dot_tn(low(every_third(z, self.xf, 9 + part)), later))
        self.reach("input")
        for part in range(2):
            back = dot_nt(later, self.pool_w_v[part * width : (part + 1) * width, :])
            first = 9 + part
            set_every_third(z, self.of, first, every_third(z, self.of, first) + back)
        for item in range(z.items):
            for slab in range(width // LANES):
                self.input_rows[item, :, slab * LANES : (slab + 1) * LANES] = self.of[
                    item, slab, 8:, :
                ]
        self.input_store = pltpu.make_async_copy(
            self.input_rows, self.input_grad, self.out_sems.at[1]
        )
        self.input_store.start()

    def reach(self, name=None):
        while self.at < len(self.plan):
            kind, c, k = self.plan[self.at]
            self.at += 1
            if kind == "seg":
                assert k == name
                return
            if c == len(self.chains) - 1:
                self.small(k)
            elif kind == "sum":
                self.sums.start(c, k)
            else:
                self.sums.finish(c, k - 1)
                at, size = self.chains[c]["base"], self.chains[c]["all"]
                self.stores.append(
                    pltpu.make_async_copy(
                        self.total.at[at : at + size],
                        self.total_out.at[at : at + size],
                        self.store_sems.at[c],
                    )
                )
                self.stores[-1].start()

    def small(self, k):
        if k:
            self.small_copy.wait()
            self.small_work[k] = self.small_work[k - 1] + self.small_landing[k - 1]
        if k < len(self.bits):
            self.small_start(k)
        else:
            self.small_total[...] = self.small_work[k]

    def small_start(self, k):
        self.small_copy = pltpu.make_async_remote_copy(
            src_ref=self.small_work.at[k],
            dst_ref=self.small_landing.at[k],
            send_sem=self.small_send.at[k],
            recv_sem=self.small_recv.at[k],
            device_id=self.sums.partner(self.bits[k]),
            device_id_type=MESH,
        )
        self.small_copy.start()

    def finish_sums(self):
        self.reach()
        for store in self.stores + [self.block_store, self.input_store]:
            store.wait()


def block_kernel(z, plan, chains, bits, names, *refs):
    Pass(z, plan, chains, bits, names, refs).run()


def chains_of(z, ff, nb):
    width = z.width
    copies = Copies(nb, z.n)
    early = 2 * ff // width + 4
    units = early + 6
    searched = len(copies.bits) == 5 and sum(rows for rows, _ in CHAINS) == units
    chosen = CHAINS if searched else [(1, k) for k in range(units)]
    chains, base = [], 0
    for rows, name in chosen:
        order = copies.order(name) if searched else copies.rotated(name)
        chains.append(copies.halving(rows * width, order, base * width))
        chains[-1]["all"] = rows * width
        base += rows
        chains[-1]["units"] = base
    chains.append(copies.by_head(z.heads, z.hd, base * width))
    chains[-1]["all"] = z.heads * z.hd
    chains.append({"steps": [("small", bit, 0, 16) for bit in copies.bits]})
    blocks = z.units * z.length // BLOCK

    def done(first, last):
        return [c for c, chain in enumerate(chains) if first < chain.get("units", 0) <= last]

    segments = [("unit", UNIT, done(unit, unit + 1)) for unit in range(early)]
    segments += [("grad", 0.0, [])] + [("block", BLOCK_STEP, [])] * blocks
    segments += [("send", SEND, []), ("table", TABLE, [len(chains) - 2]), ("up", UP, [])]
    segments += [("back", 0.0, []), ("rows", ROWS, [len(chains) - 1])]
    segments += [("qkv", QKV, done(early, early + 3)), ("pool", POOL, done(early + 3, units))]
    segments += [("input", INPUT, [])]
    return copies, chains, segments


def result_kernel(
    z,
    ff,
    total_ref,
    small_ref,
    block_in_ref,
    input_in_ref,
    block_ref,
    input_ref,
    pool_ref,
    gain1_ref,
    bias1_ref,
    query_ref,
    key_ref,
    value_ref,
    position_ref,
    content_bias_ref,
    position_bias_ref,
    output_ref,
    gain2_ref,
    bias2_ref,
    inner_ref,
    outer_ref,
    up_ref,
    held,
    wide,
    block_held,
    input_held,
    load_sems,
    store_sems,
    pass_sems,
):
    width = z.width
    through = [
        pltpu.make_async_copy(block_in_ref, block_held, pass_sems.at[0]),
        pltpu.make_async_copy(input_in_ref, input_held, pass_sems.at[1]),
    ]
    blocks = held.shape[0]
    loads = [
        pltpu.make_async_copy(
            total_ref.at[k * width : (k + 1) * width], held.at[k], load_sems.at[k]
        )
        for k in range(blocks)
    ]
    for copy in through + loads:
        copy.start()
    places = [outer_ref.at[k * width : (k + 1) * width] for k in range(ff // width)]
    places += [inner_ref.at[:, k * width : (k + 1) * width] for k in range(ff // width)]
    places += [output_ref]
    places += [up_ref.at[:, k * width : (k + 1) * width] for k in range(3)]
    places += [query_ref, key_ref, value_ref]
    places += [pool_ref.at[k * width : (k + 1) * width] for k in range(3)]
    places += [position_ref]
    gain1_ref[...] = small_ref[0:1, :]
    bias1_ref[...] = small_ref[1:2, :]
    gain2_ref[...] = small_ref[2:3, :]
    bias2_ref[...] = small_ref[3:4, :]
    for head in range(z.heads):
        lanes = slice(head * z.hd, (head + 1) * z.hd)
        content_bias_ref[head : head + 1, :] = small_ref[4:5, lanes]
        position_bias_ref[head : head + 1, :] = small_ref[5:6, lanes]
    stores = []
    for which, (source, target) in enumerate(
        ((block_held, block_ref), (input_held, input_ref))
    ):
        through[which].wait()
        stores.append(pltpu.make_async_copy(source, target, pass_sems.at[2 + which]))
        stores[-1].start()
    for k in range(blocks):
        loads[k].wait()
        if k + 1 < blocks:
            wide[k] = held[k].astype(jnp.float32)
        else:
            half = z.hd // 2
            for head in range(z.heads):
                rows = [
                    held[k, side * z.heads * half + head * half :][:half] for side in range(2)
                ]
                both = jnp.concatenate(rows, axis=0).astype(jnp.float32)
                wide[k, :, head * z.hd : (head + 1) * z.hd] = both.T
        stores.append(pltpu.make_async_copy(wide.at[k], places[k], store_sems.at[k]))
        stores[-1].start()
    for copy in stores:
        copy.wait()


def body(
    byte_rows,
    item_lengths,
    out_grad,
    pool_weight,
    norm1_gain,
    norm1_bias,
    query_weight,
    key_weight,
    value_weight,
    position_weight,
    content_bias,
    position_bias,
    output_weight,
    norm2_gain,
    norm2_bias,
    inner_weight,
    outer_weight,
    upsample_weight,
):
    items, full_rows, width = byte_rows.shape
    heads, hd = content_bias.shape
    n = lax.axis_size("seq")
    ff = inner_weight.shape[1]
    z = Sizes(n, items, full_rows, width, heads)
    r, units, length, rows = z.r, z.units, z.length, z.rows
    bf, f4 = jnp.bfloat16, jnp.float32
    slabs = width // LANES
    dma = pltpu.SemaphoreType.DMA
    copies, chains, segments = chains_of(z, ff, lax.axis_size("batch"))
    plan = copies.schedule(chains, width, segments, r * LANES * 2)
    bits = copies.bits
    count, landing = Sums.needs(chains)
    total_rows = chains[-2]["base"] + chains[-2]["all"]
    operands = {
        "x": byte_rows,
        "pool_w": pool_weight,
        "gain1": norm1_gain.reshape(1, width),
        "bias1": norm1_bias.reshape(1, width),
        "query_w": query_weight,
        "key_w": key_weight,
        "value_w": value_weight,
        "og": out_grad,
        "up_w": upsample_weight,
        "outer_w": outer_weight,
        "table": distance_table(length, width),
        "position_w": position_weight,
        "content_bias": content_bias,
        "position_bias": position_bias,
        "output_w": output_weight,
        "gain2": norm2_gain.reshape(1, width),
        "bias2": norm2_bias.reshape(1, width),
        "inner_w": inner_weight,
    }
    outs = {
        "block_out": (byte_rows.shape, bf, ANY),
        "input_grad": (byte_rows.shape, f4, ANY),
        "total_out": ((total_rows, width), bf, ANY),
        "small_total": ((8, width), f4, VMEM),
    }
    slab_rows = pltpu.VMEM((items, slabs, 3 * r + 8, LANES), f4)
    scratch = {name + "_v": pltpu.VMEM(operands[name].shape, operands[name].dtype) for name in OPERANDS}
    scratch.update(
        xf=slab_rows,
        of=slab_rows,
        bf=slab_rows,
        block_low=pltpu.VMEM(byte_rows.shape, bf),
        input_rows=pltpu.VMEM(byte_rows.shape, f4),
        halo=pltpu.VMEM((items, 16, width), bf),
        first_rows=pltpu.VMEM((items, 16, width), bf),
        next_rows=pltpu.VMEM((items, 16, width), bf),
        later=pltpu.VMEM((items, r + 8, width), f4),
        pooled=pltpu.VMEM((rows, width), f4),
        short=pltpu.VMEM((rows, width), bf),
        normed1=pltpu.VMEM((rows, width), f4),
        inverse1=pltpu.VMEM((rows, 1), f4),
        attn_in=pltpu.VMEM((rows, width), bf),
        qkv_out=pltpu.VMEM((n, r, 3 * LANES), bf),
        qkv_in=pltpu.VMEM((n, r, 3 * LANES), bf),
        att_out=pltpu.VMEM((n, r, LANES), bf),
        att_in=pltpu.VMEM((n, r, LANES), bf),
        grad_out=pltpu.VMEM((n, r, LANES), bf),
        grad_in=pltpu.VMEM((n, r, LANES), bf),
        back_out=pltpu.VMEM((n, r, 3 * LANES), bf),
        back_in=pltpu.VMEM((n, r, 3 * LANES), bf),
        qc=pltpu.VMEM((units, length, hd), bf),
        qp=pltpu.VMEM((units, length, hd), bf),
        keys=pltpu.VMEM((units, length, hd), bf),
        values=pltpu.VMEM((units, length, hd), bf),
        pos=pltpu.VMEM((length, hd), bf),
        probs=pltpu.VMEM((units, length, length), f4),
        query_grad=pltpu.VMEM((units, length, hd), bf),
        key_t=pltpu.VMEM((units, hd, length), f4),
        value_t=pltpu.VMEM((units, hd, length), f4),
        table_t=pltpu.VMEM((units, hd, length), f4),
        att=pltpu.VMEM((rows, width), bf),
        hidden=pltpu.VMEM((rows, width), f4),
        ffn_in=pltpu.VMEM((rows, width), bf),
        act=pltpu.VMEM((rows, ff), bf),
        act_grad=pltpu.VMEM((rows, ff), f4),
        inner_grad=pltpu.VMEM((rows, ff), bf),
        up_rows=pltpu.VMEM((rows, 3 * width), bf),
        summed=pltpu.VMEM((rows, width), bf),
        summed_grad=pltpu.VMEM((rows, width), bf),
        hidden_grad=pltpu.VMEM((rows, width), f4),
        branch=pltpu.VMEM((rows, width), bf),
        row_grad=pltpu.VMEM((3, rows, width), bf),
        work=pltpu.VMEM((total_rows, width), bf),
        landing=pltpu.VMEM((landing, width), bf),
        total=pltpu.VMEM((total_rows, width), bf),
        small_work=pltpu.VMEM((len(bits) + 1, 8, width), f4),
        small_landing=pltpu.VMEM((len(bits), 8, width), f4),
        load_sems=dma((len(OPERANDS),)),
        halo_sems=dma((2,)),
        next_sems=dma((2,)),
        qkv_sems=dma((2,)),
        att_sems=dma((2,)),
        grad_sems=dma((2,)),
        back_sems=dma((2,)),
        sum_send=dma((len(chains) - 1,)),
        sum_recv=dma((count,)),
        small_send=dma((len(bits),)),
        small_recv=dma((len(bits),)),
        store_sems=dma((len(chains) - 1,)),
        out_sems=dma((2,)),
    )
    names = ("lengths",) + OPERANDS + tuple(outs) + tuple(scratch)
    block_out, input_grad, total, small_t = pl.pallas_call(
        functools.partial(block_kernel, z, plan, chains, bits, names),
        out_shape=[jax.ShapeDtypeStruct(shape, dtype) for shape, dtype, _ in outs.values()],
        in_specs=[SMEM] + [ANY] * len(OPERANDS),
        out_specs=[space for _, _, space in outs.values()],
        scratch_shapes=list(scratch.values()),
        compiler_params=pltpu.CompilerParams(
            collective_id=0, has_side_effects=True, vmem_limit_bytes=60 * 2**20
        ),
    )(item_lengths, *(operands[name] for name in OPERANDS))
    blocks = total.shape[0] // width
    shapes = [
        ((items, full_rows, width), bf, ANY),
        ((items, full_rows, width), f4, ANY),
        ((3 * width, width), f4, ANY),
        ((1, width), f4, VMEM),
        ((1, width), f4, VMEM),
        ((width, width), f4, ANY),
        ((width, width), f4, ANY),
        ((width, width), f4, ANY),
        ((width, width), f4, ANY),
        ((heads, hd), f4, VMEM),
        ((heads, hd), f4, VMEM),
        ((width, width), f4, ANY),
        ((1, width), f4, VMEM),
        ((1, width), f4, VMEM),
        ((width, ff), f4, ANY),
        ((ff, width), f4, ANY),
        ((width, 3 * width), f4, ANY),
    ]
    results = pl.pallas_call(
        functools.partial(result_kernel, z, ff),
        out_shape=[jax.ShapeDtypeStruct(shape, dtype) for shape, dtype, _ in shapes],
        in_specs=[ANY, VMEM, ANY, ANY],
        out_specs=[space for _, _, space in shapes],
        scratch_shapes=[
            pltpu.VMEM((blocks, width, width), bf),
            pltpu.VMEM((blocks, width, width), f4),
            pltpu.VMEM(byte_rows.shape, bf),
            pltpu.VMEM(byte_rows.shape, f4),
            dma((blocks,)),
            dma((blocks,)),
            dma((4,)),
        ],
        compiler_params=pltpu.CompilerParams(vmem_limit_bytes=62 * 2**20),
    )(total, small_t, block_out, input_grad)
    return tuple(
        value.reshape(width) if value.shape == (1, width) else value for value in results
    )


def solution(mesh):
    split = P("batch", "seq", None)
    in_specs = (split, P("batch"), split) + (P(),) * 15
    out_specs = (split, split) + (P(),) * 15
    return jax.shard_map(body, mesh=mesh, in_specs=in_specs, out_specs=out_specs, check_vma=False)
```

```python
import functools

import jax
import jax.numpy as jnp
import numpy as np
from jax import lax
from jax.experimental import pallas as pl
from jax.experimental.pallas import tpu as pltpu
from jax.sharding import PartitionSpec as P

MESH = pl.DeviceIdType.MESH
epsilon = 1e-05
masked_value = -1e30
CHAINS = (
    (1, "yxz0z1", -1),
    (2, "z0yz1x", -4),
    (1, "xyz0z1", 13),
    (1, "xyz0z1", 2),
    (2, "yxz0z1", 20),
    (1, "xz0yz1", 1),
    (1, "xyz1z0", 6),
    (1, "z0yxz1", 1),
    (2, "xyz0z1", 4),
    (1, "yxz0z1", 1),
    (1, "xz0yz1", 11),
    (1, "yxz0z1", -3),
    (1, "xyz1z0", -2),
    (1, "yxz0z1", 5),
    (1, "xyz0z1", -5),
)
LAG, CORE_LAG, ISSUE, MARGIN = 2.6, 1.0, 0.15, 0.1
UNIT, BLOCK_STEP, SEND, TABLE, UP, ROWS, QKV, POOL, INPUT = 0.33, 0.7, 0.3, 0.4, 1.5, 2.2, 0.9, 1.6, 1.2
BLOCK = 128
LANES = 128
VMEM = pl.BlockSpec(memory_space=pltpu.VMEM)
SMEM = pl.BlockSpec(memory_space=pltpu.SMEM)
ANY = pl.BlockSpec(memory_space=pl.ANY)


def dot(left, right):
    return jnp.dot(left, right, preferred_element_type=jnp.float32)


def dot_nt(left, right):
    return lax.dot_general(
        left, right, (((1,), (1,)), ((), ())), preferred_element_type=jnp.float32
    )


def dot_tn(left, right):
    return lax.dot_general(
        left, right, (((0,), (0,)), ((), ())), preferred_element_type=jnp.float32
    )


def low(value):
    return value.astype(jnp.bfloat16)


def distance_table(short_len, width):
    distance = (short_len - 1 - np.arange(short_len)).astype(np.float32)
    steps_in = np.arange(0, width, 2).astype(np.float32)
    frequency = np.exp(-np.log(np.float32(10000.0)) * steps_in / np.float32(width))
    angles = distance[:, None] * frequency[None, :].astype(np.float32)
    both = np.concatenate([np.sin(angles), np.cos(angles)], axis=1)
    return jnp.asarray(both.astype(jnp.bfloat16))


def norm_rows(rows):
    mean = jnp.mean(rows, axis=-1, keepdims=True)
    centered = rows - mean
    inverse = lax.rsqrt(jnp.mean(centered * centered, axis=-1, keepdims=True) + epsilon)
    return centered * inverse, inverse


def norm_backward(gradient, normed, inverse, gain):
    scaled = gradient * gain
    return inverse * (
        scaled
        - jnp.mean(scaled, axis=-1, keepdims=True)
        - normed * jnp.mean(scaled * normed, axis=-1, keepdims=True)
    )


class Sizes:
    def __init__(self, n, items, full_rows, width, heads):
        self.n = n
        self.items = items
        self.r = full_rows // 3
        self.width = width
        self.heads = heads
        self.hd = width // heads
        self.units = items * heads // n
        self.length = n * self.r
        self.rows = items * self.r
        assert n % heads == 0 and self.units * self.hd <= LANES


class Exchange:
    def __init__(self, n, me, source, target, sems):
        target[me] = source[me]
        for step in range(1, n):
            peer = lax.rem(me + step, n)
            pltpu.make_async_remote_copy(
                src_ref=source.at[peer],
                dst_ref=target.at[me],
                send_sem=sems.at[0],
                recv_sem=sems.at[1],
                device_id={"seq": peer},
                device_id_type=MESH,
            ).start()
        self.all = pltpu.make_async_remote_copy(
            src_ref=source.at[1:],
            dst_ref=target.at[1:],
            send_sem=sems.at[0],
            recv_sem=sems.at[1],
            device_id={"seq": lax.rem(me + 1, n)},
            device_id_type=MESH,
        )

    def wait(self):
        self.all.wait()


def rows_by_three(z, x_ref, xf_ref):
    for item in range(z.items):
        for slab in range(z.width // LANES):
            xf_ref[item, slab, 8:, :] = x_ref[item, :, slab * LANES : (slab + 1) * LANES].astype(
                jnp.float32
            )


def every_third(z, xf_ref, first):
    items = []
    for item in range(z.items):
        slabs = [
            xf_ref[item, slab, pl.ds(first, z.r, stride=3), :] for slab in range(z.width // LANES)
        ]
        items.append(jnp.concatenate(slabs, axis=1))
    return jnp.concatenate(items, axis=0)


def set_every_third(z, xf_ref, first, value):
    for item in range(z.items):
        for slab in range(z.width // LANES):
            xf_ref[item, slab, pl.ds(first, z.r, stride=3), :] = value[
                item * z.r : (item + 1) * z.r, slab * LANES : (slab + 1) * LANES
            ]


def fold(value):
    half = value.shape[-2] // 2
    return jnp.concatenate([value[..., :half, :], value[..., half:, :]], axis=-1)


def unfold(value):
    half = value.shape[-1] // 2
    return jnp.concatenate([value[..., :half], value[..., half:]], axis=-2)


def live_rows(z, me, length, part):
    at = lax.broadcasted_iota(jnp.int32, (z.r, 1), 0) * 3 + part + me * 3 * z.r
    return (at < length).astype(jnp.float32)


def reversal():
    at = lax.broadcasted_iota(jnp.int32, (BLOCK, BLOCK), 0)
    across = lax.broadcasted_iota(jnp.int32, (BLOCK, BLOCK), 1)
    return low((at + across == BLOCK - 1).astype(jnp.float32))


class Copies:
    def __init__(self, batch_size, seq_size):
        self.core = [("batch", 1)]
        self.chips = [("batch", 1 << k) for k in range(1, batch_size.bit_length() - 1)]
        self.line = [("seq", 1 << k) for k in range(seq_size.bit_length() - 1)]
        self.bits = self.core + self.chips + self.line

    def cost(self, bit, size):
        axis, mask = bit
        if bit in self.core:
            return {"core": size / 428e3}
        near = 2 * size / 92e3
        if bit in self.line[:1] or axis == "batch":
            return {bit: near}
        return {"line": near, bit: near * (mask // 2)}

    def order(self, name):
        order = list(self.core)
        links = {"x": self.chips[0], "y": self.line[0], "z0": self.line[1], "z1": self.line[2]}
        while name:
            for key, bit in links.items():
                if name.startswith(key):
                    order.append(bit)
                    name = name[len(key) :]
        return order

    def rotated(self, k):
        links = self.chips + self.line
        k %= len(links)
        return self.core + links[k:] + links[:k]

    def hold(self, size):
        count = 1 << len(self.line)
        y = 2 * size * count / 2 / 92e3
        return {self.line[0]: y, "line": 1.5 * y, self.line[-1]: 2 * y}

    def halving(self, rows, order, base):
        down, up = [], []
        for bit in order:
            if rows % 32 == 0:
                rows //= 2
                down.append(("sum", bit, rows, rows))
                up.append(("spread", bit, rows, rows))
            else:
                down.append(("sum", bit, 0, rows))
        return {"base": base, "fixed": [], "steps": down + up[::-1], "rows": rows}

    def by_head(self, heads, hd, base):
        head_bits = self.line[: heads.bit_length() - 1]
        batch_bits = self.core + self.chips
        rest = self.line[len(head_bits) :]
        rows, parts = hd, []
        for bit in batch_bits + rest:
            if rows % 32 == 0:
                rows //= 2
                parts.append((bit, rows))
            else:
                parts.append((bit, 0))
        split = [bit for bit, size in parts if size]
        inner = split[1:]
        stride, strides = rows, {}
        for bit in inner[::-1] + head_bits + split[:1]:
            strides[bit] = stride
            stride *= 2
        down = [("sum", bit, strides.get(bit, 0), size or rows) for bit, size in parts]
        up = [("spread", bit, strides[bit], strides[bit]) for bit in strides]
        fixed = [(bit, strides[bit]) for bit in head_bits]
        return {"base": base, "fixed": fixed, "steps": down + up, "rows": rows, "strides": strides}

    def schedule(self, chains, width, segments, size):
        left = []
        for chain in chains:
            total = [0.0]
            for _, bit, _, rows in chain["steps"][::-1]:
                busy = max(self.cost(bit, 2 * rows * width).values())
                total.append(total[-1] + busy + LAG)
            left.append(total[::-1])
        free, at, plan = {}, [0] * len(chains), []
        ready = [None] * len(chains)
        now, segment, sent = 0.0, 0, {}

        def hold(name, times):
            for link, busy in self.hold(times * size).items():
                free[link] = max(free.get(link, 0.0), now) + busy
            sent[name] = max(free[link] for link in self.hold(size)) + LAG + 0.5

        sends = sum(name == "send" for name, _, _ in segments)
        hold("grad", 1)
        while True:
            best, later = None, []
            for c, chain in enumerate(chains):
                if ready[c] is None or at[c] > len(chain["steps"]):
                    continue
                if at[c] == len(chain["steps"]):
                    start = ready[c] + MARGIN
                else:
                    _, bit, _, rows = chain["steps"][at[c]]
                    cost = self.cost(bit, 2 * rows * width)
                    start = max([ready[c] + (MARGIN if at[c] else 0.0)] + [free.get(link, 0.0) - 0.3 for link in cost])
                if start <= now:
                    key = (-left[c][at[c]] - chain.get("bias", 0), c)
                    best = key if best is None or key < best else best
                else:
                    later.append(start)
            if best is not None:
                c = best[1]
                k = at[c]
                at[c] += 1
                steps = chains[c]["steps"]
                now += ISSUE
                if k and steps[k - 1][0] == "sum":
                    now += 0.4e-6 * 2 * steps[k - 1][3] * width
                if k == len(steps):
                    plan.append(("end", c, k))
                    continue
                _, bit, _, rows = steps[k]
                cost = self.cost(bit, 2 * rows * width)
                start = max([now] + [free.get(link, 0.0) for link in cost])
                for link, busy in cost.items():
                    free[link] = start + busy
                lag = CORE_LAG if bit in self.core else LAG
                ready[c] = start + max(cost.values()) + lag
                plan.append(("sum", c, k))
                continue
            if segment < len(segments):
                name, busy, releases = segments[segment]
                due = sent.get(name, 0.0)
                if due <= now:
                    plan.append(("seg", segment, name))
                    now += busy
                    for c in releases:
                        ready[c] = now
                    if name == "send":
                        hold("back", 3 / sends)
                    segment += 1
                    continue
                later.append(due)
            if not later:
                self.end = now
                return plan
            now = max(now + 0.01, min(later))


class Sums:
    def __init__(self, chains, work, landing, total, send_sems, recv_sems):
        self.chains = chains
        self.work, self.landing, self.total = work, landing, total
        self.send_sems, self.recv_sems = send_sems, recv_sems
        self.index = {"batch": lax.axis_index("batch"), "seq": lax.axis_index("seq")}
        self.open = {}
        self.offset = {}
        sem = land = 0
        self.sem, self.land = {}, {}
        for c, chain in enumerate(chains[:-1]):
            self.offset[c] = chain["base"] + sum(
                self.bit(bit) * stride for bit, stride in chain["fixed"]
            )
            for k, (phase, _, _, rows) in enumerate(chain["steps"]):
                self.sem[c, k] = sem
                sem += 1
                if phase == "sum":
                    self.land[c, k] = land
                    land += rows

    @staticmethod
    def needs(chains):
        steps = [step for chain in chains[:-1] for step in chain["steps"]]
        return len(steps), sum(step[3] for step in steps if step[0] == "sum")

    def bit(self, bit):
        axis, mask = bit
        return lax.rem(lax.div(self.index[axis], mask), 2)

    def partner(self, bit):
        axis, mask = bit
        return {axis: self.index[axis] + mask - 2 * mask * self.bit(bit)}

    def start(self, c, k):
        if k:
            self.finish(c, k - 1)
        phase, bit, stride, rows = self.chains[c]["steps"][k]
        side = self.bit(bit)
        offset = self.offset[c]
        if phase == "sum":
            other = offset + (1 - side) * stride if stride else offset
            source = self.work.at[pl.ds(pl.multiple_of(other, 16), rows)]
            target = self.landing.at[pl.ds(self.land[c, k], rows)]
            if stride:
                self.offset[c] = offset + side * stride
        else:
            here = pl.ds(pl.multiple_of(offset, 16), rows)
            source, target = self.total.at[here], self.total.at[here]
            self.offset[c] = offset - side * stride
        copy = pltpu.make_async_remote_copy(
            src_ref=source,
            dst_ref=target,
            send_sem=self.send_sems.at[c],
            recv_sem=self.recv_sems.at[self.sem[c, k]],
            device_id=self.partner(bit),
            device_id_type=MESH,
        )
        copy.start()
        self.open[c] = copy

    def finish(self, c, k):
        self.open.pop(c).wait()
        steps = self.chains[c]["steps"]
        phase, _, _, rows = steps[k]
        if phase == "sum":
            last = k + 1 == len(steps) or steps[k + 1][0] == "spread"
            held = pl.ds(pl.multiple_of(self.offset[c], 16), rows)
            landed = self.landing[self.land[c, k] : self.land[c, k] + rows, :]
            both = self.work[held, :].astype(jnp.float32) + landed.astype(jnp.float32)
            (self.total if last else self.work)[held, :] = low(both)


OPERANDS = (
    "x",
    "pool_w",
    "gain1",
    "bias1",
    "query_w",
    "key_w",
    "value_w",
    "og",
    "up_w",
    "outer_w",
    "table",
    "position_w",
    "content_bias",
    "position_bias",
    "output_w",
    "gain2",
    "bias2",
    "inner_w",
)


class Pass:
    def __init__(self, z, plan, chains, bits, names, refs):
        self.z = z
        self.__dict__.update(zip(names, refs))
        self.plan, self.chains, self.bits = plan, chains, bits
        self.me = lax.axis_index("seq")
        self.head = lax.rem(self.me, z.heads)
        self.group = lax.div(self.me, z.heads)
        self.sums = Sums(
            chains, self.work, self.landing, self.total, self.sum_send, self.sum_recv
        )
        self.at = 0
        self.loads = {}

    def run(self):
        self.enter()
        self.project()
        self.attend()
        self.feed_forward()
        self.attend_back()
        self.finish_rows()
        self.finish_sums()

    def enter(self):
        z, me = self.z, self.me
        for k, name in enumerate(OPERANDS):
            self.loads[name] = pltpu.make_async_copy(
                getattr(self, name), getattr(self, name + "_v"), self.load_sems.at[k]
            )
            self.loads[name].start()
        barrier = pltpu.get_barrier_semaphore()
        batch = [bit for bit in self.bits if bit[0] == "batch"]
        for step in range(1, z.n):
            pl.semaphore_signal(
                barrier,
                inc=1,
                device_id={"seq": lax.rem(me + step, z.n)},
                device_id_type=MESH,
            )
        for bit in batch:
            pl.semaphore_signal(
                barrier, inc=1, device_id=self.sums.partner(bit), device_id_type=MESH
            )
        pl.semaphore_wait(barrier, z.n - 1 + len(batch))
        self.before = self.neighbour(
            self.x.at[:, 3 * z.r - 16 :, :], self.halo, self.halo_sems, 1
        )

    def pool(self, part):
        width = self.z.width
        return dot(
            low(every_third(self.z, self.xf, 6 + part)),
            self.pool_w_v[part * width : (part + 1) * width, :],
        )

    def have(self, *names):
        for name in names:
            if name in self.loads:
                self.loads.pop(name).wait()

    def neighbour(self, source, target, sems, step):
        copy = pltpu.make_async_remote_copy(
            src_ref=source,
            dst_ref=target,
            send_sem=sems.at[0],
            recv_sem=sems.at[1],
            device_id={"seq": lax.rem(self.me + step, self.z.n)},
            device_id_type=MESH,
        )
        copy.start()
        return copy

    def exchange(self, name, unit):
        source, target, sems = (getattr(self, name + end) for end in ("_out", "_in", "_sems"))
        return Exchange(
            self.z.n, self.me, source.at[unit], target.at[unit], sems.at[unit]
        )

    def part(self, value, target, unit):
        z = self.z
        item = target // z.heads * z.units + unit
        head = target % z.heads
        return value[item * z.r : (item + 1) * z.r, head * z.hd : (head + 1) * z.hd]

    def to_rows(self, name, parts, target_refs):
        z = self.z
        source_ref = getattr(self, name + "_in")
        for unit in range(z.units):
            for source in range(z.n):
                item = source // z.heads * z.units + unit
                head = source % z.heads
                rows = slice(item * z.r, (item + 1) * z.r)
                lanes = slice(head * z.hd, (head + 1) * z.hd)
                for value, target_ref in zip(parts(source_ref[unit, source]), target_refs):
                    target_ref[rows, lanes] = value

    def pack(self, first, second, third):
        return jnp.concatenate([jnp.concatenate([first, second], axis=-1), fold(third)], axis=-2)

    def unpack(self, value):
        z = self.z
        return (
            value[..., : z.r, : z.hd],
            value[..., : z.r, z.hd :],
            unfold(value[..., z.r :, :]),
        )

    def live(self, part):
        z = self.z
        rows = [live_rows(z, self.me, self.lengths[item], part) for item in range(z.items)]
        return jnp.concatenate(rows, axis=0)

    def project(self):
        z, me, r, width = self.z, self.me, self.z.r, self.z.width
        self.have("x")
        rows_by_three(z, self.x_v, self.xf)
        self.xf[:, :, 0:8, :] = jnp.zeros((z.items, width // LANES, 8, LANES), jnp.float32)
        self.have("pool_w")
        pooled = self.pool(0) + self.pool(1) + self.pool(2)
        self.before.wait()
        before = jnp.where(me > 0, self.halo[...].astype(jnp.float32), 0.0)
        before = low(before.reshape(z.items * 16, width))
        parts = [dot(before, self.pool_w_v[part * width : (part + 1) * width, :]) for part in (0, 1)]
        row = lax.broadcasted_iota(jnp.int32, (z.rows, 1), 0)
        for item in range(z.items):
            at = item * 16 + 14
            extra = parts[0][at : at + 1, :] + parts[1][at + 1 : at + 2, :]
            pooled += jnp.where(row == item * r, extra, 0.0)
        self.short[...] = low(pooled)
        normed, inverse = norm_rows(self.short[...].astype(jnp.float32))
        self.normed1[...] = normed
        self.inverse1[...] = inverse
        self.have("gain1", "bias1", "query_w", "key_w", "value_w")
        self.attn_in[...] = low(normed * self.gain1_v[...] + self.bias1_v[...])
        attn_in = self.attn_in[...]
        qkv = [low(dot(attn_in, w[...])) for w in (self.query_w_v, self.key_w_v, self.value_w_v)]
        self.moves = []

        def send(unit):
            for target in range(z.n):
                self.qkv_out[unit, target] = self.pack(
                    *(self.part(value, target, unit) for value in qkv)
                )
            self.moves.append(self.exchange("qkv", unit))

        send(0)
        self.have("og", "up_w", "outer_w")
        rows_by_three(z, self.og_v, self.of)
        for part in range(3):
            self.up_rows[:, part * width : (part + 1) * width] = low(
                every_third(z, self.of, 8 + part) * self.live(part)
            )
        self.summed_grad[...] = low(dot_nt(self.up_rows[...], self.up_w_v[...]))
        for unit in range(1, z.units):
            send(unit)
        ff = self.outer_w_v.shape[0]
        for lo in range(0, ff, width):
            self.act_grad[:, lo : lo + width] = dot_nt(
                self.summed_grad[...], self.outer_w_v[lo : lo + width, :]
            )
        self.have("table", "position_w", "content_bias", "position_bias")
        first = self.head * z.hd
        pair = pl.ds(pl.multiple_of(lax.div(first, LANES) * LANES, LANES), LANES)
        both = dot(self.table_v[...], self.position_w_v[:, pair])
        self.pos[...] = low(pltpu.roll(both, LANES - lax.rem(first, LANES), 1)[:, : z.hd])

    def attend(self):
        z, hd = self.z, self.z.hd
        content_bias = self.content_bias_v[pl.ds(self.head, 1), :]
        position_bias = self.position_bias_v[pl.ds(self.head, 1), :]
        moves = []
        for unit in range(z.units):
            self.moves[unit].wait()
            queries, keys, values = (
                value.reshape(z.length, hd) for value in self.unpack(self.qkv_in[unit])
            )
            self.qc[unit] = low(queries.astype(jnp.float32) + content_bias)
            self.qp[unit] = low(queries.astype(jnp.float32) + position_bias)
            self.keys[unit] = keys
            self.values[unit] = values
            length = self.lengths[self.group * z.units + unit]
            for block in range(z.length // BLOCK):
                lo, hi = block * BLOCK, (block + 1) * BLOCK
                content = dot_nt(self.qc[unit, lo:hi, :], self.keys[unit, :hi, :])
                by_distance = dot_nt(self.qp[unit, lo:hi, :], self.pos[z.length - hi :, :])
                placed = pltpu.roll(by_distance, lo + 1, 1, stride=1, stride_axis=0)
                query_at = lo + lax.broadcasted_iota(jnp.int32, (BLOCK, hi), 0)
                key_at = lax.broadcasted_iota(jnp.int32, (BLOCK, hi), 1)
                valid = (key_at <= query_at) & (3 * key_at < length)
                logits = jnp.where(valid, (content + placed) * hd**-0.5, masked_value)
                raised = jnp.exp(logits - jnp.max(logits, axis=-1, keepdims=True))
                probs = raised / jnp.sum(raised, axis=-1, keepdims=True)
                self.probs[unit, lo:hi, :hi] = probs
                attended = low(dot(low(probs), self.values[unit, :hi, :]))
                per = BLOCK // z.r
                self.att_out[unit, block * per : (block + 1) * per] = fold(
                    attended.reshape(per, z.r, hd)
                )
            moves.append(self.exchange("att", unit))
        self.have("output_w", "gain2", "bias2", "inner_w")
        for move in moves:
            move.wait()

    def feed_forward(self):
        z, width = self.z, self.z.width
        ff = self.outer_w_v.shape[0]
        self.to_rows("att", lambda value: [unfold(value)], [self.att])
        hidden = self.short[...].astype(jnp.float32) + dot(self.att[...], self.output_w_v[...])
        normed, inverse = norm_rows(hidden)
        self.hidden[...] = hidden
        self.ffn_in[...] = low(normed * self.gain2_v[...] + self.bias2_v[...])
        ffn_in = self.ffn_in[...]
        ffn_grad = jnp.zeros((z.rows, width), jnp.float32)
        for lo in range(0, ff, width):
            cut = slice(lo, lo + width)
            inner = dot(ffn_in, self.inner_w_v[:, cut])
            normal_cdf = 0.5 * (1.0 + lax.erf(inner * 0.7071067811865476))
            density = jnp.exp(-0.5 * inner * inner) * 0.3989422804014327
            self.act[:, cut] = low(inner * normal_cdf)
            inner_grad = low(self.act_grad[:, cut] * (normal_cdf + inner * density))
            self.inner_grad[:, cut] = inner_grad
            ffn_grad += dot_nt(inner_grad, self.inner_w_v[:, cut])
        self.small_work[0, 2:3, :] = jnp.sum(ffn_grad * normed, axis=0, keepdims=True)
        self.small_work[0, 3:4, :] = jnp.sum(ffn_grad, axis=0, keepdims=True)
        hidden_grad = self.summed_grad[...].astype(jnp.float32) + norm_backward(
            ffn_grad, normed, inverse, self.gain2_v[...]
        )
        self.hidden_grad[...] = hidden_grad
        self.branch[...] = low(hidden_grad)
        att_grad = low(dot_nt(self.branch[...], self.output_w_v[...]))
        self.moves = []
        for unit in range(z.units):
            for target in range(z.n):
                self.grad_out[unit, target] = fold(self.part(att_grad, target, unit))
            self.moves.append(self.exchange("grad", unit))
        row = 0
        for lo in range(0, ff, width):
            self.reach("unit")
            self.work[row : row + width, :] = low(
                dot_tn(self.act[:, lo : lo + width], self.summed_grad[...])
            )
            row += width
        for lo in range(0, ff, width):
            self.reach("unit")
            self.work[row : row + width, :] = low(
                dot_tn(self.ffn_in[...], self.inner_grad[:, lo : lo + width])
            )
            row += width
        self.reach("unit")
        self.work[row : row + width, :] = low(dot_tn(self.att[...], self.branch[...]))
        row += width
        self.summed[...] = low(self.hidden[...] + dot(self.act[...], self.outer_w_v[...]))
        for lo in range(0, 3 * width, width):
            self.reach("unit")
            self.work[row : row + width, :] = low(
                dot_tn(self.summed[...], self.up_rows[:, lo : lo + width])
            )
            row += width
        self.row = row
        self.reach("grad")

    def upsample(self):
        z, width = self.z, self.z.width
        for part in range(3):
            up = dot(self.summed[...], self.up_w_v[:, part * width : (part + 1) * width])
            set_every_third(
                z, self.bf, 8 + part, every_third(z, self.xf, 8 + part) + up * self.live(part)
            )
        for item in range(z.items):
            for slab in range(width // LANES):
                self.block_out[item, :, slab * LANES : (slab + 1) * LANES] = low(
                    self.bf[item, slab, 8:, :]
                )

    def attend_back(self):
        z, r, hd, length = self.z, self.z.r, self.z.hd, self.z.length
        flip = reversal()
        moves = []
        content_sum = jnp.zeros((1, hd), jnp.float32)
        position_sum = jnp.zeros((1, hd), jnp.float32)
        self.key_t[...] = jnp.zeros_like(self.key_t)
        self.value_t[...] = jnp.zeros_like(self.value_t)
        self.table_t[...] = jnp.zeros_like(self.table_t)
        for unit in range(z.units):
            self.moves[unit].wait()
            att_grad = unfold(self.grad_in[unit]).reshape(length, hd)
            for block in range(length // BLOCK):
                self.reach("block")
                lo, hi = block * BLOCK, (block + 1) * BLOCK
                block_grad = att_grad[lo:hi]
                probs = self.probs[unit, lo:hi, :hi]
                prob_grad = dot_nt(block_grad, self.values[unit, :hi, :])
                delta = jnp.sum(probs * prob_grad, axis=-1, keepdims=True)
                raw = low(probs * (prob_grad - delta) * hd**-0.5)
                content = dot(raw, self.keys[unit, :hi, :])
                self.key_t[unit, :, :hi] += dot_tn(self.qc[unit, lo:hi, :], raw)
                self.value_t[unit, :, :hi] += dot_tn(block_grad, low(probs))
                by_distance = low(pltpu.roll(dot(flip, raw), 0, 1, stride=1, stride_axis=0))
                position = dot(by_distance, self.pos[length - hi :, :])
                upper = low(position)
                lower = low(position - upper.astype(jnp.float32))
                position = dot(flip, upper) + dot(flip, lower)
                flipped_q = low(dot(flip, self.qp[unit, lo:hi, :]))
                self.table_t[unit, :, length - hi :] += dot_tn(flipped_q, by_distance)
                content_sum += jnp.sum(content, axis=0, keepdims=True)
                position_sum += jnp.sum(position, axis=0, keepdims=True)
                self.query_grad[unit, lo:hi, :] = low(content + position)
            self.reach("send")
            parts = (
                self.query_grad[unit],
                low(self.key_t[unit].T),
                low(self.value_t[unit].T),
            )
            self.back_out[unit] = self.pack(*(value.reshape(z.n, r, hd) for value in parts))
            moves.append(self.exchange("back", unit))
        own = lax.broadcasted_iota(jnp.int32, (1, z.width), 1) // hd == self.head
        for row, value in ((4, content_sum), (5, position_sum)):
            spread = jnp.concatenate([value] * z.heads, axis=1)
            self.small_work[0, row : row + 1, :] = jnp.where(own, spread, 0.0)
        self.reach("table")
        table_sum = 0.0
        for unit in range(z.units):
            table_sum += dot(low(self.table_t[unit]), self.table_v[...])
        half = hd // 2
        base = self.chains[-2]["base"]
        for side in range(2):
            at = pl.multiple_of(base + side * z.heads * half + self.head * half, 16)
            self.work[pl.ds(at, half), :] = low(table_sum[side * half : (side + 1) * half])
        self.reach("up")
        self.upsample()
        self.reach("back")
        for move in moves:
            move.wait()

    def finish_rows(self):
        z, me, r, width = self.z, self.me, self.z.r, self.z.width
        self.reach("rows")
        self.to_rows("back", self.unpack, [self.row_grad.at[which] for which in range(3)])
        attn_grad = (
            dot_nt(self.row_grad[0], self.query_w_v[...])
            + dot_nt(self.row_grad[1], self.key_w_v[...])
            + dot_nt(self.row_grad[2], self.value_w_v[...])
        )
        normed = self.normed1[...]
        self.small_work[0, 0:1, :] = jnp.sum(attn_grad * normed, axis=0, keepdims=True)
        self.small_work[0, 1:2, :] = jnp.sum(attn_grad, axis=0, keepdims=True)
        self.small_work[0, 6:8, :] = jnp.zeros((2, width), jnp.float32)
        short_grad = low(
            self.hidden_grad[...]
            + norm_backward(attn_grad, normed, self.inverse1[...], self.gain1_v[...])
        )
        for item in range(z.items):
            self.first_rows[item] = short_grad[item * r : item * r + 16, :]
            self.later[item, 0:r, :] = short_grad[item * r : (item + 1) * r, :].astype(jnp.float32)
        halo = self.neighbour(self.first_rows, self.next_rows, self.next_sems, z.n - 1)
        row = self.row
        self.reach("qkv")
        for which in range(3):
            self.work[row : row + width, :] = low(dot_tn(self.attn_in[...], self.row_grad[which]))
            row += width
        self.reach("pool")
        own = dot_nt(short_grad, self.pool_w_v[2 * width :, :])
        set_every_third(z, self.of, 8, every_third(z, self.of, 8) + own)
        self.work[row + 2 * width : row + 3 * width, :] = low(
            dot_tn(low(every_third(z, self.xf, 8)), short_grad)
        )
        halo.wait()
        for item in range(z.items):
            after = jnp.where(me < z.n - 1, self.next_rows[item].astype(jnp.float32), 0.0)
            self.later[item, r : r + 8, :] = after[0:8, :]
        later = low(
            jnp.concatenate([self.later[item, 1 : r + 1, :] for item in range(z.items)], axis=0)
        )
        for part in range(2):
            cut = slice(row + part * width, row + (part + 1) * width)
            self.work[cut, :] = low(dot_tn(low(every_third(z, self.xf, 9 + part)), later))
        self.reach("input")
        for part in range(2):
            back = dot_nt(later, self.pool_w_v[part * width : (part + 1) * width, :])
            first = 9 + part
            set_every_third(z, self.of, first, every_third(z, self.of, first) + back)
        for item in range(z.items):
            for slab in range(width // LANES):
                self.input_grad[item, :, slab * LANES : (slab + 1) * LANES] = self.of[
                    item, slab, 8:, :
                ]

    def reach(self, name=None):
        while self.at < len(self.plan):
            kind, c, k = self.plan[self.at]
            self.at += 1
            if kind == "seg":
                assert k == name
                return
            if c == len(self.chains) - 1:
                self.small(k)
            elif kind == "sum":
                self.sums.start(c, k)
            else:
                self.sums.finish(c, k - 1)

    def small(self, k):
        if k:
            self.small_copy.wait()
            self.small_work[k] = self.small_work[k - 1] + self.small_landing[k - 1]
        if k < len(self.bits):
            self.small_start(k)
        else:
            self.small_total[...] = self.small_work[k]

    def small_start(self, k):
        self.small_copy = pltpu.make_async_remote_copy(
            src_ref=self.small_work.at[k],
            dst_ref=self.small_landing.at[k],
            send_sem=self.small_send.at[k],
            recv_sem=self.small_recv.at[k],
            device_id=self.sums.partner(self.bits[k]),
            device_id_type=MESH,
        )
        self.small_copy.start()

    def finish_sums(self):
        self.reach()


def block_kernel(z, plan, chains, bits, names, *refs):
    Pass(z, plan, chains, bits, names, refs).run()


def chains_of(z, ff, nb):
    width = z.width
    copies = Copies(nb, z.n)
    early = 2 * ff // width + 4
    units = early + 6
    searched = len(copies.bits) == 5 and sum(rows for rows, _, _ in CHAINS) == units
    chosen = CHAINS if searched else [(1, k, 0) for k in range(units)]
    chains, base = [], 0
    for rows, name, bias in chosen:
        order = copies.order(name) if searched else copies.rotated(name)
        chains.append(copies.halving(rows * width, order, base * width))
        chains[-1]["all"] = rows * width
        chains[-1]["bias"] = bias
        base += rows
        chains[-1]["units"] = base
    chains.append(copies.by_head(z.heads, z.hd, base * width))
    chains[-1]["all"] = z.heads * z.hd
    chains.append({"steps": [("small", bit, 0, 16) for bit in copies.bits]})
    blocks = z.length // BLOCK

    def done(first, last):
        return [c for c, chain in enumerate(chains) if first < chain.get("units", 0) <= last]

    segments = [("unit", UNIT, done(unit, unit + 1)) for unit in range(early)]
    segments += [("grad", 0.0, [])]
    segments += ([("block", BLOCK_STEP, [])] * blocks + [("send", SEND, [])]) * z.units
    segments += [("table", TABLE, [len(chains) - 2]), ("up", UP, [])]
    segments += [("back", 0.0, []), ("rows", ROWS, [len(chains) - 1])]
    segments += [("qkv", QKV, done(early, early + 3)), ("pool", POOL, done(early + 3, units))]
    segments += [("input", INPUT, [])]
    return copies, chains, segments


def result_kernel(
    z,
    ff,
    total_ref,
    small_ref,
    block_in_ref,
    input_in_ref,
    block_ref,
    input_ref,
    pool_ref,
    gain1_ref,
    bias1_ref,
    query_ref,
    key_ref,
    value_ref,
    position_ref,
    content_bias_ref,
    position_bias_ref,
    output_ref,
    gain2_ref,
    bias2_ref,
    inner_ref,
    outer_ref,
    up_ref,
    wide,
    store_sems,
    pass_sems,
):
    width = z.width
    blocks = wide.shape[0]
    places = [outer_ref.at[k * width : (k + 1) * width] for k in range(ff // width)]
    places += [inner_ref.at[:, k * width : (k + 1) * width] for k in range(ff // width)]
    places += [output_ref]
    places += [up_ref.at[:, k * width : (k + 1) * width] for k in range(3)]
    places += [query_ref, key_ref, value_ref]
    places += [pool_ref.at[k * width : (k + 1) * width] for k in range(3)]
    places += [position_ref]
    gain1_ref[...] = small_ref[0:1, :]
    bias1_ref[...] = small_ref[1:2, :]
    gain2_ref[...] = small_ref[2:3, :]
    bias2_ref[...] = small_ref[3:4, :]
    for head in range(z.heads):
        lanes = slice(head * z.hd, (head + 1) * z.hd)
        content_bias_ref[head : head + 1, :] = small_ref[4:5, lanes]
        position_bias_ref[head : head + 1, :] = small_ref[5:6, lanes]
    stores = []
    for which, (source, target) in enumerate(
        ((block_in_ref, block_ref), (input_in_ref, input_ref))
    ):
        stores.append(pltpu.make_async_copy(source, target, pass_sems.at[which]))
        stores[-1].start()
    for k in range(blocks):
        if k + 1 < blocks:
            wide[k] = total_ref[k * width : (k + 1) * width, :].astype(jnp.float32)
        else:
            half = z.hd // 2
            for head in range(z.heads):
                rows = []
                for side in range(2):
                    at = k * width + side * z.heads * half + head * half
                    rows.append(total_ref[at : at + half, :])
                both = jnp.concatenate(rows, axis=0).astype(jnp.float32)
                wide[k, :, head * z.hd : (head + 1) * z.hd] = both.T
        stores.append(pltpu.make_async_copy(wide.at[k], places[k], store_sems.at[k]))
        stores[-1].start()
    for copy in stores:
        copy.wait()


def body(
    byte_rows,
    item_lengths,
    out_grad,
    pool_weight,
    norm1_gain,
    norm1_bias,
    query_weight,
    key_weight,
    value_weight,
    position_weight,
    content_bias,
    position_bias,
    output_weight,
    norm2_gain,
    norm2_bias,
    inner_weight,
    outer_weight,
    upsample_weight,
):
    items, full_rows, width = byte_rows.shape
    heads, hd = content_bias.shape
    n = lax.axis_size("seq")
    ff = inner_weight.shape[1]
    z = Sizes(n, items, full_rows, width, heads)
    r, units, length, rows = z.r, z.units, z.length, z.rows
    bf, f4 = jnp.bfloat16, jnp.float32
    slabs = width // LANES
    dma = pltpu.SemaphoreType.DMA
    copies, chains, segments = chains_of(z, ff, lax.axis_size("batch"))
    plan = copies.schedule(chains, width, segments, r * LANES * 2)
    bits = copies.bits
    count, landing = Sums.needs(chains)
    total_rows = chains[-2]["base"] + chains[-2]["all"]
    operands = {
        "x": byte_rows,
        "pool_w": pool_weight,
        "gain1": norm1_gain.reshape(1, width),
        "bias1": norm1_bias.reshape(1, width),
        "query_w": query_weight,
        "key_w": key_weight,
        "value_w": value_weight,
        "og": out_grad,
        "up_w": upsample_weight,
        "outer_w": outer_weight,
        "table": distance_table(length, width),
        "position_w": position_weight,
        "content_bias": content_bias,
        "position_bias": position_bias,
        "output_w": output_weight,
        "gain2": norm2_gain.reshape(1, width),
        "bias2": norm2_bias.reshape(1, width),
        "inner_w": inner_weight,
    }
    outs = {
        "block_out": (byte_rows.shape, bf, VMEM),
        "input_grad": (byte_rows.shape, f4, VMEM),
        "total": ((total_rows, width), bf, VMEM),
        "small_total": ((8, width), f4, VMEM),
    }
    slab_rows = pltpu.VMEM((items, slabs, 3 * r + 8, LANES), f4)
    scratch = {name + "_v": pltpu.VMEM(operands[name].shape, operands[name].dtype) for name in OPERANDS}
    scratch.update(
        xf=slab_rows,
        of=slab_rows,
        bf=slab_rows,
        halo=pltpu.VMEM((items, 16, width), bf),
        first_rows=pltpu.VMEM((items, 16, width), bf),
        next_rows=pltpu.VMEM((items, 16, width), bf),
        later=pltpu.VMEM((items, r + 8, width), f4),
        short=pltpu.VMEM((rows, width), bf),
        normed1=pltpu.VMEM((rows, width), f4),
        inverse1=pltpu.VMEM((rows, 1), f4),
        attn_in=pltpu.VMEM((rows, width), bf),
        qkv_out=pltpu.VMEM((units, n, 3 * r // 2, 2 * hd), bf),
        qkv_in=pltpu.VMEM((units, n, 3 * r // 2, 2 * hd), bf),
        att_out=pltpu.VMEM((units, n, r // 2, 2 * hd), bf),
        att_in=pltpu.VMEM((units, n, r // 2, 2 * hd), bf),
        grad_out=pltpu.VMEM((units, n, r // 2, 2 * hd), bf),
        grad_in=pltpu.VMEM((units, n, r // 2, 2 * hd), bf),
        back_out=pltpu.VMEM((units, n, 3 * r // 2, 2 * hd), bf),
        back_in=pltpu.VMEM((units, n, 3 * r // 2, 2 * hd), bf),
        qc=pltpu.VMEM((units, length, hd), bf),
        qp=pltpu.VMEM((units, length, hd), bf),
        keys=pltpu.VMEM((units, length, hd), bf),
        values=pltpu.VMEM((units, length, hd), bf),
        pos=pltpu.VMEM((length, hd), bf),
        probs=pltpu.VMEM((units, length, length), f4),
        query_grad=pltpu.VMEM((units, length, hd), bf),
        key_t=pltpu.VMEM((units, hd, length), f4),
        value_t=pltpu.VMEM((units, hd, length), f4),
        table_t=pltpu.VMEM((units, hd, length), f4),
        att=pltpu.VMEM((rows, width), bf),
        hidden=pltpu.VMEM((rows, width), f4),
        ffn_in=pltpu.VMEM((rows, width), bf),
        act=pltpu.VMEM((rows, ff), bf),
        act_grad=pltpu.VMEM((rows, ff), f4),
        inner_grad=pltpu.VMEM((rows, ff), bf),
        up_rows=pltpu.VMEM((rows, 3 * width), bf),
        summed=pltpu.VMEM((rows, width), bf),
        summed_grad=pltpu.VMEM((rows, width), bf),
        hidden_grad=pltpu.VMEM((rows, width), f4),
        branch=pltpu.VMEM((rows, width), bf),
        row_grad=pltpu.VMEM((3, rows, width), bf),
        work=pltpu.VMEM((total_rows, width), bf),
        landing=pltpu.VMEM((landing, width), bf),
        small_work=pltpu.VMEM((len(bits) + 1, 8, width), f4),
        small_landing=pltpu.VMEM((len(bits), 8, width), f4),
        load_sems=dma((len(OPERANDS),)),
        halo_sems=dma((2,)),
        next_sems=dma((2,)),
        qkv_sems=dma((units, 2)),
        att_sems=dma((units, 2)),
        grad_sems=dma((units, 2)),
        back_sems=dma((units, 2)),
        sum_send=dma((len(chains) - 1,)),
        sum_recv=dma((count,)),
        small_send=dma((len(bits),)),
        small_recv=dma((len(bits),)),
    )
    names = ("lengths",) + OPERANDS + tuple(outs) + tuple(scratch)
    block_out, input_grad, total, small_t = pl.pallas_call(
        functools.partial(block_kernel, z, plan, chains, bits, names),
        out_shape=[
            pltpu.VMEM(shape, dtype) if space is VMEM else jax.ShapeDtypeStruct(shape, dtype)
            for shape, dtype, space in outs.values()
        ],
        in_specs=[SMEM] + [ANY] * len(OPERANDS),
        out_specs=[space for _, _, space in outs.values()],
        scratch_shapes=list(scratch.values()),
        compiler_params=pltpu.CompilerParams(
            collective_id=0, has_side_effects=True, vmem_limit_bytes=50 * 2**20
        ),
    )(item_lengths, *(operands[name] for name in OPERANDS))
    blocks = total.shape[0] // width
    shapes = [
        ((items, full_rows, width), bf, ANY),
        ((items, full_rows, width), f4, ANY),
        ((3 * width, width), f4, ANY),
        ((1, width), f4, VMEM),
        ((1, width), f4, VMEM),
        ((width, width), f4, ANY),
        ((width, width), f4, ANY),
        ((width, width), f4, ANY),
        ((width, width), f4, ANY),
        ((heads, hd), f4, VMEM),
        ((heads, hd), f4, VMEM),
        ((width, width), f4, ANY),
        ((1, width), f4, VMEM),
        ((1, width), f4, VMEM),
        ((width, ff), f4, ANY),
        ((ff, width), f4, ANY),
        ((width, 3 * width), f4, ANY),
    ]
    results = pl.pallas_call(
        functools.partial(result_kernel, z, ff),
        out_shape=[jax.ShapeDtypeStruct(shape, dtype) for shape, dtype, _ in shapes],
        in_specs=[VMEM] * 4,
        out_specs=[space for _, _, space in shapes],
        scratch_shapes=[
            pltpu.VMEM((blocks, width, width), f4),
            dma((blocks,)),
            dma((2,)),
        ],
        compiler_params=pltpu.CompilerParams(vmem_limit_bytes=30 * 2**20),
    )(total, small_t, block_out, input_grad)
    return tuple(
        value.reshape(width) if value.shape == (1, width) else value for value in results
    )


def solution(mesh):
    split = P("batch", "seq", None)
    in_specs = (split, P("batch"), split) + (P(),) * 15
    out_specs = (split, split) + (P(),) * 15
    return jax.shard_map(body, mesh=mesh, in_specs=in_specs, out_specs=out_specs, check_vma=False)
```

```python
import functools

import jax
import jax.numpy as jnp
import numpy as np
from jax import lax
from jax.experimental import pallas as pl
from jax.experimental.pallas import tpu as pltpu
from jax.sharding import PartitionSpec as P

MESH = pl.DeviceIdType.MESH
epsilon = 1e-05
masked_value = -1e30
CHAINS = (
    (1, "yxz0z1", 19),
    (1, "z0z1yx", -15),
    (2, "xyz0z1", 20),
    (1, "yz0xz1", 17),
    (2, "yxz1z0", 20),
    (2, "z0xyz1", 3),
    (2, "xyz0z1", 14),
    (1, "xyz0z1", -8),
    (1, "xyz0z1", -17),
    (2, "yxz0z1", 3),
    (1, "xyz0z1", 7),
    (1, "yxz1z0", 12),
    (1, "xyz0z1", 7),
)
LAG, CORE_LAG, ISSUE, MARGIN = 2.6, 1.0, 0.15, 0.1
UNIT, BRANCH, BLOCK_STEP, SEND, TABLE, UP, ROWS, QKV, POOL, INPUT = 0.33, 0.9, 0.7, 0.3, 0.4, 0.5, 0.7, 0.3, 0.4, 0.4
BLOCK = 128
LANES = 128
VMEM = pl.BlockSpec(memory_space=pltpu.VMEM)
SMEM = pl.BlockSpec(memory_space=pltpu.SMEM)
ANY = pl.BlockSpec(memory_space=pl.ANY)


def dot(left, right):
    return jnp.dot(left, right, preferred_element_type=jnp.float32)


def dot_nt(left, right):
    return lax.dot_general(
        left, right, (((1,), (1,)), ((), ())), preferred_element_type=jnp.float32
    )


def dot_tn(left, right):
    return lax.dot_general(
        left, right, (((0,), (0,)), ((), ())), preferred_element_type=jnp.float32
    )


def low(value):
    return value.astype(jnp.bfloat16)


def distance_table(short_len, width):
    distance = (short_len - 1 - np.arange(short_len)).astype(np.float32)
    steps_in = np.arange(0, width, 2).astype(np.float32)
    frequency = np.exp(-np.log(np.float32(10000.0)) * steps_in / np.float32(width))
    angles = distance[:, None] * frequency[None, :].astype(np.float32)
    both = np.concatenate([np.sin(angles), np.cos(angles)], axis=1)
    return jnp.asarray(both.astype(jnp.bfloat16))


def norm_rows(rows):
    mean = jnp.mean(rows, axis=-1, keepdims=True)
    centered = rows - mean
    inverse = lax.rsqrt(jnp.mean(centered * centered, axis=-1, keepdims=True) + epsilon)
    return centered * inverse, inverse


def norm_backward(gradient, normed, inverse, gain):
    scaled = gradient * gain
    return inverse * (
        scaled
        - jnp.mean(scaled, axis=-1, keepdims=True)
        - normed * jnp.mean(scaled * normed, axis=-1, keepdims=True)
    )


class Sizes:
    def __init__(self, n, items, full_rows, width, heads):
        self.n = n
        self.items = items
        self.r = full_rows // 3
        self.width = width
        self.heads = heads
        self.hd = width // heads
        self.units = items * heads // n
        self.length = n * self.r
        self.rows = items * self.r
        assert n % heads == 0 and self.units * self.hd <= LANES


class Exchange:
    def __init__(self, n, me, source, target, sems, rows):
        target[me, rows] = source[me, rows]
        for step in range(1, n):
            peer = lax.rem(me + step, n)
            pltpu.make_async_remote_copy(
                src_ref=source.at[peer, rows],
                dst_ref=target.at[me, rows],
                send_sem=sems.at[0],
                recv_sem=sems.at[1],
                device_id={"seq": peer},
                device_id_type=MESH,
            ).start()
        self.all = pltpu.make_async_remote_copy(
            src_ref=source.at[1:, rows],
            dst_ref=target.at[1:, rows],
            send_sem=sems.at[0],
            recv_sem=sems.at[1],
            device_id={"seq": lax.rem(me + 1, n)},
            device_id_type=MESH,
        )

    def wait(self):
        self.all.wait()


def rows_by_three(z, x_ref, xf_ref):
    for item in range(z.items):
        for slab in range(z.width // LANES):
            xf_ref[item, slab, 8:, :] = x_ref[item, :, slab * LANES : (slab + 1) * LANES].astype(
                jnp.float32
            )


def every_third(z, xf_ref, first):
    items = []
    for item in range(z.items):
        slabs = [
            xf_ref[item, slab, pl.ds(first, z.r, stride=3), :] for slab in range(z.width // LANES)
        ]
        items.append(jnp.concatenate(slabs, axis=1))
    return jnp.concatenate(items, axis=0)


def set_every_third(z, xf_ref, first, value):
    for item in range(z.items):
        for slab in range(z.width // LANES):
            xf_ref[item, slab, pl.ds(first, z.r, stride=3), :] = value[
                item * z.r : (item + 1) * z.r, slab * LANES : (slab + 1) * LANES
            ]


def fold(value):
    half = value.shape[-2] // 2
    return jnp.concatenate([value[..., :half, :], value[..., half:, :]], axis=-1)


def unfold(value):
    half = value.shape[-1] // 2
    return jnp.concatenate([value[..., :half], value[..., half:]], axis=-2)


def live_rows(z, me, length, part):
    at = lax.broadcasted_iota(jnp.int32, (z.r, 1), 0) * 3 + part + me * 3 * z.r
    return (at < length).astype(jnp.float32)


def reversal():
    at = lax.broadcasted_iota(jnp.int32, (BLOCK, BLOCK), 0)
    across = lax.broadcasted_iota(jnp.int32, (BLOCK, BLOCK), 1)
    return low((at + across == BLOCK - 1).astype(jnp.float32))


class Copies:
    def __init__(self, batch_size, seq_size):
        self.core = [("batch", 1)]
        self.chips = [("batch", 1 << k) for k in range(1, batch_size.bit_length() - 1)]
        self.line = [("seq", 1 << k) for k in range(seq_size.bit_length() - 1)]
        self.bits = self.core + self.chips + self.line

    def cost(self, bit, size):
        axis, mask = bit
        if bit in self.core:
            return {"core": size / 428e3}
        near = 2 * size / 92e3
        if bit in self.line[:1] or axis == "batch":
            return {bit: near}
        return {"line": near, bit: near * (mask // 2)}

    def order(self, name):
        order = list(self.core)
        links = {"x": self.chips[0], "y": self.line[0], "z0": self.line[1], "z1": self.line[2]}
        while name:
            for key, bit in links.items():
                if name.startswith(key):
                    order.append(bit)
                    name = name[len(key) :]
        return order

    def rotated(self, k):
        links = self.chips + self.line
        k %= len(links)
        return self.core + links[k:] + links[:k]

    def hold(self, size):
        count = 1 << len(self.line)
        y = 2 * size * count / 2 / 92e3
        return {self.line[0]: y, "line": 1.5 * y, self.line[-1]: 2 * y}

    def halving(self, rows, order, base):
        down, up = [], []
        for bit in order:
            if rows % 32 == 0:
                rows //= 2
                down.append(("sum", bit, rows, rows))
                up.append(("spread", bit, rows, rows))
            else:
                down.append(("sum", bit, 0, rows))
        return {"base": base, "fixed": [], "steps": down + up[::-1], "rows": rows}

    def by_head(self, heads, hd, base):
        head_bits = self.line[: heads.bit_length() - 1]
        batch_bits = self.core + self.chips
        rest = self.line[len(head_bits) :]
        rows, parts = hd, []
        for bit in batch_bits + rest:
            if rows % 32 == 0:
                rows //= 2
                parts.append((bit, rows))
            else:
                parts.append((bit, 0))
        split = [bit for bit, size in parts if size]
        inner = split[1:]
        stride, strides = rows, {}
        for bit in inner[::-1] + head_bits + split[:1]:
            strides[bit] = stride
            stride *= 2
        down = [("sum", bit, strides.get(bit, 0), size or rows) for bit, size in parts]
        up = [("spread", bit, strides[bit], strides[bit]) for bit in strides]
        fixed = [(bit, strides[bit]) for bit in head_bits]
        return {"base": base, "fixed": fixed, "steps": down + up, "rows": rows, "strides": strides}

    def schedule(self, chains, width, segments, size):
        left = []
        for chain in chains:
            total = [0.0]
            for _, bit, _, rows in chain["steps"][::-1]:
                busy = max(self.cost(bit, 2 * rows * width).values())
                total.append(total[-1] + busy + LAG)
            left.append(total[::-1])
        free, at, plan = {}, [0] * len(chains), []
        ready = [None] * len(chains)
        now, segment, sent = 0.0, 0, {}

        def hold(name, times):
            for link, busy in self.hold(times * size).items():
                free[link] = max(free.get(link, 0.0), now) + busy
            sent[name] = max(free[link] for link in self.hold(size)) + LAG + 0.5

        sends = sum(name == "send" for name, _, _ in segments)
        while True:
            best, later = None, []
            for c, chain in enumerate(chains):
                if ready[c] is None or at[c] > len(chain["steps"]):
                    continue
                if at[c] == len(chain["steps"]):
                    start = ready[c] + MARGIN
                else:
                    _, bit, _, rows = chain["steps"][at[c]]
                    cost = self.cost(bit, 2 * rows * width)
                    start = max([ready[c] + (MARGIN if at[c] else 0.0)] + [free.get(link, 0.0) - 0.3 for link in cost])
                if start <= now:
                    key = (-left[c][at[c]] - chain.get("bias", 0), c)
                    best = key if best is None or key < best else best
                else:
                    later.append(start)
            if best is not None:
                c = best[1]
                k = at[c]
                at[c] += 1
                steps = chains[c]["steps"]
                now += ISSUE
                if k and steps[k - 1][0] == "sum":
                    now += 0.4e-6 * 2 * steps[k - 1][3] * width
                if k == len(steps):
                    plan.append(("end", c, k))
                    continue
                _, bit, _, rows = steps[k]
                cost = self.cost(bit, 2 * rows * width)
                start = max([now] + [free.get(link, 0.0) for link in cost])
                for link, busy in cost.items():
                    free[link] = start + busy
                lag = CORE_LAG if bit in self.core else LAG
                ready[c] = start + max(cost.values()) + lag
                plan.append(("sum", c, k))
                continue
            if segment < len(segments):
                name, busy, releases = segments[segment]
                due = sent.get(name, 0.0)
                if due <= now:
                    plan.append(("seg", segment, name))
                    now += busy
                    for c in releases:
                        ready[c] = now
                    if name == "branch":
                        hold("grad", 1)
                    if name == "send":
                        hold("back", 3 / sends)
                    segment += 1
                    continue
                later.append(due)
            if not later:
                self.end = now
                return plan
            now = max(now + 0.01, min(later))


class Sums:
    def __init__(self, chains, work, landing, total, send_sems, recv_sems):
        self.chains = chains
        self.work, self.landing, self.total = work, landing, total
        self.send_sems, self.recv_sems = send_sems, recv_sems
        self.index = {"batch": lax.axis_index("batch"), "seq": lax.axis_index("seq")}
        self.open = {}
        self.offset = {}
        sem = land = 0
        self.sem, self.land = {}, {}
        for c, chain in enumerate(chains[:-1]):
            self.offset[c] = chain["base"] + sum(
                self.bit(bit) * stride for bit, stride in chain["fixed"]
            )
            for k, (phase, _, _, rows) in enumerate(chain["steps"]):
                self.sem[c, k] = sem
                sem += 1
                if phase == "sum":
                    self.land[c, k] = land
                    land += rows

    @staticmethod
    def needs(chains):
        steps = [step for chain in chains[:-1] for step in chain["steps"]]
        return len(steps), sum(step[3] for step in steps if step[0] == "sum")

    def bit(self, bit):
        axis, mask = bit
        return lax.rem(lax.div(self.index[axis], mask), 2)

    def partner(self, bit):
        axis, mask = bit
        return {axis: self.index[axis] + mask - 2 * mask * self.bit(bit)}

    def start(self, c, k):
        if k:
            self.finish(c, k - 1)
        phase, bit, stride, rows = self.chains[c]["steps"][k]
        side = self.bit(bit)
        offset = self.offset[c]
        if phase == "sum":
            other = offset + (1 - side) * stride if stride else offset
            source = self.work.at[pl.ds(pl.multiple_of(other, 16), rows)]
            target = self.landing.at[pl.ds(self.land[c, k], rows)]
            if stride:
                self.offset[c] = offset + side * stride
        else:
            here = pl.ds(pl.multiple_of(offset, 16), rows)
            source, target = self.total.at[here], self.total.at[here]
            self.offset[c] = offset - side * stride
        copy = pltpu.make_async_remote_copy(
            src_ref=source,
            dst_ref=target,
            send_sem=self.send_sems.at[c],
            recv_sem=self.recv_sems.at[self.sem[c, k]],
            device_id=self.partner(bit),
            device_id_type=MESH,
        )
        copy.start()
        self.open[c] = copy

    def finish(self, c, k):
        self.open.pop(c).wait()
        steps = self.chains[c]["steps"]
        phase, _, _, rows = steps[k]
        if phase == "sum":
            last = k + 1 == len(steps) or steps[k + 1][0] == "spread"
            held = pl.ds(pl.multiple_of(self.offset[c], 16), rows)
            landed = self.landing[self.land[c, k] : self.land[c, k] + rows, :]
            both = self.work[held, :].astype(jnp.float32) + landed.astype(jnp.float32)
            (self.total if last else self.work)[held, :] = low(both)


OPERANDS = (
    "x",
    "pool_w",
    "gain1",
    "bias1",
    "query_w",
    "key_w",
    "value_w",
    "og",
    "up_w",
    "outer_w",
    "table",
    "position_w",
    "content_bias",
    "position_bias",
    "output_w",
    "gain2",
    "bias2",
    "inner_w",
)


class Pass:
    def __init__(self, z, plan, chains, bits, names, refs):
        self.z = z
        self.__dict__.update(zip(names, refs))
        self.plan, self.chains, self.bits = plan, chains, bits
        self.me = lax.axis_index("seq")
        self.head = lax.rem(self.me, z.heads)
        self.group = lax.div(self.me, z.heads)
        self.sums = Sums(
            chains, self.work, self.landing, self.total, self.sum_send, self.sum_recv
        )
        self.at = 0
        self.loads = {}

    def run(self):
        self.enter()
        self.project()
        self.attend()
        self.feed_forward()
        self.attend_back()
        self.finish_rows()
        self.finish_sums()

    def enter(self):
        z, me = self.z, self.me
        for k, name in enumerate(OPERANDS):
            self.loads[name] = pltpu.make_async_copy(
                getattr(self, name), getattr(self, name + "_v"), self.load_sems.at[k]
            )
            self.loads[name].start()
        barrier = pltpu.get_barrier_semaphore()
        batch = [bit for bit in self.bits if bit[0] == "batch"]
        for step in range(1, z.n):
            pl.semaphore_signal(
                barrier,
                inc=1,
                device_id={"seq": lax.rem(me + step, z.n)},
                device_id_type=MESH,
            )
        for bit in batch:
            pl.semaphore_signal(
                barrier, inc=1, device_id=self.sums.partner(bit), device_id_type=MESH
            )
        pl.semaphore_wait(barrier, z.n - 1 + len(batch))
        self.before = self.neighbour(
            self.x.at[:, 3 * z.r - 16 :, :], self.halo, self.halo_sems, 1
        )

    def pool(self, part):
        width = self.z.width
        return dot(
            low(every_third(self.z, self.xf, 6 + part)),
            self.pool_w_v[part * width : (part + 1) * width, :],
        )

    def have(self, *names):
        for name in names:
            if name in self.loads:
                self.loads.pop(name).wait()

    def neighbour(self, source, target, sems, step):
        copy = pltpu.make_async_remote_copy(
            src_ref=source,
            dst_ref=target,
            send_sem=sems.at[0],
            recv_sem=sems.at[1],
            device_id={"seq": lax.rem(self.me + step, self.z.n)},
            device_id_type=MESH,
        )
        copy.start()
        return copy

    def exchange(self, name, unit, rows=None, sems=None):
        source, target = (getattr(self, name + end).at[unit] for end in ("_out", "_in"))
        sems = getattr(self, name + "_sems").at[unit if sems is None else sems]
        rows = slice(0, source.shape[1]) if rows is None else rows
        return Exchange(self.z.n, self.me, source, target, sems, rows)

    def part(self, value, target, unit):
        z = self.z
        item = target // z.heads * z.units + unit
        head = target % z.heads
        return value[item * z.r : (item + 1) * z.r, head * z.hd : (head + 1) * z.hd]

    def to_rows(self, name, parts, target_refs):
        z = self.z
        source_ref = getattr(self, name + "_in")
        for unit in range(z.units):
            for source in range(z.n):
                item = source // z.heads * z.units + unit
                head = source % z.heads
                rows = slice(item * z.r, (item + 1) * z.r)
                lanes = slice(head * z.hd, (head + 1) * z.hd)
                for value, target_ref in zip(parts(source_ref[unit, source]), target_refs):
                    target_ref[rows, lanes] = value

    def pack(self, first, second, third):
        pair, folded = jnp.concatenate([first, second], axis=-1), fold(third)
        parts = [pair[..., 16:, :], folded[..., 16:, :], pair[..., :16, :], folded[..., :16, :]]
        return jnp.concatenate(parts, axis=-2)

    def unpack(self, value):
        r, hd = self.z.r, self.z.hd
        late = 3 * r // 2 - 32
        pair = jnp.concatenate([value[..., late : late + 16, :], value[..., : r - 16, :]], axis=-2)
        folded = [value[..., late + 16 :, :], value[..., r - 16 : late, :]]
        return pair[..., :hd], pair[..., hd:], unfold(jnp.concatenate(folded, axis=-2))

    def live(self, part):
        z = self.z
        rows = [live_rows(z, self.me, self.lengths[item], part) for item in range(z.items)]
        return jnp.concatenate(rows, axis=0)

    def project(self):
        z, me, r, width = self.z, self.me, self.z.r, self.z.width
        self.have("x")
        rows_by_three(z, self.x_v, self.xf)
        self.xf[:, :, 0:8, :] = jnp.zeros((z.items, width // LANES, 8, LANES), jnp.float32)
        self.have("pool_w")
        pooled = self.pool(0) + self.pool(1) + self.pool(2)
        self.have("gain1", "bias1", "query_w", "key_w", "value_w")
        weights = (self.query_w_v, self.key_w_v, self.value_w_v)

        def normalize(rows):
            short = low(rows)
            normed, inverse = norm_rows(short.astype(jnp.float32))
            attn_in = low(normed * self.gain1_v[...] + self.bias1_v[...])
            return short, normed, inverse, attn_in

        kept = (self.short, self.normed1, self.inverse1, self.attn_in)
        for ref, value in zip(kept, normalize(pooled)):
            ref[...] = value
        qkv = [low(dot(self.attn_in[...], w[...])) for w in weights]
        late = 3 * r // 2 - 32
        self.moves = []

        def fill(unit):
            for target in range(z.n):
                self.qkv_out[unit, target] = self.pack(
                    *(self.part(value, target, unit) for value in qkv)
                )

        fill(0)
        self.moves.append([self.exchange("qkv", 0, slice(0, late))])
        self.before.wait()
        before = jnp.where(me > 0, self.halo[...].astype(jnp.float32), 0.0)
        before = low(before.reshape(z.items * 16, width))
        parts = [dot(before, self.pool_w_v[part * width : (part + 1) * width, :]) for part in (0, 1)]
        row = lax.broadcasted_iota(jnp.int32, (16, 1), 0)
        first = []
        for item in range(z.items):
            at = item * 16 + 14
            extra = parts[0][at : at + 1, :] + parts[1][at + 1 : at + 2, :]
            first.append(pooled[item * r : item * r + 16, :] + jnp.where(row == 0, extra, 0.0))
        first = normalize(jnp.concatenate(first, axis=0))
        for ref, value in zip(kept, first):
            for item in range(z.items):
                ref[item * r : item * r + 16, :] = value[item * 16 : (item + 1) * 16, :]
        for which, w in enumerate(weights):
            value = low(dot(first[3], w[...]))
            pieces = []
            for item in range(z.items):
                pieces += [
                    value[item * 16 : (item + 1) * 16, :],
                    qkv[which][item * r + 16 : (item + 1) * r, :],
                ]
            qkv[which] = jnp.concatenate(pieces, axis=0)
        for target in range(z.n):
            packed = self.pack(*(self.part(value, target, 0) for value in qkv))
            self.qkv_out[0, target, late:, :] = packed[late:, :]
        self.moves[0].append(self.exchange("qkv", 0, slice(late, late + 32), z.units))
        self.have("og", "up_w", "outer_w")
        rows_by_three(z, self.og_v, self.of)
        for part in range(3):
            self.up_rows[:, part * width : (part + 1) * width] = low(
                every_third(z, self.of, 8 + part) * self.live(part)
            )
        self.summed_grad[...] = low(dot_nt(self.up_rows[...], self.up_w_v[...]))
        for unit in range(1, z.units):
            fill(unit)
            self.moves.append([self.exchange("qkv", unit)])
        ff = self.outer_w_v.shape[0]
        for lo in range(0, ff, width):
            self.act_grad[:, lo : lo + width] = dot_nt(
                self.summed_grad[...], self.outer_w_v[lo : lo + width, :]
            )
        self.have("table", "position_w", "content_bias", "position_bias")
        first = self.head * z.hd
        pair = pl.ds(pl.multiple_of(lax.div(first, LANES) * LANES, LANES), LANES)
        both = dot(self.table_v[...], self.position_w_v[:, pair])
        self.pos[...] = low(pltpu.roll(both, LANES - lax.rem(first, LANES), 1)[:, : z.hd])

    def attend(self):
        z, hd = self.z, self.z.hd
        content_bias = self.content_bias_v[pl.ds(self.head, 1), :]
        position_bias = self.position_bias_v[pl.ds(self.head, 1), :]
        moves = []
        for unit in range(z.units):
            for move in self.moves[unit]:
                move.wait()
            queries, keys, values = (
                value.reshape(z.length, hd) for value in self.unpack(self.qkv_in[unit])
            )
            self.qc[unit] = low(queries.astype(jnp.float32) + content_bias)
            self.qp[unit] = low(queries.astype(jnp.float32) + position_bias)
            self.keys[unit] = keys
            self.values[unit] = values
            length = self.lengths[self.group * z.units + unit]
            for block in range(z.length // BLOCK):
                lo, hi = block * BLOCK, (block + 1) * BLOCK
                content = dot_nt(self.qc[unit, lo:hi, :], self.keys[unit, :hi, :])
                by_distance = dot_nt(self.qp[unit, lo:hi, :], self.pos[z.length - hi :, :])
                placed = pltpu.roll(by_distance, lo + 1, 1, stride=1, stride_axis=0)
                query_at = lo + lax.broadcasted_iota(jnp.int32, (BLOCK, hi), 0)
                key_at = lax.broadcasted_iota(jnp.int32, (BLOCK, hi), 1)
                valid = (key_at <= query_at) & (3 * key_at < length)
                logits = jnp.where(valid, (content + placed) * hd**-0.5, masked_value)
                raised = jnp.exp(logits - jnp.max(logits, axis=-1, keepdims=True))
                probs = raised / jnp.sum(raised, axis=-1, keepdims=True)
                self.probs[unit, lo:hi, :hi] = probs
                attended = low(dot(low(probs), self.values[unit, :hi, :]))
                per = BLOCK // z.r
                self.att_out[unit, block * per : (block + 1) * per] = fold(
                    attended.reshape(per, z.r, hd)
                )
            moves.append(self.exchange("att", unit))
        self.have("output_w", "gain2", "bias2", "inner_w")
        for move in moves:
            move.wait()

    def feed_forward(self):
        z, width = self.z, self.z.width
        ff = self.outer_w_v.shape[0]
        self.to_rows("att", lambda value: [unfold(value)], [self.att])
        hidden = self.short[...].astype(jnp.float32) + dot(self.att[...], self.output_w_v[...])
        normed, inverse = norm_rows(hidden)
        self.hidden[...] = hidden
        self.ffn_in[...] = low(normed * self.gain2_v[...] + self.bias2_v[...])
        ffn_in = self.ffn_in[...]
        ffn_grad = jnp.zeros((z.rows, width), jnp.float32)
        for lo in range(0, ff, width):
            cut = slice(lo, lo + width)
            inner = dot(ffn_in, self.inner_w_v[:, cut])
            normal_cdf = 0.5 * (1.0 + lax.erf(inner * 0.7071067811865476))
            density = jnp.exp(-0.5 * inner * inner) * 0.3989422804014327
            self.act[:, cut] = low(inner * normal_cdf)
            inner_grad = low(self.act_grad[:, cut] * (normal_cdf + inner * density))
            self.inner_grad[:, cut] = inner_grad
            ffn_grad += dot_nt(inner_grad, self.inner_w_v[:, cut])
        row = 0
        for lo in range(0, ff, width):
            self.reach("unit")
            self.work[row : row + width, :] = low(
                dot_tn(self.act[:, lo : lo + width], self.summed_grad[...])
            )
            row += width
        self.reach("branch")
        self.small_work[0, 2:3, :] = jnp.sum(ffn_grad * normed, axis=0, keepdims=True)
        self.small_work[0, 3:4, :] = jnp.sum(ffn_grad, axis=0, keepdims=True)
        hidden_grad = self.summed_grad[...].astype(jnp.float32) + norm_backward(
            ffn_grad, normed, inverse, self.gain2_v[...]
        )
        self.hidden_grad[...] = hidden_grad
        self.branch[...] = low(hidden_grad)
        att_grad = low(dot_nt(self.branch[...], self.output_w_v[...]))
        self.moves = []
        for unit in range(z.units):
            for target in range(z.n):
                self.grad_out[unit, target] = fold(self.part(att_grad, target, unit))
            self.moves.append(self.exchange("grad", unit))
        for lo in range(0, ff, width):
            self.reach("unit")
            self.work[row : row + width, :] = low(
                dot_tn(self.ffn_in[...], self.inner_grad[:, lo : lo + width])
            )
            row += width
        self.reach("unit")
        self.work[row : row + width, :] = low(dot_tn(self.att[...], self.branch[...]))
        row += width
        self.summed[...] = low(self.hidden[...] + dot(self.act[...], self.outer_w_v[...]))
        for lo in range(0, 3 * width, width):
            self.reach("unit")
            self.work[row : row + width, :] = low(
                dot_tn(self.summed[...], self.up_rows[:, lo : lo + width])
            )
            row += width
        self.row = row
        self.reach("grad")

    def upsample(self):
        z, width = self.z, self.z.width
        for part in range(3):
            self.reach("up")
            up = dot(self.summed[...], self.up_w_v[:, part * width : (part + 1) * width])
            set_every_third(
                z, self.bf, 8 + part, every_third(z, self.xf, 8 + part) + up * self.live(part)
            )
        for item in range(z.items):
            for slab in range(width // LANES):
                self.block_out[item, :, slab * LANES : (slab + 1) * LANES] = low(
                    self.bf[item, slab, 8:, :]
                )

    def attend_back(self):
        z, r, hd, length = self.z, self.z.r, self.z.hd, self.z.length
        flip = reversal()
        moves = []
        content_sum = jnp.zeros((1, hd), jnp.float32)
        position_sum = jnp.zeros((1, hd), jnp.float32)
        self.key_t[...] = jnp.zeros_like(self.key_t)
        self.value_t[...] = jnp.zeros_like(self.value_t)
        self.table_t[...] = jnp.zeros_like(self.table_t)
        for unit in range(z.units):
            self.moves[unit].wait()
            att_grad = unfold(self.grad_in[unit]).reshape(length, hd)
            for block in range(length // BLOCK):
                self.reach("block")
                lo, hi = block * BLOCK, (block + 1) * BLOCK
                block_grad = att_grad[lo:hi]
                probs = self.probs[unit, lo:hi, :hi]
                prob_grad = dot_nt(block_grad, self.values[unit, :hi, :])
                delta = jnp.sum(probs * prob_grad, axis=-1, keepdims=True)
                raw = low(probs * (prob_grad - delta) * hd**-0.5)
                content = dot(raw, self.keys[unit, :hi, :])
                self.key_t[unit, :, :hi] += dot_tn(self.qc[unit, lo:hi, :], raw)
                self.value_t[unit, :, :hi] += dot_tn(block_grad, low(probs))
                by_distance = low(pltpu.roll(dot(flip, raw), 0, 1, stride=1, stride_axis=0))
                position = dot(by_distance, self.pos[length - hi :, :])
                upper = low(position)
                lower = low(position - upper.astype(jnp.float32))
                position = dot(flip, upper) + dot(flip, lower)
                flipped_q = low(dot(flip, self.qp[unit, lo:hi, :]))
                self.table_t[unit, :, length - hi :] += dot_tn(flipped_q, by_distance)
                content_sum += jnp.sum(content, axis=0, keepdims=True)
                position_sum += jnp.sum(position, axis=0, keepdims=True)
                self.query_grad[unit, lo:hi, :] = low(content + position)
            self.reach("send")
            parts = (
                self.query_grad[unit],
                low(self.key_t[unit].T),
                low(self.value_t[unit].T),
            )
            self.back_out[unit] = self.pack(*(value.reshape(z.n, r, hd) for value in parts))
            moves.append(self.exchange("back", unit))
        own = lax.broadcasted_iota(jnp.int32, (1, z.width), 1) // hd == self.head
        for row, value in ((4, content_sum), (5, position_sum)):
            spread = jnp.concatenate([value] * z.heads, axis=1)
            self.small_work[0, row : row + 1, :] = jnp.where(own, spread, 0.0)
        self.reach("table")
        table_sum = 0.0
        for unit in range(z.units):
            table_sum += dot(low(self.table_t[unit]), self.table_v[...])
        half = hd // 2
        base = self.chains[-2]["base"]
        for side in range(2):
            at = pl.multiple_of(base + side * z.heads * half + self.head * half, 16)
            self.work[pl.ds(at, half), :] = low(table_sum[side * half : (side + 1) * half])
        self.upsample()
        self.reach("back")
        for move in moves:
            move.wait()

    def finish_rows(self):
        z, me, r, width = self.z, self.me, self.z.r, self.z.width
        self.reach("rows")
        self.to_rows("back", self.unpack, [self.row_grad.at[which] for which in range(3)])
        self.reach("rows")
        attn_grad = (
            dot_nt(self.row_grad[0], self.query_w_v[...])
            + dot_nt(self.row_grad[1], self.key_w_v[...])
            + dot_nt(self.row_grad[2], self.value_w_v[...])
        )
        self.reach("rows")
        normed = self.normed1[...]
        self.small_work[0, 0:1, :] = jnp.sum(attn_grad * normed, axis=0, keepdims=True)
        self.small_work[0, 1:2, :] = jnp.sum(attn_grad, axis=0, keepdims=True)
        self.small_work[0, 6:8, :] = jnp.zeros((2, width), jnp.float32)
        short_grad = low(
            self.hidden_grad[...]
            + norm_backward(attn_grad, normed, self.inverse1[...], self.gain1_v[...])
        )
        for item in range(z.items):
            self.first_rows[item] = short_grad[item * r : item * r + 16, :]
            self.later[item, 0:r, :] = short_grad[item * r : (item + 1) * r, :].astype(jnp.float32)
        halo = self.neighbour(self.first_rows, self.next_rows, self.next_sems, z.n - 1)
        row = self.row
        for which in range(3):
            self.reach("qkv")
            self.work[row : row + width, :] = low(dot_tn(self.attn_in[...], self.row_grad[which]))
            row += width
        self.reach("pool")
        self.work[row : row + width, :] = low(dot_tn(low(every_third(z, self.xf, 8)), short_grad))
        halo.wait()
        for item in range(z.items):
            after = jnp.where(me < z.n - 1, self.next_rows[item].astype(jnp.float32), 0.0)
            self.later[item, r : r + 8, :] = after[0:8, :]
        later = low(
            jnp.concatenate([self.later[item, 1 : r + 1, :] for item in range(z.items)], axis=0)
        )
        for part in range(2):
            row += width
            self.reach("pool")
            self.work[row : row + width, :] = low(
                dot_tn(low(every_third(z, self.xf, 9 + part)), later)
            )
        for part, rows, first in ((2, short_grad, 8), (0, later, 9), (1, later, 10)):
            self.reach("input")
            back = dot_nt(rows, self.pool_w_v[part * width : (part + 1) * width, :])
            set_every_third(z, self.of, first, every_third(z, self.of, first) + back)
        for item in range(z.items):
            for slab in range(width // LANES):
                self.input_grad[item, :, slab * LANES : (slab + 1) * LANES] = self.of[
                    item, slab, 8:, :
                ]

    def reach(self, name=None):
        while self.at < len(self.plan):
            kind, c, k = self.plan[self.at]
            self.at += 1
            if kind == "seg":
                assert k == name
                return
            if c == len(self.chains) - 1:
                self.small(k)
            elif kind == "sum":
                self.sums.start(c, k)
            else:
                self.sums.finish(c, k - 1)

    def small(self, k):
        if k:
            self.small_copy.wait()
            self.small_work[k] = self.small_work[k - 1] + self.small_landing[k - 1]
        if k < len(self.bits):
            self.small_start(k)
        else:
            self.small_total[...] = self.small_work[k]

    def small_start(self, k):
        self.small_copy = pltpu.make_async_remote_copy(
            src_ref=self.small_work.at[k],
            dst_ref=self.small_landing.at[k],
            send_sem=self.small_send.at[k],
            recv_sem=self.small_recv.at[k],
            device_id=self.sums.partner(self.bits[k]),
            device_id_type=MESH,
        )
        self.small_copy.start()

    def finish_sums(self):
        self.reach()


def block_kernel(z, plan, chains, bits, names, *refs):
    Pass(z, plan, chains, bits, names, refs).run()


def chains_of(z, ff, nb):
    width = z.width
    copies = Copies(nb, z.n)
    early = 2 * ff // width + 4
    units = early + 6
    searched = len(copies.bits) == 5 and sum(rows for rows, _, _ in CHAINS) == units
    chosen = CHAINS if searched else [(1, k, 0) for k in range(units)]
    chains, base = [], 0
    for rows, name, bias in chosen:
        order = copies.order(name) if searched else copies.rotated(name)
        chains.append(copies.halving(rows * width, order, base * width))
        chains[-1]["all"] = rows * width
        chains[-1]["bias"] = bias
        base += rows
        chains[-1]["units"] = base
    chains.append(copies.by_head(z.heads, z.hd, base * width))
    chains[-1]["all"] = z.heads * z.hd
    chains.append({"steps": [("small", bit, 0, 16) for bit in copies.bits]})
    blocks = z.length // BLOCK

    def done(first, last):
        return [c for c, chain in enumerate(chains) if first < chain.get("units", 0) <= last]

    segments = [("unit", UNIT, done(unit, unit + 1)) for unit in range(early)]
    segments.insert(ff // width, ("branch", BRANCH, []))
    segments += [("grad", 0.0, [])]
    segments += ([("block", BLOCK_STEP, [])] * blocks + [("send", SEND, [])]) * z.units
    segments += [("table", TABLE, [len(chains) - 2])] + [("up", UP, [])] * 3 + [("back", 0.0, [])]
    segments += [("rows", ROWS, []), ("rows", ROWS, []), ("rows", ROWS, [len(chains) - 1])]
    for name, cost, first in (("qkv", QKV, early), ("pool", POOL, early + 3)):
        segments += [(name, cost, done(unit, unit + 1)) for unit in range(first, first + 3)]
    segments += [("input", INPUT, [])] * 3
    return copies, chains, segments


def result_kernel(
    z,
    ff,
    total_ref,
    small_ref,
    block_in_ref,
    input_in_ref,
    block_ref,
    input_ref,
    pool_ref,
    gain1_ref,
    bias1_ref,
    query_ref,
    key_ref,
    value_ref,
    position_ref,
    content_bias_ref,
    position_bias_ref,
    output_ref,
    gain2_ref,
    bias2_ref,
    inner_ref,
    outer_ref,
    up_ref,
    wide,
    store_sems,
    pass_sems,
):
    width = z.width
    blocks = wide.shape[0]
    places = [outer_ref.at[k * width : (k + 1) * width] for k in range(ff // width)]
    places += [inner_ref.at[:, k * width : (k + 1) * width] for k in range(ff // width)]
    places += [output_ref]
    places += [up_ref.at[:, k * width : (k + 1) * width] for k in range(3)]
    places += [query_ref, key_ref, value_ref]
    places += [pool_ref.at[k * width : (k + 1) * width] for k in (2, 0, 1)]
    places += [position_ref]
    gain1_ref[...] = small_ref[0:1, :]
    bias1_ref[...] = small_ref[1:2, :]
    gain2_ref[...] = small_ref[2:3, :]
    bias2_ref[...] = small_ref[3:4, :]
    for head in range(z.heads):
        lanes = slice(head * z.hd, (head + 1) * z.hd)
        content_bias_ref[head : head + 1, :] = small_ref[4:5, lanes]
        position_bias_ref[head : head + 1, :] = small_ref[5:6, lanes]
    stores = []
    for which, (source, target) in enumerate(
        ((block_in_ref, block_ref), (input_in_ref, input_ref))
    ):
        stores.append(pltpu.make_async_copy(source, target, pass_sems.at[which]))
        stores[-1].start()
    order = list(range(blocks - 1))
    for k in order[:4] + [blocks - 1] + order[4:]:
        if k + 1 < blocks:
            wide[k] = total_ref[k * width : (k + 1) * width, :].astype(jnp.float32)
        else:
            half = z.hd // 2
            for head in range(z.heads):
                rows = []
                for side in range(2):
                    at = k * width + side * z.heads * half + head * half
                    rows.append(total_ref[at : at + half, :])
                both = jnp.concatenate(rows, axis=0).astype(jnp.float32)
                wide[k, :, head * z.hd : (head + 1) * z.hd] = both.T
        stores.append(pltpu.make_async_copy(wide.at[k], places[k], store_sems.at[k]))
        stores[-1].start()
    for copy in stores:
        copy.wait()


def body(
    byte_rows,
    item_lengths,
    out_grad,
    pool_weight,
    norm1_gain,
    norm1_bias,
    query_weight,
    key_weight,
    value_weight,
    position_weight,
    content_bias,
    position_bias,
    output_weight,
    norm2_gain,
    norm2_bias,
    inner_weight,
    outer_weight,
    upsample_weight,
):
    items, full_rows, width = byte_rows.shape
    heads, hd = content_bias.shape
    n = lax.axis_size("seq")
    ff = inner_weight.shape[1]
    z = Sizes(n, items, full_rows, width, heads)
    r, units, length, rows = z.r, z.units, z.length, z.rows
    bf, f4 = jnp.bfloat16, jnp.float32
    slabs = width // LANES
    dma = pltpu.SemaphoreType.DMA
    copies, chains, segments = chains_of(z, ff, lax.axis_size("batch"))
    plan = copies.schedule(chains, width, segments, r * LANES * 2)
    bits = copies.bits
    count, landing = Sums.needs(chains)
    total_rows = chains[-2]["base"] + chains[-2]["all"]
    operands = {
        "x": byte_rows,
        "pool_w": pool_weight,
        "gain1": norm1_gain.reshape(1, width),
        "bias1": norm1_bias.reshape(1, width),
        "query_w": query_weight,
        "key_w": key_weight,
        "value_w": value_weight,
        "og": out_grad,
        "up_w": upsample_weight,
        "outer_w": outer_weight,
        "table": distance_table(length, width),
        "position_w": position_weight,
        "content_bias": content_bias,
        "position_bias": position_bias,
        "output_w": output_weight,
        "gain2": norm2_gain.reshape(1, width),
        "bias2": norm2_bias.reshape(1, width),
        "inner_w": inner_weight,
    }
    outs = {
        "block_out": (byte_rows.shape, bf, VMEM),
        "input_grad": (byte_rows.shape, f4, VMEM),
        "total": ((total_rows, width), bf, VMEM),
        "small_total": ((8, width), f4, VMEM),
    }
    slab_rows = pltpu.VMEM((items, slabs, 3 * r + 8, LANES), f4)
    scratch = {name + "_v": pltpu.VMEM(operands[name].shape, operands[name].dtype) for name in OPERANDS}
    scratch.update(
        xf=slab_rows,
        of=slab_rows,
        bf=slab_rows,
        halo=pltpu.VMEM((items, 16, width), bf),
        first_rows=pltpu.VMEM((items, 16, width), bf),
        next_rows=pltpu.VMEM((items, 16, width), bf),
        later=pltpu.VMEM((items, r + 8, width), f4),
        short=pltpu.VMEM((rows, width), bf),
        normed1=pltpu.VMEM((rows, width), f4),
        inverse1=pltpu.VMEM((rows, 1), f4),
        attn_in=pltpu.VMEM((rows, width), bf),
        qkv_out=pltpu.VMEM((units, n, 3 * r // 2, 2 * hd), bf),
        qkv_in=pltpu.VMEM((units, n, 3 * r // 2, 2 * hd), bf),
        att_out=pltpu.VMEM((units, n, r // 2, 2 * hd), bf),
        att_in=pltpu.VMEM((units, n, r // 2, 2 * hd), bf),
        grad_out=pltpu.VMEM((units, n, r // 2, 2 * hd), bf),
        grad_in=pltpu.VMEM((units, n, r // 2, 2 * hd), bf),
        back_out=pltpu.VMEM((units, n, 3 * r // 2, 2 * hd), bf),
        back_in=pltpu.VMEM((units, n, 3 * r // 2, 2 * hd), bf),
        qc=pltpu.VMEM((units, length, hd), bf),
        qp=pltpu.VMEM((units, length, hd), bf),
        keys=pltpu.VMEM((units, length, hd), bf),
        values=pltpu.VMEM((units, length, hd), bf),
        pos=pltpu.VMEM((length, hd), bf),
        probs=pltpu.VMEM((units, length, length), f4),
        query_grad=pltpu.VMEM((units, length, hd), bf),
        key_t=pltpu.VMEM((units, hd, length), f4),
        value_t=pltpu.VMEM((units, hd, length), f4),
        table_t=pltpu.VMEM((units, hd, length), f4),
        att=pltpu.VMEM((rows, width), bf),
        hidden=pltpu.VMEM((rows, width), f4),
        ffn_in=pltpu.VMEM((rows, width), bf),
        act=pltpu.VMEM((rows, ff), bf),
        act_grad=pltpu.VMEM((rows, ff), f4),
        inner_grad=pltpu.VMEM((rows, ff), bf),
        up_rows=pltpu.VMEM((rows, 3 * width), bf),
        summed=pltpu.VMEM((rows, width), bf),
        summed_grad=pltpu.VMEM((rows, width), bf),
        hidden_grad=pltpu.VMEM((rows, width), f4),
        branch=pltpu.VMEM((rows, width), bf),
        row_grad=pltpu.VMEM((3, rows, width), bf),
        work=pltpu.VMEM((total_rows, width), bf),
        landing=pltpu.VMEM((landing, width), bf),
        small_work=pltpu.VMEM((len(bits) + 1, 8, width), f4),
        small_landing=pltpu.VMEM((len(bits), 8, width), f4),
        load_sems=dma((len(OPERANDS),)),
        halo_sems=dma((2,)),
        next_sems=dma((2,)),
        qkv_sems=dma((units + 1, 2)),
        att_sems=dma((units, 2)),
        grad_sems=dma((units, 2)),
        back_sems=dma((units, 2)),
        sum_send=dma((len(chains) - 1,)),
        sum_recv=dma((count,)),
        small_send=dma((len(bits),)),
        small_recv=dma((len(bits),)),
    )
    names = ("lengths",) + OPERANDS + tuple(outs) + tuple(scratch)
    block_out, input_grad, total, small_t = pl.pallas_call(
        functools.partial(block_kernel, z, plan, chains, bits, names),
        out_shape=[
            pltpu.VMEM(shape, dtype) if space is VMEM else jax.ShapeDtypeStruct(shape, dtype)
            for shape, dtype, space in outs.values()
        ],
        in_specs=[SMEM] + [ANY] * len(OPERANDS),
        out_specs=[space for _, _, space in outs.values()],
        scratch_shapes=list(scratch.values()),
        compiler_params=pltpu.CompilerParams(
            collective_id=0, has_side_effects=True, vmem_limit_bytes=50 * 2**20
        ),
    )(item_lengths, *(operands[name] for name in OPERANDS))
    blocks = total.shape[0] // width
    shapes = [
        ((items, full_rows, width), bf, ANY),
        ((items, full_rows, width), f4, ANY),
        ((3 * width, width), f4, ANY),
        ((1, width), f4, VMEM),
        ((1, width), f4, VMEM),
        ((width, width), f4, ANY),
        ((width, width), f4, ANY),
        ((width, width), f4, ANY),
        ((width, width), f4, ANY),
        ((heads, hd), f4, VMEM),
        ((heads, hd), f4, VMEM),
        ((width, width), f4, ANY),
        ((1, width), f4, VMEM),
        ((1, width), f4, VMEM),
        ((width, ff), f4, ANY),
        ((ff, width), f4, ANY),
        ((width, 3 * width), f4, ANY),
    ]
    results = pl.pallas_call(
        functools.partial(result_kernel, z, ff),
        out_shape=[jax.ShapeDtypeStruct(shape, dtype) for shape, dtype, _ in shapes],
        in_specs=[VMEM] * 4,
        out_specs=[space for _, _, space in shapes],
        scratch_shapes=[
            pltpu.VMEM((blocks, width, width), f4),
            dma((blocks,)),
            dma((2,)),
        ],
        compiler_params=pltpu.CompilerParams(vmem_limit_bytes=30 * 2**20),
    )(total, small_t, block_out, input_grad)
    return tuple(
        value.reshape(width) if value.shape == (1, width) else value for value in results
    )


def solution(mesh):
    split = P("batch", "seq", None)
    in_specs = (split, P("batch"), split) + (P(),) * 15
    out_specs = (split, split) + (P(),) * 15
    return jax.shard_map(body, mesh=mesh, in_specs=in_specs, out_specs=out_specs, check_vma=False)
```

```python
import functools

import jax
import jax.numpy as jnp
import numpy as np
from jax import lax
from jax.experimental import pallas as pl
from jax.experimental.pallas import tpu as pltpu
from jax.sharding import PartitionSpec as P

MESH = pl.DeviceIdType.MESH
epsilon = 1e-05
masked_value = -1e30
CHAINS = (
    (1, "yxz0z1", 19),
    (1, "z0z1yx", -15),
    (2, "xyz0z1", 20),
    (1, "yz0xz1", 17),
    (2, "yxz1z0", 20),
    (2, "z0xyz1", 3),
    (2, "xyz0z1", 14),
    (1, "xyz0z1", -8),
    (1, "xyz0z1", -17),
    (2, "yxz0z1", 3),
    (1, "xyz0z1", 7),
    (1, "yxz1z0", 12),
    (1, "xyz0z1", 7),
)
LAG, CORE_LAG, ISSUE, MARGIN = 2.6, 1.0, 0.15, 0.1
UNIT, BRANCH, BLOCK_STEP, SEND, TABLE, UP, ROWS, QKV, POOL, INPUT = 0.33, 0.9, 0.7, 0.3, 0.4, 0.5, 0.7, 0.3, 0.4, 0.4
BLOCK = 128
LANES = 128
VMEM = pl.BlockSpec(memory_space=pltpu.VMEM)
SMEM = pl.BlockSpec(memory_space=pltpu.SMEM)
ANY = pl.BlockSpec(memory_space=pl.ANY)


def dot(left, right):
    return jnp.dot(left, right, preferred_element_type=jnp.float32)


def dot_nt(left, right):
    return lax.dot_general(
        left, right, (((1,), (1,)), ((), ())), preferred_element_type=jnp.float32
    )


def dot_tn(left, right):
    return lax.dot_general(
        left, right, (((0,), (0,)), ((), ())), preferred_element_type=jnp.float32
    )


def low(value):
    return value.astype(jnp.bfloat16)


def distance_table(short_len, width):
    distance = (short_len - 1 - np.arange(short_len)).astype(np.float32)
    steps_in = np.arange(0, width, 2).astype(np.float32)
    frequency = np.exp(-np.log(np.float32(10000.0)) * steps_in / np.float32(width))
    angles = distance[:, None] * frequency[None, :].astype(np.float32)
    both = np.concatenate([np.sin(angles), np.cos(angles)], axis=1)
    return jnp.asarray(both.astype(jnp.bfloat16))


def norm_rows(rows):
    mean = jnp.mean(rows, axis=-1, keepdims=True)
    centered = rows - mean
    inverse = lax.rsqrt(jnp.mean(centered * centered, axis=-1, keepdims=True) + epsilon)
    return centered * inverse, inverse


def norm_backward(gradient, normed, inverse, gain):
    scaled = gradient * gain
    return inverse * (
        scaled
        - jnp.mean(scaled, axis=-1, keepdims=True)
        - normed * jnp.mean(scaled * normed, axis=-1, keepdims=True)
    )


class Sizes:
    def __init__(self, n, items, full_rows, width, heads):
        self.n = n
        self.items = items
        self.r = full_rows // 3
        self.width = width
        self.heads = heads
        self.hd = width // heads
        self.units = items * heads // n
        self.length = n * self.r
        self.rows = items * self.r
        assert n % heads == 0 and self.units * self.hd <= LANES


class Exchange:
    def __init__(self, n, me, source, target, sems, rows):
        target[me, rows] = source[me, rows]
        for step in range(1, n):
            peer = lax.rem(me + step, n)
            pltpu.make_async_remote_copy(
                src_ref=source.at[peer, rows],
                dst_ref=target.at[me, rows],
                send_sem=sems.at[0],
                recv_sem=sems.at[1],
                device_id={"seq": peer},
                device_id_type=MESH,
            ).start()
        self.all = pltpu.make_async_remote_copy(
            src_ref=source.at[1:, rows],
            dst_ref=target.at[1:, rows],
            send_sem=sems.at[0],
            recv_sem=sems.at[1],
            device_id={"seq": lax.rem(me + 1, n)},
            device_id_type=MESH,
        )

    def wait(self):
        self.all.wait()


def rows_by_three(z, x_ref, xf_ref):
    for item in range(z.items):
        for slab in range(z.width // LANES):
            xf_ref[item, slab, 8:, :] = x_ref[item, :, slab * LANES : (slab + 1) * LANES].astype(
                jnp.float32
            )


def every_third(z, xf_ref, first):
    items = []
    for item in range(z.items):
        slabs = [
            xf_ref[item, slab, pl.ds(first, z.r, stride=3), :] for slab in range(z.width // LANES)
        ]
        items.append(jnp.concatenate(slabs, axis=1))
    return jnp.concatenate(items, axis=0)


def set_every_third(z, xf_ref, first, value):
    for item in range(z.items):
        for slab in range(z.width // LANES):
            xf_ref[item, slab, pl.ds(first, z.r, stride=3), :] = value[
                item * z.r : (item + 1) * z.r, slab * LANES : (slab + 1) * LANES
            ]


def fold(value):
    half = value.shape[-2] // 2
    return jnp.concatenate([value[..., :half, :], value[..., half:, :]], axis=-1)


def unfold(value):
    half = value.shape[-1] // 2
    return jnp.concatenate([value[..., :half], value[..., half:]], axis=-2)


def live_rows(z, me, length, part):
    at = lax.broadcasted_iota(jnp.int32, (z.r, 1), 0) * 3 + part + me * 3 * z.r
    return (at < length).astype(jnp.float32)


def reversal():
    at = lax.broadcasted_iota(jnp.int32, (BLOCK, BLOCK), 0)
    across = lax.broadcasted_iota(jnp.int32, (BLOCK, BLOCK), 1)
    return low((at + across == BLOCK - 1).astype(jnp.float32))


class Copies:
    def __init__(self, batch_size, seq_size):
        self.core = [("batch", 1)]
        self.chips = [("batch", 1 << k) for k in range(1, batch_size.bit_length() - 1)]
        self.line = [("seq", 1 << k) for k in range(seq_size.bit_length() - 1)]
        self.bits = self.core + self.chips + self.line

    def cost(self, bit, size):
        axis, mask = bit
        if bit in self.core:
            return {"core": size / 428e3}
        near = 2 * size / 92e3
        if bit in self.line[:1] or axis == "batch":
            return {bit: near}
        return {"line": near, bit: near * (mask // 2)}

    def order(self, name):
        order = list(self.core)
        links = {"x": self.chips[0], "y": self.line[0], "z0": self.line[1], "z1": self.line[2]}
        while name:
            for key, bit in links.items():
                if name.startswith(key):
                    order.append(bit)
                    name = name[len(key) :]
        return order

    def rotated(self, k):
        links = self.chips + self.line
        k %= len(links)
        return self.core + links[k:] + links[:k]

    def hold(self, size):
        count = 1 << len(self.line)
        y = 2 * size * count / 2 / 92e3
        return {self.line[0]: y, "line": 1.5 * y, self.line[-1]: 2 * y}

    def halving(self, rows, order, base):
        down, up = [], []
        for bit in order:
            if rows % 32 == 0:
                rows //= 2
                down.append(("sum", bit, rows, rows))
                up.append(("spread", bit, rows, rows))
            else:
                down.append(("sum", bit, 0, rows))
        return {"base": base, "fixed": [], "steps": down + up[::-1], "rows": rows}

    def by_head(self, heads, hd, base):
        head_bits = self.line[: heads.bit_length() - 1]
        batch_bits = self.core + self.chips
        rest = self.line[len(head_bits) :]
        rows, parts = hd, []
        for bit in batch_bits + rest:
            if rows % 32 == 0:
                rows //= 2
                parts.append((bit, rows))
            else:
                parts.append((bit, 0))
        split = [bit for bit, size in parts if size]
        inner = split[1:]
        stride, strides = rows, {}
        for bit in inner[::-1] + head_bits + split[:1]:
            strides[bit] = stride
            stride *= 2
        down = [("sum", bit, strides.get(bit, 0), size or rows) for bit, size in parts]
        up = [("spread", bit, strides[bit], strides[bit]) for bit in strides]
        fixed = [(bit, strides[bit]) for bit in head_bits]
        return {"base": base, "fixed": fixed, "steps": down + up, "rows": rows, "strides": strides}

    def schedule(self, chains, width, segments, size):
        left = []
        for chain in chains:
            total = [0.0]
            for _, bit, _, rows in chain["steps"][::-1]:
                busy = max(self.cost(bit, 2 * rows * width).values())
                total.append(total[-1] + busy + LAG)
            left.append(total[::-1])
        free, at, plan = {}, [0] * len(chains), []
        ready = [None] * len(chains)
        now, segment, sent = 0.0, 0, {}

        def hold(name, times):
            for link, busy in self.hold(times * size).items():
                free[link] = max(free.get(link, 0.0), now) + busy
            sent[name] = max(free[link] for link in self.hold(size)) + LAG + 0.5

        sends = sum(name == "send" for name, _, _ in segments)
        while True:
            best, later = None, []
            for c, chain in enumerate(chains):
                if ready[c] is None or at[c] > len(chain["steps"]):
                    continue
                if at[c] == len(chain["steps"]):
                    start = ready[c] + MARGIN
                else:
                    _, bit, _, rows = chain["steps"][at[c]]
                    cost = self.cost(bit, 2 * rows * width)
                    start = max([ready[c] + (MARGIN if at[c] else 0.0)] + [free.get(link, 0.0) - 0.3 for link in cost])
                if start <= now:
                    key = (-left[c][at[c]] - chain.get("bias", 0), c)
                    best = key if best is None or key < best else best
                else:
                    later.append(start)
            if best is not None:
                c = best[1]
                k = at[c]
                at[c] += 1
                steps = chains[c]["steps"]
                now += ISSUE
                if k and steps[k - 1][0] == "sum":
                    now += 0.4e-6 * 2 * steps[k - 1][3] * width
                if k == len(steps):
                    plan.append(("end", c, k))
                    continue
                _, bit, _, rows = steps[k]
                cost = self.cost(bit, 2 * rows * width)
                start = max([now] + [free.get(link, 0.0) for link in cost])
                for link, busy in cost.items():
                    free[link] = start + busy
                lag = CORE_LAG if bit in self.core else LAG
                ready[c] = start + max(cost.values()) + lag
                plan.append(("sum", c, k))
                continue
            if segment < len(segments):
                name, busy, releases = segments[segment]
                due = sent.get(name, 0.0)
                if due <= now:
                    plan.append(("seg", segment, name))
                    now += busy
                    for c in releases:
                        ready[c] = now
                    if name == "branch":
                        hold("grad", 1)
                    if name == "send":
                        hold("back", 3 / sends)
                    segment += 1
                    continue
                later.append(due)
            if not later:
                self.end = now
                return plan
            now = max(now + 0.01, min(later))


class Sums:
    def __init__(self, chains, work, landing, total, send_sems, recv_sems):
        self.chains = chains
        self.work, self.landing, self.total = work, landing, total
        self.send_sems, self.recv_sems = send_sems, recv_sems
        self.index = {"batch": lax.axis_index("batch"), "seq": lax.axis_index("seq")}
        self.open = {}
        self.offset = {}
        sem = land = 0
        self.sem, self.land = {}, {}
        for c, chain in enumerate(chains[:-1]):
            self.offset[c] = chain["base"] + sum(
                self.bit(bit) * stride for bit, stride in chain["fixed"]
            )
            for k, (phase, _, _, rows) in enumerate(chain["steps"]):
                self.sem[c, k] = sem
                sem += 1
                if phase == "sum":
                    self.land[c, k] = land
                    land += rows

    @staticmethod
    def needs(chains):
        steps = [step for chain in chains[:-1] for step in chain["steps"]]
        return len(steps), sum(step[3] for step in steps if step[0] == "sum")

    def bit(self, bit):
        axis, mask = bit
        return lax.rem(lax.div(self.index[axis], mask), 2)

    def partner(self, bit):
        axis, mask = bit
        return {axis: self.index[axis] + mask - 2 * mask * self.bit(bit)}

    def start(self, c, k):
        if k:
            self.finish(c, k - 1)
        phase, bit, stride, rows = self.chains[c]["steps"][k]
        side = self.bit(bit)
        offset = self.offset[c]
        if phase == "sum":
            other = offset + (1 - side) * stride if stride else offset
            source = self.work.at[pl.ds(pl.multiple_of(other, 16), rows)]
            target = self.landing.at[pl.ds(self.land[c, k], rows)]
            if stride:
                self.offset[c] = offset + side * stride
        else:
            here = pl.ds(pl.multiple_of(offset, 16), rows)
            source, target = self.total.at[here], self.total.at[here]
            self.offset[c] = offset - side * stride
        copy = pltpu.make_async_remote_copy(
            src_ref=source,
            dst_ref=target,
            send_sem=self.send_sems.at[c],
            recv_sem=self.recv_sems.at[self.sem[c, k]],
            device_id=self.partner(bit),
            device_id_type=MESH,
        )
        copy.start()
        self.open[c] = copy

    def finish(self, c, k):
        self.open.pop(c).wait()
        steps = self.chains[c]["steps"]
        phase, _, _, rows = steps[k]
        if phase == "sum":
            last = k + 1 == len(steps) or steps[k + 1][0] == "spread"
            held = pl.ds(pl.multiple_of(self.offset[c], 16), rows)
            landed = self.landing[self.land[c, k] : self.land[c, k] + rows, :]
            both = self.work[held, :].astype(jnp.float32) + landed.astype(jnp.float32)
            (self.total if last else self.work)[held, :] = low(both)


OPERANDS = (
    "x",
    "pool_w",
    "gain1",
    "bias1",
    "query_w",
    "key_w",
    "value_w",
    "og",
    "up_w",
    "outer_w",
    "table",
    "position_w",
    "content_bias",
    "position_bias",
    "output_w",
    "gain2",
    "bias2",
    "inner_w",
)


class Pass:
    def __init__(self, z, plan, chains, bits, names, refs):
        self.z = z
        self.__dict__.update(zip(names, refs))
        self.plan, self.chains, self.bits = plan, chains, bits
        self.me = lax.axis_index("seq")
        self.head = lax.rem(self.me, z.heads)
        self.group = lax.div(self.me, z.heads)
        self.sums = Sums(
            chains, self.work, self.landing, self.total, self.sum_send, self.sum_recv
        )
        self.at = 0
        self.loads = {}

    def run(self):
        self.enter()
        self.project()
        self.attend()
        self.feed_forward()
        self.attend_back()
        self.finish_rows()
        self.finish_sums()

    def enter(self):
        z, me = self.z, self.me
        for k, name in enumerate(OPERANDS):
            self.loads[name] = pltpu.make_async_copy(
                getattr(self, name), getattr(self, name + "_v"), self.load_sems.at[k]
            )
            self.loads[name].start()
        barrier = pltpu.get_barrier_semaphore()
        batch = [bit for bit in self.bits if bit[0] == "batch"]
        for step in range(1, z.n):
            pl.semaphore_signal(
                barrier,
                inc=1,
                device_id={"seq": lax.rem(me + step, z.n)},
                device_id_type=MESH,
            )
        for bit in batch:
            pl.semaphore_signal(
                barrier, inc=1, device_id=self.sums.partner(bit), device_id_type=MESH
            )
        self.greeted = len(batch)

    def pool(self, part):
        width = self.z.width
        return dot(
            low(every_third(self.z, self.xf, 6 + part)),
            self.pool_w_v[part * width : (part + 1) * width, :],
        )

    def have(self, *names):
        for name in names:
            if name in self.loads:
                self.loads.pop(name).wait()

    def neighbour(self, source, target, sems, step):
        copy = pltpu.make_async_remote_copy(
            src_ref=source,
            dst_ref=target,
            send_sem=sems.at[0],
            recv_sem=sems.at[1],
            device_id={"seq": lax.rem(self.me + step, self.z.n)},
            device_id_type=MESH,
        )
        copy.start()
        return copy

    def exchange(self, name, unit, rows=None, sems=None):
        source, target = (getattr(self, name + end).at[unit] for end in ("_out", "_in"))
        sems = getattr(self, name + "_sems").at[unit if sems is None else sems]
        rows = slice(0, source.shape[1]) if rows is None else rows
        return Exchange(self.z.n, self.me, source, target, sems, rows)

    def part(self, value, target, unit):
        z = self.z
        item = target // z.heads * z.units + unit
        head = target % z.heads
        return value[item * z.r : (item + 1) * z.r, head * z.hd : (head + 1) * z.hd]

    def to_rows(self, name, parts, target_refs):
        z = self.z
        source_ref = getattr(self, name + "_in")
        for unit in range(z.units):
            for source in range(z.n):
                item = source // z.heads * z.units + unit
                head = source % z.heads
                rows = slice(item * z.r, (item + 1) * z.r)
                lanes = slice(head * z.hd, (head + 1) * z.hd)
                for value, target_ref in zip(parts(source_ref[unit, source]), target_refs):
                    target_ref[rows, lanes] = value

    def pack(self, first, second, third):
        pair, folded = jnp.concatenate([first, second], axis=-1), fold(third)
        parts = [pair[..., 16:, :], folded[..., 16:, :], pair[..., :16, :], folded[..., :16, :]]
        return jnp.concatenate(parts, axis=-2)

    def unpack(self, value):
        r, hd = self.z.r, self.z.hd
        late = 3 * r // 2 - 32
        pair = jnp.concatenate([value[..., late : late + 16, :], value[..., : r - 16, :]], axis=-2)
        folded = [value[..., late + 16 :, :], value[..., r - 16 : late, :]]
        return pair[..., :hd], pair[..., hd:], unfold(jnp.concatenate(folded, axis=-2))

    def live(self, part):
        z = self.z
        rows = [live_rows(z, self.me, self.lengths[item], part) for item in range(z.items)]
        return jnp.concatenate(rows, axis=0)

    def project(self):
        z, me, r, width = self.z, self.me, self.z.r, self.z.width
        self.have("x")
        rows_by_three(z, self.x_v, self.xf)
        self.xf[:, :, 0:8, :] = jnp.zeros((z.items, width // LANES, 8, LANES), jnp.float32)
        self.have("pool_w")
        pooled = self.pool(0) + self.pool(1) + self.pool(2)
        pl.semaphore_wait(pltpu.get_barrier_semaphore(), z.n - 1 + self.greeted)
        self.before = self.neighbour(
            self.x.at[:, 3 * z.r - 16 :, :], self.halo, self.halo_sems, 1
        )
        self.have("gain1", "bias1", "query_w", "key_w", "value_w")
        weights = (self.query_w_v, self.key_w_v, self.value_w_v)

        def normalize(rows):
            short = low(rows)
            normed, inverse = norm_rows(short.astype(jnp.float32))
            attn_in = low(normed * self.gain1_v[...] + self.bias1_v[...])
            return short, normed, inverse, attn_in

        kept = (self.short, self.normed1, self.inverse1, self.attn_in)
        for ref, value in zip(kept, normalize(pooled)):
            ref[...] = value
        qkv = [low(dot(self.attn_in[...], w[...])) for w in weights]
        late = 3 * r // 2 - 32
        self.moves = []

        def fill(unit):
            for target in range(z.n):
                self.qkv_out[unit, target] = self.pack(
                    *(self.part(value, target, unit) for value in qkv)
                )

        fill(0)
        self.moves.append([self.exchange("qkv", 0, slice(0, late))])
        self.before.wait()
        before = jnp.where(me > 0, self.halo[...].astype(jnp.float32), 0.0)
        before = low(before.reshape(z.items * 16, width))
        parts = [dot(before, self.pool_w_v[part * width : (part + 1) * width, :]) for part in (0, 1)]
        row = lax.broadcasted_iota(jnp.int32, (16, 1), 0)
        first = []
        for item in range(z.items):
            at = item * 16 + 14
            extra = parts[0][at : at + 1, :] + parts[1][at + 1 : at + 2, :]
            first.append(pooled[item * r : item * r + 16, :] + jnp.where(row == 0, extra, 0.0))
        first = normalize(jnp.concatenate(first, axis=0))
        for ref, value in zip(kept, first):
            for item in range(z.items):
                ref[item * r : item * r + 16, :] = value[item * 16 : (item + 1) * 16, :]
        for which, w in enumerate(weights):
            value = low(dot(first[3], w[...]))
            pieces = []
            for item in range(z.items):
                pieces += [
                    value[item * 16 : (item + 1) * 16, :],
                    qkv[which][item * r + 16 : (item + 1) * r, :],
                ]
            qkv[which] = jnp.concatenate(pieces, axis=0)
        for target in range(z.n):
            packed = self.pack(*(self.part(value, target, 0) for value in qkv))
            self.qkv_out[0, target, late:, :] = packed[late:, :]
        self.moves[0].append(self.exchange("qkv", 0, slice(late, late + 32), z.units))
        self.have("og", "up_w", "outer_w")
        rows_by_three(z, self.og_v, self.of)
        for part in range(3):
            self.up_rows[:, part * width : (part + 1) * width] = low(
                every_third(z, self.of, 8 + part) * self.live(part)
            )
        self.summed_grad[...] = low(dot_nt(self.up_rows[...], self.up_w_v[...]))
        for unit in range(1, z.units):
            fill(unit)
            self.moves.append([self.exchange("qkv", unit)])
        ff = self.outer_w_v.shape[0]
        for lo in range(0, ff, width):
            self.act_grad[:, lo : lo + width] = dot_nt(
                self.summed_grad[...], self.outer_w_v[lo : lo + width, :]
            )
        self.have("table", "position_w", "content_bias", "position_bias")
        first = self.head * z.hd
        pair = pl.ds(pl.multiple_of(lax.div(first, LANES) * LANES, LANES), LANES)
        both = dot(self.table_v[...], self.position_w_v[:, pair])
        self.pos[...] = low(pltpu.roll(both, LANES - lax.rem(first, LANES), 1)[:, : z.hd])

    def attend(self):
        z, hd = self.z, self.z.hd
        content_bias = self.content_bias_v[pl.ds(self.head, 1), :]
        position_bias = self.position_bias_v[pl.ds(self.head, 1), :]
        moves = []
        for unit in range(z.units):
            for move in self.moves[unit]:
                move.wait()
            queries, keys, values = (
                value.reshape(z.length, hd) for value in self.unpack(self.qkv_in[unit])
            )
            self.qc[unit] = low(queries.astype(jnp.float32) + content_bias)
            self.qp[unit] = low(queries.astype(jnp.float32) + position_bias)
            self.keys[unit] = keys
            self.values[unit] = values
            length = self.lengths[self.group * z.units + unit]
            for block in range(z.length // BLOCK):
                lo, hi = block * BLOCK, (block + 1) * BLOCK
                content = dot_nt(self.qc[unit, lo:hi, :], self.keys[unit, :hi, :])
                by_distance = dot_nt(self.qp[unit, lo:hi, :], self.pos[z.length - hi :, :])
                placed = pltpu.roll(by_distance, lo + 1, 1, stride=1, stride_axis=0)
                query_at = lo + lax.broadcasted_iota(jnp.int32, (BLOCK, hi), 0)
                key_at = lax.broadcasted_iota(jnp.int32, (BLOCK, hi), 1)
                valid = (key_at <= query_at) & (3 * key_at < length)
                logits = jnp.where(valid, (content + placed) * hd**-0.5, masked_value)
                raised = jnp.exp(logits - jnp.max(logits, axis=-1, keepdims=True))
                probs = raised * (1.0 / jnp.sum(raised, axis=-1, keepdims=True))
                self.probs[unit, lo:hi, :hi] = probs
                attended = low(dot(low(probs), self.values[unit, :hi, :]))
                per = BLOCK // z.r
                self.att_out[unit, block * per : (block + 1) * per] = fold(
                    attended.reshape(per, z.r, hd)
                )
            moves.append(self.exchange("att", unit))
        self.have("output_w", "gain2", "bias2", "inner_w")
        for move in moves:
            move.wait()

    def feed_forward(self):
        z, width = self.z, self.z.width
        ff = self.outer_w_v.shape[0]
        self.to_rows("att", lambda value: [unfold(value)], [self.att])
        hidden = self.short[...].astype(jnp.float32) + dot(self.att[...], self.output_w_v[...])
        normed, inverse = norm_rows(hidden)
        self.hidden[...] = hidden
        self.ffn_in[...] = low(normed * self.gain2_v[...] + self.bias2_v[...])
        ffn_in = self.ffn_in[...]
        ffn_grad = jnp.zeros((z.rows, width), jnp.float32)
        for lo in range(0, ff, width):
            cut = slice(lo, lo + width)
            inner = dot(ffn_in, self.inner_w_v[:, cut])
            normal_cdf = 0.5 * (1.0 + lax.erf(inner * 0.7071067811865476))
            density = jnp.exp(-0.5 * inner * inner) * 0.3989422804014327
            self.act[:, cut] = low(inner * normal_cdf)
            inner_grad = low(self.act_grad[:, cut] * (normal_cdf + inner * density))
            self.inner_grad[:, cut] = inner_grad
            ffn_grad += dot_nt(inner_grad, self.inner_w_v[:, cut])
        row = 0
        for lo in range(0, ff, width):
            self.reach("unit")
            self.work[row : row + width, :] = low(
                dot_tn(self.act[:, lo : lo + width], self.summed_grad[...])
            )
            row += width
        self.reach("branch")
        self.small_work[0, 2:3, :] = jnp.sum(ffn_grad * normed, axis=0, keepdims=True)
        self.small_work[0, 3:4, :] = jnp.sum(ffn_grad, axis=0, keepdims=True)
        hidden_grad = self.summed_grad[...].astype(jnp.float32) + norm_backward(
            ffn_grad, normed, inverse, self.gain2_v[...]
        )
        self.hidden_grad[...] = hidden_grad
        self.branch[...] = low(hidden_grad)
        att_grad = low(dot_nt(self.branch[...], self.output_w_v[...]))
        self.moves = []
        for unit in range(z.units):
            for target in range(z.n):
                self.grad_out[unit, target] = fold(self.part(att_grad, target, unit))
            self.moves.append(self.exchange("grad", unit))
        for lo in range(0, ff, width):
            self.reach("unit")
            self.work[row : row + width, :] = low(
                dot_tn(self.ffn_in[...], self.inner_grad[:, lo : lo + width])
            )
            row += width
        self.reach("unit")
        self.work[row : row + width, :] = low(dot_tn(self.att[...], self.branch[...]))
        row += width
        self.summed[...] = low(self.hidden[...] + dot(self.act[...], self.outer_w_v[...]))
        for lo in range(0, 3 * width, width):
            self.reach("unit")
            self.work[row : row + width, :] = low(
                dot_tn(self.summed[...], self.up_rows[:, lo : lo + width])
            )
            row += width
        self.row = row
        self.reach("grad")

    def upsample(self):
        z, width = self.z, self.z.width
        for part in range(3):
            self.reach("up")
            up = dot(self.summed[...], self.up_w_v[:, part * width : (part + 1) * width])
            set_every_third(
                z, self.bf, 8 + part, every_third(z, self.xf, 8 + part) + up * self.live(part)
            )
        for item in range(z.items):
            for slab in range(width // LANES):
                self.block_out[item, :, slab * LANES : (slab + 1) * LANES] = low(
                    self.bf[item, slab, 8:, :]
                )

    def attend_back(self):
        z, r, hd, length = self.z, self.z.r, self.z.hd, self.z.length
        flip = reversal()
        moves = []
        content_sum = jnp.zeros((1, hd), jnp.float32)
        position_sum = jnp.zeros((1, hd), jnp.float32)
        self.key_t[...] = jnp.zeros_like(self.key_t)
        self.value_t[...] = jnp.zeros_like(self.value_t)
        self.table_t[...] = jnp.zeros_like(self.table_t)
        for unit in range(z.units):
            self.moves[unit].wait()
            att_grad = unfold(self.grad_in[unit]).reshape(length, hd)
            for block in range(length // BLOCK):
                self.reach("block")
                lo, hi = block * BLOCK, (block + 1) * BLOCK
                block_grad = att_grad[lo:hi]
                probs = self.probs[unit, lo:hi, :hi]
                prob_grad = dot_nt(block_grad, self.values[unit, :hi, :])
                delta = jnp.sum(probs * prob_grad, axis=-1, keepdims=True)
                raw = low(probs * (prob_grad - delta) * hd**-0.5)
                content = dot(raw, self.keys[unit, :hi, :])
                self.key_t[unit, :, :hi] += dot_tn(self.qc[unit, lo:hi, :], raw)
                self.value_t[unit, :, :hi] += dot_tn(block_grad, low(probs))
                by_distance = low(pltpu.roll(dot(flip, raw), 0, 1, stride=1, stride_axis=0))
                position = dot(by_distance, self.pos[length - hi :, :])
                upper = low(position)
                lower = low(position - upper.astype(jnp.float32))
                position = dot(flip, upper) + dot(flip, lower)
                flipped_q = low(dot(flip, self.qp[unit, lo:hi, :]))
                self.table_t[unit, :, length - hi :] += dot_tn(flipped_q, by_distance)
                content_sum += jnp.sum(content, axis=0, keepdims=True)
                position_sum += jnp.sum(position, axis=0, keepdims=True)
                self.query_grad[unit, lo:hi, :] = low(content + position)
            self.reach("send")
            parts = (
                self.query_grad[unit],
                low(self.key_t[unit].T),
                low(self.value_t[unit].T),
            )
            self.back_out[unit] = self.pack(*(value.reshape(z.n, r, hd) for value in parts))
            moves.append(self.exchange("back", unit))
        own = lax.broadcasted_iota(jnp.int32, (1, z.width), 1) // hd == self.head
        for row, value in ((4, content_sum), (5, position_sum)):
            spread = jnp.concatenate([value] * z.heads, axis=1)
            self.small_work[0, row : row + 1, :] = jnp.where(own, spread, 0.0)
        self.reach("table")
        table_sum = 0.0
        for unit in range(z.units):
            table_sum += dot(low(self.table_t[unit]), self.table_v[...])
        half = hd // 2
        base = self.chains[-2]["base"]
        for side in range(2):
            at = pl.multiple_of(base + side * z.heads * half + self.head * half, 16)
            self.work[pl.ds(at, half), :] = low(table_sum[side * half : (side + 1) * half])
        self.upsample()
        self.reach("back")
        for move in moves:
            move.wait()

    def finish_rows(self):
        z, me, r, width = self.z, self.me, self.z.r, self.z.width
        self.reach("rows")
        self.to_rows("back", self.unpack, [self.row_grad.at[which] for which in range(3)])
        self.reach("rows")
        attn_grad = (
            dot_nt(self.row_grad[0], self.query_w_v[...])
            + dot_nt(self.row_grad[1], self.key_w_v[...])
            + dot_nt(self.row_grad[2], self.value_w_v[...])
        )
        self.reach("rows")
        normed = self.normed1[...]
        self.small_work[0, 0:1, :] = jnp.sum(attn_grad * normed, axis=0, keepdims=True)
        self.small_work[0, 1:2, :] = jnp.sum(attn_grad, axis=0, keepdims=True)
        self.small_work[0, 6:8, :] = jnp.zeros((2, width), jnp.float32)
        short_grad = low(
            self.hidden_grad[...]
            + norm_backward(attn_grad, normed, self.inverse1[...], self.gain1_v[...])
        )
        for item in range(z.items):
            self.first_rows[item] = short_grad[item * r : item * r + 16, :]
            self.later[item, 0:r, :] = short_grad[item * r : (item + 1) * r, :].astype(jnp.float32)
        halo = self.neighbour(self.first_rows, self.next_rows, self.next_sems, z.n - 1)
        row = self.row
        for which in range(3):
            self.reach("qkv")
            self.work[row : row + width, :] = low(dot_tn(self.attn_in[...], self.row_grad[which]))
            row += width
        self.reach("pool")
        self.work[row : row + width, :] = low(dot_tn(low(every_third(z, self.xf, 8)), short_grad))
        halo.wait()
        for item in range(z.items):
            after = jnp.where(me < z.n - 1, self.next_rows[item].astype(jnp.float32), 0.0)
            self.later[item, r : r + 8, :] = after[0:8, :]
        later = low(
            jnp.concatenate([self.later[item, 1 : r + 1, :] for item in range(z.items)], axis=0)
        )
        for part in range(2):
            row += width
            self.reach("pool")
            self.work[row : row + width, :] = low(
                dot_tn(low(every_third(z, self.xf, 9 + part)), later)
            )
        for part, rows, first in ((2, short_grad, 8), (0, later, 9), (1, later, 10)):
            self.reach("input")
            back = dot_nt(rows, self.pool_w_v[part * width : (part + 1) * width, :])
            set_every_third(z, self.of, first, every_third(z, self.of, first) + back)
        for item in range(z.items):
            for slab in range(width // LANES):
                self.input_grad[item, :, slab * LANES : (slab + 1) * LANES] = self.of[
                    item, slab, 8:, :
                ]

    def reach(self, name=None):
        while self.at < len(self.plan):
            kind, c, k = self.plan[self.at]
            self.at += 1
            if kind == "seg":
                assert k == name
                return
            if c == len(self.chains) - 1:
                self.small(k)
            elif kind == "sum":
                self.sums.start(c, k)
            else:
                self.sums.finish(c, k - 1)

    def small(self, k):
        if k:
            self.small_copy.wait()
            self.small_work[k] = self.small_work[k - 1] + self.small_landing[k - 1]
        if k < len(self.bits):
            self.small_start(k)
        else:
            self.small_total[...] = self.small_work[k]

    def small_start(self, k):
        self.small_copy = pltpu.make_async_remote_copy(
            src_ref=self.small_work.at[k],
            dst_ref=self.small_landing.at[k],
            send_sem=self.small_send.at[k],
            recv_sem=self.small_recv.at[k],
            device_id=self.sums.partner(self.bits[k]),
            device_id_type=MESH,
        )
        self.small_copy.start()

    def finish_sums(self):
        self.reach()


def block_kernel(z, plan, chains, bits, names, *refs):
    Pass(z, plan, chains, bits, names, refs).run()


def chains_of(z, ff, nb):
    width = z.width
    copies = Copies(nb, z.n)
    early = 2 * ff // width + 4
    units = early + 6
    searched = len(copies.bits) == 5 and sum(rows for rows, _, _ in CHAINS) == units
    chosen = CHAINS if searched else [(1, k, 0) for k in range(units)]
    chains, base = [], 0
    for rows, name, bias in chosen:
        order = copies.order(name) if searched else copies.rotated(name)
        chains.append(copies.halving(rows * width, order, base * width))
        chains[-1]["all"] = rows * width
        chains[-1]["bias"] = bias
        base += rows
        chains[-1]["units"] = base
    chains.append(copies.by_head(z.heads, z.hd, base * width))
    chains[-1]["all"] = z.heads * z.hd
    chains.append({"steps": [("small", bit, 0, 16) for bit in copies.bits]})
    blocks = z.length // BLOCK

    def done(first, last):
        return [c for c, chain in enumerate(chains) if first < chain.get("units", 0) <= last]

    segments = [("unit", UNIT, done(unit, unit + 1)) for unit in range(early)]
    segments.insert(ff // width, ("branch", BRANCH, []))
    segments += [("grad", 0.0, [])]
    segments += ([("block", BLOCK_STEP, [])] * blocks + [("send", SEND, [])]) * z.units
    segments += [("table", TABLE, [len(chains) - 2])] + [("up", UP, [])] * 3 + [("back", 0.0, [])]
    segments += [("rows", ROWS, []), ("rows", ROWS, []), ("rows", ROWS, [len(chains) - 1])]
    for name, cost, first in (("qkv", QKV, early), ("pool", POOL, early + 3)):
        segments += [(name, cost, done(unit, unit + 1)) for unit in range(first, first + 3)]
    segments += [("input", INPUT, [])] * 3
    return copies, chains, segments


def result_kernel(
    z,
    ff,
    total_ref,
    small_ref,
    block_in_ref,
    input_in_ref,
    block_ref,
    input_ref,
    pool_ref,
    gain1_ref,
    bias1_ref,
    query_ref,
    key_ref,
    value_ref,
    position_ref,
    content_bias_ref,
    position_bias_ref,
    output_ref,
    gain2_ref,
    bias2_ref,
    inner_ref,
    outer_ref,
    up_ref,
    wide,
    store_sems,
    pass_sems,
):
    width = z.width
    blocks = wide.shape[0]
    places = [outer_ref.at[k * width : (k + 1) * width] for k in range(ff // width)]
    places += [inner_ref.at[:, k * width : (k + 1) * width] for k in range(ff // width)]
    places += [output_ref]
    places += [up_ref.at[:, k * width : (k + 1) * width] for k in range(3)]
    places += [query_ref, key_ref, value_ref]
    places += [pool_ref.at[k * width : (k + 1) * width] for k in (2, 0, 1)]
    places += [position_ref]
    gain1_ref[...] = small_ref[0:1, :]
    bias1_ref[...] = small_ref[1:2, :]
    gain2_ref[...] = small_ref[2:3, :]
    bias2_ref[...] = small_ref[3:4, :]
    for head in range(z.heads):
        lanes = slice(head * z.hd, (head + 1) * z.hd)
        content_bias_ref[head : head + 1, :] = small_ref[4:5, lanes]
        position_bias_ref[head : head + 1, :] = small_ref[5:6, lanes]
    stores = []
    for which, (source, target) in enumerate(
        ((block_in_ref, block_ref), (input_in_ref, input_ref))
    ):
        stores.append(pltpu.make_async_copy(source, target, pass_sems.at[which]))
        stores[-1].start()
    order = list(range(blocks - 1))
    for k in order[:4] + [blocks - 1] + order[4:]:
        if k + 1 < blocks:
            wide[k] = total_ref[k * width : (k + 1) * width, :].astype(jnp.float32)
        else:
            half = z.hd // 2
            for head in range(z.heads):
                rows = []
                for side in range(2):
                    at = k * width + side * z.heads * half + head * half
                    rows.append(total_ref[at : at + half, :])
                both = jnp.concatenate(rows, axis=0).astype(jnp.float32)
                wide[k, :, head * z.hd : (head + 1) * z.hd] = both.T
        stores.append(pltpu.make_async_copy(wide.at[k], places[k], store_sems.at[k]))
        stores[-1].start()
    for copy in stores:
        copy.wait()


def body(
    byte_rows,
    item_lengths,
    out_grad,
    pool_weight,
    norm1_gain,
    norm1_bias,
    query_weight,
    key_weight,
    value_weight,
    position_weight,
    content_bias,
    position_bias,
    output_weight,
    norm2_gain,
    norm2_bias,
    inner_weight,
    outer_weight,
    upsample_weight,
):
    items, full_rows, width = byte_rows.shape
    heads, hd = content_bias.shape
    n = lax.axis_size("seq")
    ff = inner_weight.shape[1]
    z = Sizes(n, items, full_rows, width, heads)
    r, units, length, rows = z.r, z.units, z.length, z.rows
    bf, f4 = jnp.bfloat16, jnp.float32
    slabs = width // LANES
    dma = pltpu.SemaphoreType.DMA
    copies, chains, segments = chains_of(z, ff, lax.axis_size("batch"))
    plan = copies.schedule(chains, width, segments, r * LANES * 2)
    bits = copies.bits
    count, landing = Sums.needs(chains)
    total_rows = chains[-2]["base"] + chains[-2]["all"]
    operands = {
        "x": byte_rows,
        "pool_w": pool_weight,
        "gain1": norm1_gain.reshape(1, width),
        "bias1": norm1_bias.reshape(1, width),
        "query_w": query_weight,
        "key_w": key_weight,
        "value_w": value_weight,
        "og": out_grad,
        "up_w": upsample_weight,
        "outer_w": outer_weight,
        "table": distance_table(length, width),
        "position_w": position_weight,
        "content_bias": content_bias,
        "position_bias": position_bias,
        "output_w": output_weight,
        "gain2": norm2_gain.reshape(1, width),
        "bias2": norm2_bias.reshape(1, width),
        "inner_w": inner_weight,
    }
    outs = {
        "block_out": (byte_rows.shape, bf, VMEM),
        "input_grad": (byte_rows.shape, f4, VMEM),
        "total": ((total_rows, width), bf, VMEM),
        "small_total": ((8, width), f4, VMEM),
    }
    slab_rows = pltpu.VMEM((items, slabs, 3 * r + 8, LANES), f4)
    scratch = {name + "_v": pltpu.VMEM(operands[name].shape, operands[name].dtype) for name in OPERANDS}
    scratch.update(
        xf=slab_rows,
        of=slab_rows,
        bf=slab_rows,
        halo=pltpu.VMEM((items, 16, width), bf),
        first_rows=pltpu.VMEM((items, 16, width), bf),
        next_rows=pltpu.VMEM((items, 16, width), bf),
        later=pltpu.VMEM((items, r + 8, width), f4),
        short=pltpu.VMEM((rows, width), bf),
        normed1=pltpu.VMEM((rows, width), f4),
        inverse1=pltpu.VMEM((rows, 1), f4),
        attn_in=pltpu.VMEM((rows, width), bf),
        qkv_out=pltpu.VMEM((units, n, 3 * r // 2, 2 * hd), bf),
        qkv_in=pltpu.VMEM((units, n, 3 * r // 2, 2 * hd), bf),
        att_out=pltpu.VMEM((units, n, r // 2, 2 * hd), bf),
        att_in=pltpu.VMEM((units, n, r // 2, 2 * hd), bf),
        grad_out=pltpu.VMEM((units, n, r // 2, 2 * hd), bf),
        grad_in=pltpu.VMEM((units, n, r // 2, 2 * hd), bf),
        back_out=pltpu.VMEM((units, n, 3 * r // 2, 2 * hd), bf),
        back_in=pltpu.VMEM((units, n, 3 * r // 2, 2 * hd), bf),
        qc=pltpu.VMEM((units, length, hd), bf),
        qp=pltpu.VMEM((units, length, hd), bf),
        keys=pltpu.VMEM((units, length, hd), bf),
        values=pltpu.VMEM((units, length, hd), bf),
        pos=pltpu.VMEM((length, hd), bf),
        probs=pltpu.VMEM((units, length, length), f4),
        query_grad=pltpu.VMEM((units, length, hd), bf),
        key_t=pltpu.VMEM((units, hd, length), f4),
        value_t=pltpu.VMEM((units, hd, length), f4),
        table_t=pltpu.VMEM((units, hd, length), f4),
        att=pltpu.VMEM((rows, width), bf),
        hidden=pltpu.VMEM((rows, width), f4),
        ffn_in=pltpu.VMEM((rows, width), bf),
        act=pltpu.VMEM((rows, ff), bf),
        act_grad=pltpu.VMEM((rows, ff), f4),
        inner_grad=pltpu.VMEM((rows, ff), bf),
        up_rows=pltpu.VMEM((rows, 3 * width), bf),
        summed=pltpu.VMEM((rows, width), bf),
        summed_grad=pltpu.VMEM((rows, width), bf),
        hidden_grad=pltpu.VMEM((rows, width), f4),
        branch=pltpu.VMEM((rows, width), bf),
        row_grad=pltpu.VMEM((3, rows, width), bf),
        work=pltpu.VMEM((total_rows, width), bf),
        landing=pltpu.VMEM((landing, width), bf),
        small_work=pltpu.VMEM((len(bits) + 1, 8, width), f4),
        small_landing=pltpu.VMEM((len(bits), 8, width), f4),
        load_sems=dma((len(OPERANDS),)),
        halo_sems=dma((2,)),
        next_sems=dma((2,)),
        qkv_sems=dma((units + 1, 2)),
        att_sems=dma((units, 2)),
        grad_sems=dma((units, 2)),
        back_sems=dma((units, 2)),
        sum_send=dma((len(chains) - 1,)),
        sum_recv=dma((count,)),
        small_send=dma((len(bits),)),
        small_recv=dma((len(bits),)),
    )
    names = ("lengths",) + OPERANDS + tuple(outs) + tuple(scratch)
    block_out, input_grad, total, small_t = pl.pallas_call(
        functools.partial(block_kernel, z, plan, chains, bits, names),
        out_shape=[
            pltpu.VMEM(shape, dtype) if space is VMEM else jax.ShapeDtypeStruct(shape, dtype)
            for shape, dtype, space in outs.values()
        ],
        in_specs=[SMEM] + [ANY] * len(OPERANDS),
        out_specs=[space for _, _, space in outs.values()],
        scratch_shapes=list(scratch.values()),
        compiler_params=pltpu.CompilerParams(
            collective_id=0, has_side_effects=True, vmem_limit_bytes=50 * 2**20
        ),
    )(item_lengths, *(operands[name] for name in OPERANDS))
    blocks = total.shape[0] // width
    shapes = [
        ((items, full_rows, width), bf, ANY),
        ((items, full_rows, width), f4, ANY),
        ((3 * width, width), f4, ANY),
        ((1, width), f4, VMEM),
        ((1, width), f4, VMEM),
        ((width, width), f4, ANY),
        ((width, width), f4, ANY),
        ((width, width), f4, ANY),
        ((width, width), f4, ANY),
        ((heads, hd), f4, VMEM),
        ((heads, hd), f4, VMEM),
        ((width, width), f4, ANY),
        ((1, width), f4, VMEM),
        ((1, width), f4, VMEM),
        ((width, ff), f4, ANY),
        ((ff, width), f4, ANY),
        ((width, 3 * width), f4, ANY),
    ]
    results = pl.pallas_call(
        functools.partial(result_kernel, z, ff),
        out_shape=[jax.ShapeDtypeStruct(shape, dtype) for shape, dtype, _ in shapes],
        in_specs=[VMEM] * 4,
        out_specs=[space for _, _, space in shapes],
        scratch_shapes=[
            pltpu.VMEM((blocks, width, width), f4),
            dma((blocks,)),
            dma((2,)),
        ],
        compiler_params=pltpu.CompilerParams(vmem_limit_bytes=30 * 2**20),
    )(total, small_t, block_out, input_grad)
    return tuple(
        value.reshape(width) if value.shape == (1, width) else value for value in results
    )


def solution(mesh):
    split = P("batch", "seq", None)
    in_specs = (split, P("batch"), split) + (P(),) * 15
    out_specs = (split, split) + (P(),) * 15
    return jax.shard_map(body, mesh=mesh, in_specs=in_specs, out_specs=out_specs, check_vma=False)
```
